512 devices in a mesh: group: 2 (over core), dp: 16 (over y, z_hi), tensor: 16 (over z_lo, x).
Axes of the slice: x: 4, y: 8, z: 8 (z_hi: 2, z_lo: 4; z = z_hi * 4 + z_lo), core: 2. Of those that a mesh axis runs over, the one named last changes fastest.
Arguments:
- activations: bfloat16 [2, 4096, 8192], P('group', 'dp', 'tensor'), may hold values from -6 to 6
- cotangent: bfloat16 [2, 4096, 5120], P('group', 'dp'), may hold values from -6 to 6
- weight: bfloat16 [8192, 5120], P('tensor', 'dp'), may hold values from -0.0625 to 0.0625
- moment_one: float32 [2, 8192, 5120], P('group', 'tensor', 'dp'), may hold values from -256 to 256
- moment_two: float32 [2, 8192, 5120], P('group', 'tensor', 'dp'), may hold values from 500 to 8000
- queries: bfloat16 [4, 32, 8192], P(None, 'dp', 'tensor'), may hold values from -6 to 6
- cache_keys: bfloat16 [32, 2048, 128], P('dp'), may hold values from -6 to 6
- cache_values: bfloat16 [32, 2048, 128], P('dp'), may hold values from -6 to 6
- new_keys: bfloat16 [4, 32, 1024], P(None, 'dp'), may hold values from -16 to 16
- new_values: bfloat16 [4, 32, 1024], P(None, 'dp'), may hold values from -6 to 6
- lengths: int32 [32], P('dp'), may hold values from 2 to 256, as said below
- token_ids: int32 [4, 32], P(None, 'dp'), may hold values from 0 to 151935, as said below
Outputs:
- update: bfloat16 [8192, 5120], P('tensor', 'dp')
- decoded: bfloat16 [4, 32, 5120], P(None, 'dp')
The draws below stay inside these ranges and needn't reach their ends.
Inputs may be any that keep to these rules, and one draw needn't show every extreme that they name: Slots 0 to lengths[r] - 1 of row r hold keys and values; one row of every draw fills all 256 slots. `token_ids`: the id 151645 ends a row's response; the steps after it are padding.
All inputs are finite; a program needn't handle non-finite values.
Results may differ from the reference program's by a relative error of at most 0.0016.
The reference program's roundings to bfloat16 on the way count: a program that leaves them out, or rounds other values in their place, can miss the bound.
Values may be sent and summed in bfloat16 or wider, within the bound.
No kernel may reach another device: no remote copies, remote signals or barrier semaphores. Data moves between devices by JAX's collectives and lax.ppermute only.
A program may use at most 64 MiB of HBM per device.

```python
import math
import jax
import jax.numpy as jnp
from jax import lax

D = 5120
HEADS = 64
KVH = 8
HD = 128
VOCAB = 151936
EOS = 151645
STEPS = 4
CACHE = 256
TOKENS = 4096
ROWS = 32
QD = 8192


def draw_queries(key, part):
    key = jax.random.fold_in(key, 11)
    array_shape = (STEPS, ROWS, HEADS, HD)
    drawn = jnp.clip(jax.random.normal(key, array_shape, jnp.float32), -6.0, 6.0)
    return drawn.reshape(STEPS, ROWS, HEADS * HD).astype(jnp.bfloat16)


def draw_cache_keys(key, part):
    key = jax.random.fold_in(key, 12)
    array_shape = (ROWS, KVH, CACHE, HD)
    drawn = jnp.clip(jax.random.normal(key, array_shape, jnp.float32), -6.0, 6.0)
    return drawn.reshape(ROWS, KVH * CACHE, HD).astype(jnp.bfloat16)


def draw_lengths(key, part):
    key = jax.random.fold_in(key, 13)
    first_key, second_key = jax.random.split(key)
    drawn = jax.random.randint(first_key, (ROWS,), 2, CACHE + 1)
    longest = jax.random.randint(second_key, (), 0, ROWS)
    return jnp.where(jnp.arange(ROWS) == longest, CACHE, drawn).astype(jnp.int32)


def draw_token_ids(key, part):
    key = jax.random.fold_in(key, 14)
    first_key, second_key = jax.random.split(key)
    drawn = jax.random.randint(first_key, (STEPS, ROWS), 0, VOCAB)
    ending = jax.random.randint(second_key, (STEPS, ROWS), 0, 4) == 0
    return jnp.where(ending, EOS, drawn).astype(jnp.int32)


def levels(stream_key, dims, shards, least, top_value):
    loudness, own = 1.0, jax.random.fold_in(stream_key, 6)
    for axis_at, parts in shards:
        draws = jnp.exp(jax.random.uniform(jax.random.fold_in(own, axis_at), (parts,), jnp.float32, least / len(shards), top_value / len(shards)))
        loudness = loudness * jnp.repeat(draws, dims[axis_at] // parts).reshape([-1 if axis == axis_at else 1 for axis in range(len(dims))])
    return loudness


def bell_draw(own_key, dims, width, bound, pieces=(), kind=jnp.bfloat16):
    array = width * jax.random.normal(own_key, dims, jnp.float32)
    if pieces:
        array = array * levels(own_key, dims, pieces, -0.22, 0.18)
    return jnp.clip(array, -bound, bound).astype(kind)


def setup_inputs(seed: int = 0) -> dict:
    streams_of = jax.random.split(jax.random.key(seed), 13)
    return {
        "activations": bell_draw(streams_of[0], (2, TOKENS, QD), 1.0, 6.0, ((0, 2), (1, 16), (2, 16))),
        "cotangent": bell_draw(streams_of[1], (2, TOKENS, D), 1.0, 6.0, ((0, 2), (1, 16))),
        "weight": bell_draw(streams_of[2], (QD, D), QD ** -0.5, 0.0625, ((0, 16), (1, 16))),
        "moment_one": bell_draw(streams_of[3], (2, QD, D), 40.0, 256.0, ((0, 2), (1, 16), (2, 16)), jnp.float32),
        "moment_two": jnp.clip(jnp.exp(math.log(8000.0) - 2.7725887 * jax.random.uniform(streams_of[4], (2, QD, D), jnp.float32) ** levels(streams_of[4], (2, QD, D), ((0, 2), (1, 16), (2, 16)), -0.2, 0.2)), 500.0, 8000.0),
        "queries": draw_queries(jax.random.fold_in(streams_of[12], 71), 0),
        "cache_keys": draw_cache_keys(jax.random.fold_in(streams_of[12], 71), 0),
        "cache_values": bell_draw(streams_of[7], (ROWS, KVH * CACHE, HD), 1.0, 6.0, ((0, 16),)),
        "new_keys": bell_draw(streams_of[8], (STEPS, ROWS, KVH * HD), 2.5, 16.0, ((1, 16),)),
        "new_values": bell_draw(streams_of[9], (STEPS, ROWS, KVH * HD), 1.0, 6.0, ((1, 16),)),
        "lengths": draw_lengths(jax.random.fold_in(streams_of[12], 71), 0),
        "token_ids": draw_token_ids(jax.random.fold_in(streams_of[12], 71), 0),
    }


learning_rate = 0.0003
weight_decay = 0.1
beta_one = 0.9
beta_two = 0.95
first_bias = 1.0 - 0.9 ** 10
second_bias = 1.0 - 0.95 ** 10
epsilon = 1e-08

def reference(activations, cotangent, weight, moment_one, moment_two, queries, cache_keys, cache_values, new_keys, new_values, lengths, token_ids):
    gradient = jnp.dot(activations[1].T, cotangent[1], preferred_element_type=jnp.float32)
    first_moment = beta_one * moment_one[1] + (1.0 - beta_one) * gradient
    second_moment = beta_two * moment_two[1] + (1.0 - beta_two) * gradient * gradient
    update = (first_moment / first_bias / (jnp.sqrt(second_moment / second_bias) + epsilon)).astype(jnp.bfloat16)
    widened = weight.astype(jnp.float32)
    renewed = (widened - learning_rate * (update.astype(jnp.float32) + weight_decay * widened)).astype(jnp.bfloat16)
    highest = lax.Precision.HIGHEST
    group_size = HEADS // KVH
    query_blocks = queries.astype(jnp.float32).reshape(STEPS, ROWS, KVH, group_size, HD)
    key_blocks = cache_keys.astype(jnp.float32).reshape(ROWS, KVH, CACHE, HD)
    value_blocks = cache_values.astype(jnp.float32).reshape(ROWS, KVH, CACHE, HD)
    fresh_keys = new_keys.astype(jnp.float32).reshape(STEPS, ROWS, KVH, HD)
    fresh_values = new_values.astype(jnp.float32).reshape(STEPS, ROWS, KVH, HD)
    score_scale = 1.0 / math.sqrt(HD)
    cache_scores = jnp.einsum('trkgd,rkpd->trkgp', query_blocks, key_blocks, precision=highest) * score_scale
    step_scores = jnp.einsum('trkgd,urkd->trkgu', query_blocks, fresh_keys, precision=highest) * score_scale
    positions = jnp.arange(CACHE, dtype=jnp.int32)
    cache_valid = positions[None, :] < lengths[:, None]
    step_index = jnp.arange(STEPS, dtype=jnp.int32)
    step_valid = step_index[None, :] <= step_index[:, None]
    cache_scores = jnp.where(cache_valid[None, :, None, None, :], cache_scores, -jnp.inf)
    step_scores = jnp.where(step_valid[:, None, None, None, :], step_scores, -jnp.inf)
    peak = jnp.maximum(lax.optimization_barrier(jnp.max(cache_scores, axis=-1)), lax.optimization_barrier(jnp.max(step_scores, axis=-1)))[..., None]
    cache_exp = jnp.exp(cache_scores - peak)
    step_exp = jnp.exp(step_scores - peak)
    denominator = lax.optimization_barrier(jnp.sum(cache_exp, axis=-1, keepdims=True)) + lax.optimization_barrier(jnp.sum(step_exp, axis=-1, keepdims=True))
    cache_probs = (cache_exp / denominator).astype(jnp.bfloat16).astype(jnp.float32)
    step_probs = (step_exp / denominator).astype(jnp.bfloat16).astype(jnp.float32)
    mixed = jnp.einsum('trkgp,rkpd->trkgd', cache_probs, value_blocks, precision=highest)
    mixed = mixed + jnp.einsum('trkgu,urkd->trkgd', step_probs, fresh_values, precision=highest)
    finished = (token_ids == EOS).astype(jnp.int32)
    earlier = jnp.cumsum(finished, axis=0) - finished
    mixed = jnp.where((earlier == 0)[:, :, None, None, None], mixed, 0.0)
    attention = mixed.astype(jnp.bfloat16).reshape(STEPS * ROWS, HEADS * HD)
    decoded = jnp.dot(attention, renewed, preferred_element_type=jnp.float32).astype(jnp.bfloat16)
    return (update, decoded.reshape(STEPS, ROWS, D))
```

```python
import functools
import math

import jax
import jax.numpy as jnp
import numpy as np
from jax import lax
from jax.experimental import pallas as pl
from jax.experimental.pallas import tpu as pltpu
from jax.sharding import PartitionSpec as P

D = 5120
KVH = 8
HD = 128
EOS = 151645
STEPS = 4
CACHE = 256

learning_rate = 0.0003
weight_decay = 0.1
beta_one = 0.9
beta_two = 0.95
first_bias = 1.0 - 0.9**10
second_bias = 1.0 - 0.95**10
epsilon = 1e-08

AXES = ("group", "dp", "tensor")
SHAPE = (2, 8, 2, 4, 4)
TOK = 256
FEAT = 512
COLS = 320
ROWS = 8
PAD = 16
HOPS = (0, 1, 2, 3, 4, -1, -2, -3)
f32, bf16 = jnp.float32, jnp.bfloat16


def permute(value, target):
    pairs = []
    for flat, place in enumerate(np.ndindex(*SHAPE)):
        to = target(*place)
        if to is not None:
            pairs.append((flat, int(np.ravel_multi_index(to, SHAPE))))
    return lax.ppermute(value, AXES, pairs)


def keeper(zh, x):
    return 1 if (x & 1) == zh else 0


def to_partner(g, y, zh, zl, x):
    return (0, y, 1 - zh, zl, x) if g == 1 else None


def along_y(step):
    return lambda g, y, zh, zl, x: (g, (y + step) % 8, zh, zl, x)


def transposed(g, y, zh, zl, x):
    return (g, zl * 2 + (x >> 1), x & 1, y >> 1, (y & 1) * 2 + zh)


def cot_transposed(g, y, zh, zl, x):
    if g == 0:
        return None
    _, y2, zh2, zl2, x2 = transposed(g, y, zh, zl, x)
    return (keeper(zh2, x2), y2, zh2, zl2, x2)


def along_zl(flip):
    def target(g, y, zh, zl, x):
        return (g, y, zh, zl ^ flip, x) if g == keeper(zh, x) else None

    return target


def along_x(step):
    def target(g, y, zh, zl, x):
        return (g, y, zh, zl, (x + step) % 4) if g == keeper(zh, x) else None

    return target


def other_core(g, y, zh, zl, x):
    return (1 - g, y, zh, zl, x)


def to_rollout(g, y, zh, zl, x):
    return (0, y, zh, zl, x) if g == 1 else None


def attend_kernel(head_ref, lengths_ref, ids_ref, q_ref, k_ref, v_ref, nk_ref, nv_ref, out_ref):
    queries = q_ref[...]
    query = jnp.concatenate(
        [queries[:, h * HD : (h + 1) * HD] for h in range(4)], axis=0
    ).astype(bf16)
    keys = k_ref[...].reshape(2 * CACHE, HD)
    values = v_ref[...].reshape(2 * CACHE, HD)
    fresh_keys = nk_ref[...].astype(bf16)
    fresh_values = nv_ref[...].astype(bf16)
    scale = 1.0 / math.sqrt(HD)
    nt = (((1,), (1,)), ((), ()))
    cache_scores = lax.dot_general(query, keys, nt, preferred_element_type=f32) * scale
    step_scores = lax.dot_general(query, fresh_keys, nt, preferred_element_type=f32) * scale
    count = 4 * ROWS

    def place(width):
        place_row = lax.broadcasted_iota(jnp.int32, (count, width), 0) & (ROWS - 1)
        place_key = lax.broadcasted_iota(jnp.int32, (count, width), 1)
        return place_row >> 1, place_row & 1, place_key

    step, row, key = place(2 * CACHE)
    length = jnp.where(row == 0, lengths_ref[0], lengths_ref[1])
    cache_valid = ((key >> 8) == row) & ((key & (CACHE - 1)) < length)
    step, row, key = place(ROWS)
    step_valid = ((key & 1) == row) & ((key >> 1) <= step)
    cache_scores = jnp.where(cache_valid, cache_scores, -jnp.inf)
    step_scores = jnp.where(step_valid, step_scores, -jnp.inf)
    peak = jnp.maximum(
        jnp.max(cache_scores, axis=-1, keepdims=True), jnp.max(step_scores, axis=-1, keepdims=True)
    )
    cache_exp = jnp.exp(cache_scores - peak)
    step_exp = jnp.exp(step_scores - peak)
    denominator = jnp.sum(cache_exp, axis=-1, keepdims=True) + jnp.sum(
        step_exp, axis=-1, keepdims=True
    )
    cache_probs = (cache_exp / denominator).astype(bf16)
    step_probs = (step_exp / denominator).astype(bf16)
    nn = (((1,), (0,)), ((), ()))
    mixed = lax.dot_general(cache_probs, values, nn, preferred_element_type=f32)
    mixed = mixed + lax.dot_general(step_probs, fresh_values, nn, preferred_element_type=f32)
    step, row, _ = place(HD)
    dead = jnp.zeros((count, HD), jnp.int32)
    for u in range(STEPS - 1):
        for r in range(2):
            ended = (ids_ref[u, r] == EOS).astype(jnp.int32)
            dead = dead + jnp.where((row == r) & (step > u), ended, 0)
    mixed = jnp.where(dead == 0, mixed, 0.0)
    flat = jnp.concatenate([mixed[h * ROWS : (h + 1) * ROWS] for h in range(4)], axis=1)
    out_ref[...] = jnp.concatenate([flat, jnp.zeros_like(flat)], axis=0).astype(bf16)


def attend(head, queries, cache_keys, cache_values, new_keys, new_values, lengths, token_ids):
    whole = lambda *shape: pl.BlockSpec(shape, lambda i, *_: (0,) * len(shape))
    cache = pl.BlockSpec((2, CACHE, HD), lambda i, m, *_: (0, m[0], 0))
    fresh = pl.BlockSpec((ROWS, HD), lambda i, m, *_: (0, m[0]))
    return pl.pallas_call(
        attend_kernel,
        out_shape=jax.ShapeDtypeStruct((PAD, FEAT), bf16),
        grid_spec=pltpu.PrefetchScalarGridSpec(
            num_scalar_prefetch=3,
            grid=(1,),
            in_specs=[whole(ROWS, FEAT), cache, cache, fresh, fresh],
            out_specs=whole(PAD, FEAT),
        ),
        name="attend",
    )(
        head,
        lengths,
        token_ids,
        queries.astype(f32).reshape(ROWS, FEAT),
        cache_keys,
        cache_values,
        new_keys.astype(f32).reshape(ROWS, KVH * HD),
        new_values.astype(f32).reshape(ROWS, KVH * HD),
    )


def gradient_kernel(index_ref, *refs):
    chunks, blocks, out_ref = refs[:8], refs[8:12], refs[12]
    for n in range(8):
        slot, which = index_ref[8 + n], index_ref[16 + n]
        block = blocks[0][slot]
        for b in range(1, 4):
            block = jnp.where(which == b, blocks[b][slot], block)
        part = jnp.dot(block, chunks[n][:TOK, :], preferred_element_type=f32)
        if n == 0:
            out_ref[:COLS, :] = part
        else:
            out_ref[:COLS, :] += part
        place = pl.multiple_of(COLS + index_ref[n] * ROWS, ROWS)
        out_ref[pl.ds(place, ROWS), :] = chunks[n][TOK:, :].astype(f32)[:ROWS]


def gradient(index, chunks, blocks):
    vmem = pl.BlockSpec(memory_space=pltpu.VMEM)
    return pl.pallas_call(
        gradient_kernel,
        out_shape=jax.ShapeDtypeStruct((COLS + 8 * ROWS, FEAT), f32),
        in_specs=[pl.BlockSpec(memory_space=pltpu.SMEM)] + [vmem] * 12,
        out_specs=vmem,
        compiler_params=pltpu.CompilerParams(vmem_limit_bytes=32 * 2**20),
        cost_estimate=pl.CostEstimate(
            flops=2 * 8 * TOK * COLS * FEAT, bytes_accessed=6 * 2**20, transcendentals=0
        ),
        name="gradient",
    )(index, *chunks, *blocks)


def step_kernel(
    side_ref, mine_ref, got_ref, one_ref, one_got, two_ref, two_got, weight_ref, update_ref, out_ref
):
    learner = side_ref[0] == 1
    grad = mine_ref[:COLS, :] + got_ref[:COLS, :]
    moment_one = jnp.where(learner, one_ref[...], one_got[...])
    moment_two = jnp.where(learner, two_ref[...], two_got[...])
    first_moment = beta_one * moment_one + (1.0 - beta_one) * grad
    second_moment = beta_two * moment_two + (1.0 - beta_two) * grad * grad
    update = (
        first_moment / first_bias / (jnp.sqrt(second_moment / second_bias) + epsilon)
    ).astype(bf16)
    update_ref[...] = update
    widened = weight_ref[...].astype(f32)
    renewed = (
        widened - learning_rate * (update.astype(f32) + weight_decay * widened)
    ).astype(bf16)
    mine, got = mine_ref[COLS:, :], got_ref[COLS:, :]
    even = side_ref[1] == 0
    for zh in range(2):
        rows = jnp.where(even, mine, got) if zh == 0 else jnp.where(even, got, mine)
        part = lax.dot_general(
            rows.astype(bf16), renewed, (((1,), (1,)), ((), ())), preferred_element_type=f32
        )
        for y in range(8):
            out_ref[y * 2 + zh] = part[y * ROWS : (y + 1) * ROWS]


def step(side, mine, got, one, one_got, two, two_got, weight):
    vmem = pl.BlockSpec(memory_space=pltpu.VMEM)
    return pl.pallas_call(
        step_kernel,
        out_shape=(
            jax.ShapeDtypeStruct((COLS, FEAT), bf16),
            jax.ShapeDtypeStruct((16, ROWS, COLS), f32),
        ),
        in_specs=[pl.BlockSpec(memory_space=pltpu.SMEM)] + [vmem] * 7,
        out_specs=(vmem, vmem),
        compiler_params=pltpu.CompilerParams(vmem_limit_bytes=32 * 2**20),
        name="step",
    )(side, mine, got, one, one_got, two, two_got, weight)


def local(
    activations,
    cotangent,
    weight,
    moment_one,
    moment_two,
    queries,
    cache_keys,
    cache_values,
    new_keys,
    new_values,
    lengths,
    token_ids,
):
    g = lax.axis_index("group")
    p = lax.axis_index("dp")
    q = lax.axis_index("tensor")
    y, zh, zl, x = p >> 1, p & 1, q >> 2, q & 3

    rows = attend(
        (q >> 1).reshape(1),
        queries,
        cache_keys,
        cache_values,
        new_keys,
        new_values,
        lengths,
        token_ids,
    )
    payload = jnp.concatenate([activations[0], rows], axis=0)
    base = jnp.where(g == 1, payload, permute(payload, to_partner))

    cut = lax.dynamic_slice_in_dim(cotangent[0], q * COLS, COLS, 1).T
    own = permute(cut, cot_transposed)
    pair = jnp.stack([own, permute(own, along_zl(3))])
    four = jnp.concatenate([pair, permute(pair, along_zl(1))], axis=0)
    from_left = permute(four, along_x(1))
    from_right = permute(four, along_x(-1))
    from_far = permute(four, along_x(2))

    up, down = [base], [base]
    for n in range(4):
        up.append(permute(up[-1], along_y(1)))
        if n < 3:
            down.append(permute(down[-1], along_y(-1)))
    chunks = up + down[1:]

    one, two = moment_one[0].T, moment_two[0].T
    one_got = permute(one, to_rollout)
    two_got = permute(two, to_rollout)

    origin = (y - np.array(HOPS, np.int32)) & 7
    parity = jnp.where(g == 1, zh, 1 - zh)
    flip = (origin >> 1) ^ zl
    slot = jnp.where(flip == 0, 0, jnp.where(flip == 3, 1, jnp.where(flip == 1, 2, 3)))
    source = 2 * (origin & 1) + parity
    keeps = parity == (x & 1)
    which = jnp.where(
        keeps, jnp.where(source == x, 0, 1), jnp.where(source == ((x - 1) & 3), 2, 3)
    )
    index = jnp.concatenate([origin, slot, which]).astype(jnp.int32)
    mine = gradient(index, chunks, (four, from_far, from_left, from_right))
    got = permute(mine, other_core)

    side = jnp.stack([g, parity]).astype(jnp.int32)
    update, partial = step(side, mine, got, one, one_got, two, two_got, weight.T)

    shares = lax.all_to_all(partial, "tensor", split_axis=0, concat_axis=0, tiled=True)
    summed = jnp.sum(shares, axis=0).astype(bf16)
    block = permute(summed, transposed)
    spread = jnp.broadcast_to(block[None], (16, ROWS, COLS))
    gathered = lax.all_to_all(spread, "tensor", split_axis=0, concat_axis=0, tiled=True)
    decoded = gathered.transpose(1, 0, 2).reshape(STEPS, ROWS // STEPS, D)
    return (update.T, decoded)


def solution(mesh):
    return jax.shard_map(
        local,
        mesh=mesh,
        in_specs=(
            P("group", "dp", "tensor"),
            P("group", "dp", None),
            P("tensor", "dp"),
            P("group", "tensor", "dp"),
            P("group", "tensor", "dp"),
            P(None, "dp", "tensor"),
            P("dp", None, None),
            P("dp", None, None),
            P(None, "dp", None),
            P(None, "dp", None),
            P("dp"),
            P(None, "dp"),
        ),
        out_specs=(P("tensor", "dp"), P(None, "dp", None)),
        check_vma=False,
    )
```

```python
import math

import jax
import jax.numpy as jnp
import numpy as np
from jax import lax
from jax.experimental import pallas as pl
from jax.experimental.pallas import tpu as pltpu
from jax.sharding import PartitionSpec as P

D = 5120
KVH = 8
HD = 128
EOS = 151645
STEPS = 4
CACHE = 256

learning_rate = 0.0003
weight_decay = 0.1
beta_one = 0.9
beta_two = 0.95
first_bias = 1.0 - 0.9**10
second_bias = 1.0 - 0.95**10
epsilon = 1e-08

AXES = ("group", "dp", "tensor")
SHAPE = (2, 8, 2, 4, 4)
TOK = 256
FEAT = 512
COLS = 320
ROWS = 8
PAD = 16
f32, bf16 = jnp.float32, jnp.bfloat16


def permute(value, target):
    pairs = []
    for flat, place in enumerate(np.ndindex(*SHAPE)):
        to = target(*place)
        if to is not None:
            pairs.append((flat, int(np.ravel_multi_index(to, SHAPE))))
    return lax.ppermute(value, AXES, pairs)


def on_learner(y, zh, block_y, block_zh):
    return (y - block_y - (zh != block_zh)) % 8 < 4


def keeper(y, zh, zl, x):
    return int(on_learner(y, zh, 2 * zl + (x >> 1), x & 1))


def along_y(step, core, to=None):
    def target(g, y, zh, zl, x):
        return (core if to is None else to, (y + step) % 8, zh, zl, x) if g == core else None

    return target


def along_z(step, core, to):
    def target(g, y, zh, zl, x):
        z = (zh * 4 + zl + step) % 8
        return (to, y, z // 4, z % 4, x) if g == core else None

    return target


def transposed(g, y, zh, zl, x):
    return (g, zl * 2 + (x >> 1), x & 1, y >> 1, (y & 1) * 2 + zh)


def cot_transposed(g, *place):
    to = transposed(g, *place)[1:]
    return (keeper(*to), *to) if g == 1 else None


def along_zl(flip):
    def target(g, y, zh, zl, x):
        return (g, y, zh, zl ^ flip, x) if g == keeper(y, zh, zl, x) else None

    return target


def along_x(step):
    return lambda g, y, zh, zl, x: (g, y, zh, zl, (x + step) % 4)


def other_core(g, y, zh, zl, x):
    return (1 - g, y, zh, zl, x)


def to_rollout(g, y, zh, zl, x):
    return (0, y, zh, zl, x) if g == 1 else None


CHUNKS = (
    ((0, -1), (0, -2), (0, -3), (0, -4), (1, 0), (1, -1), (1, -2), (1, -3)),
    ((0, 0), (0, 1), (0, 2), (0, 3), (1, 1), (1, 2), (1, 3), (1, 4)),
)


def device_table():
    table = np.zeros((512, 32), np.int32)
    for flat, (g, y, zh, zl, x) in enumerate(np.ndindex(*SHAPE)):
        kept = [[z for z in range(4) if keeper(y, zh, z, c) == g] for c in range(4)]
        table[flat, 0] = g
        table[flat, 1:3] = [z ^ zl for z in kept[x]]
        for n, (other, hop) in enumerate(CHUNKS[g]):
            block_y, block_zh = (y - hop) % 8, zh ^ other
            block_x = 2 * (block_y & 1) + block_zh
            table[flat, 8 + n] = block_y * 2 + block_zh
            table[flat, 16 + n] = (block_x - x) % 4
            table[flat, 24 + n] = kept[block_x].index(block_y >> 1)
    return table


def attend_kernel(
    head_ref, lengths_ref, ids_ref, act_ref, q_ref, k_ref, v_ref, nk_ref, nv_ref, out_ref, q_rows, nk_rows, nv_rows
):
    out_ref[:TOK, :] = act_ref[...]
    for t in range(STEPS):
        place = slice(2 * t, 2 * t + 2)
        q_rows[place, :] = q_ref[t].astype(f32)
        nk_rows[place, :] = nk_ref[t].astype(f32)
        nv_rows[place, :] = nv_ref[t].astype(f32)
    queries = q_rows[...]
    query = jnp.concatenate(
        [queries[:, h * HD : (h + 1) * HD] for h in range(4)], axis=0
    ).astype(bf16)
    keys = k_ref[...].reshape(2 * CACHE, HD)
    values = v_ref[...].reshape(2 * CACHE, HD)
    fresh_keys = nk_rows[...].astype(bf16)
    fresh_values = nv_rows[...].astype(bf16)
    scale = 1.0 / math.sqrt(HD)
    nt = (((1,), (1,)), ((), ()))
    cache_scores = lax.dot_general(query, keys, nt, preferred_element_type=f32) * scale
    step_scores = lax.dot_general(query, fresh_keys, nt, preferred_element_type=f32) * scale
    count = 4 * ROWS

    def place(width):
        place_row = lax.broadcasted_iota(jnp.int32, (count, width), 0) & (ROWS - 1)
        place_key = lax.broadcasted_iota(jnp.int32, (count, width), 1)
        return place_row >> 1, place_row & 1, place_key

    step, row, key = place(2 * CACHE)
    length = jnp.where(row == 0, lengths_ref[0], lengths_ref[1])
    cache_valid = ((key >> 8) == row) & ((key & (CACHE - 1)) < length)
    step, row, key = place(ROWS)
    step_valid = ((key & 1) == row) & ((key >> 1) <= step)
    cache_scores = jnp.where(cache_valid, cache_scores, -jnp.inf)
    step_scores = jnp.where(step_valid, step_scores, -jnp.inf)
    peak = jnp.maximum(
        jnp.max(cache_scores, axis=-1, keepdims=True), jnp.max(step_scores, axis=-1, keepdims=True)
    )
    cache_exp = jnp.exp(cache_scores - peak)
    step_exp = jnp.exp(step_scores - peak)
    denominator = jnp.sum(cache_exp, axis=-1, keepdims=True) + jnp.sum(
        step_exp, axis=-1, keepdims=True
    )
    cache_probs = (cache_exp / denominator).astype(bf16)
    step_probs = (step_exp / denominator).astype(bf16)
    nn = (((1,), (0,)), ((), ()))
    mixed = lax.dot_general(cache_probs, values, nn, preferred_element_type=f32)
    mixed = mixed + lax.dot_general(step_probs, fresh_values, nn, preferred_element_type=f32)
    step, row, _ = place(HD)
    dead = jnp.zeros((count, HD), jnp.int32)
    for u in range(STEPS - 1):
        for r in range(2):
            ended = (ids_ref[r, u] == EOS).astype(jnp.int32)
            dead = dead + jnp.where((row == r) & (step > u), ended, 0)
    mixed = jnp.where(dead == 0, mixed, 0.0)
    flat = jnp.concatenate([mixed[h * ROWS : (h + 1) * ROWS] for h in range(4)], axis=1)
    out_ref[TOK:, :] = jnp.concatenate([flat, jnp.zeros_like(flat)], axis=0).astype(bf16)


def attend(head, act, queries, cache_keys, cache_values, new_keys, new_values, lengths, ids):
    whole = lambda *shape: pl.BlockSpec(shape, lambda i, *_: (0,) * len(shape))
    cache = pl.BlockSpec((2, CACHE, HD), lambda i, m, *_: (0, m[0], 0))
    fresh = pl.BlockSpec((STEPS, 2, HD), lambda i, m, *_: (0, 0, m[0]))
    return pl.pallas_call(
        attend_kernel,
        out_shape=jax.ShapeDtypeStruct((TOK + PAD, FEAT), bf16),
        grid_spec=pltpu.PrefetchScalarGridSpec(
            num_scalar_prefetch=3,
            grid=(1,),
            in_specs=[whole(TOK, FEAT), whole(STEPS, 2, FEAT), cache, cache, fresh, fresh],
            out_specs=whole(TOK + PAD, FEAT),
            scratch_shapes=[
                pltpu.VMEM((ROWS, FEAT), f32),
                pltpu.VMEM((ROWS, HD), f32),
                pltpu.VMEM((ROWS, HD), f32),
            ],
        ),
        name="attend",
    )(head, lengths, ids, act, queries, cache_keys, cache_values, new_keys, new_values)


def gradient_kernel(table_ref, *refs):
    chunks, pairs, out_ref = (refs[:8], refs[8:16]), refs[16:20], refs[-4]
    chunk_rows, pair_rows, sems = refs[-3:]

    def accumulate(mine):
        copies = [
            pltpu.make_async_copy(ref, chunk_rows.at[n], sems.at[n]) for n, ref in enumerate(mine)
        ] + [
            pltpu.make_async_copy(ref, pair_rows.at[n], sems.at[8 + n])
            for n, ref in enumerate(pairs)
        ]
        for copy in copies:
            copy.start()
        out_ref[COLS:, :] = jnp.zeros((16 * ROWS, FEAT), f32)
        for copy in copies[8:]:
            copy.wait()
        for n in range(8):
            copies[n].wait()
            block = pair_rows[table_ref[16 + n], table_ref[24 + n]]
            part = jnp.dot(block, chunk_rows[n, :TOK, :], preferred_element_type=f32)
            if n == 0:
                out_ref[:COLS, :] = part
            else:
                out_ref[:COLS, :] += part
            place = pl.multiple_of(COLS + table_ref[8 + n] * ROWS, ROWS)
            out_ref[pl.ds(place, ROWS), :] = chunk_rows[n, TOK:, :].astype(f32)[:ROWS]

    for side in range(2):

        @pl.when(table_ref[0] == side)
        def _():
            accumulate(chunks[side])


def gradient(table, rollout_chunks, learner_chunks, pairs, others):
    hbm = pl.BlockSpec(memory_space=pl.ANY)
    operands = (*rollout_chunks, *learner_chunks, *pairs, *others)
    return pl.pallas_call(
        gradient_kernel,
        out_shape=jax.ShapeDtypeStruct((COLS + 16 * ROWS, FEAT), f32),
        in_specs=[pl.BlockSpec(memory_space=pltpu.SMEM)] + [hbm] * len(operands),
        out_specs=pl.BlockSpec(memory_space=pltpu.VMEM),
        scratch_shapes=[
            pltpu.VMEM((8, TOK + PAD, FEAT), bf16),
            pltpu.VMEM((4, 2, COLS, TOK), bf16),
            pltpu.SemaphoreType.DMA((12,)),
        ],
        compiler_params=pltpu.CompilerParams(vmem_limit_bytes=32 * 2**20),
        cost_estimate=pl.CostEstimate(
            flops=2 * 8 * TOK * COLS * FEAT, bytes_accessed=6 * 2**20, transcendentals=0
        ),
        name="gradient",
    )(table, *operands)


def step_kernel(
    table_ref, mine_ref, got_ref, one_ref, one_got, two_ref, two_got, weight_ref, update_ref, out_ref
):
    learner = table_ref[0] == 1
    grad = mine_ref[:COLS, :] + got_ref[:COLS, :]
    moment_one = jnp.where(learner, one_ref[...], one_got[...])
    moment_two = jnp.where(learner, two_ref[...], two_got[...])
    first_moment = beta_one * moment_one + (1.0 - beta_one) * grad
    second_moment = beta_two * moment_two + (1.0 - beta_two) * grad * grad
    update = (
        first_moment / first_bias / (jnp.sqrt(second_moment / second_bias) + epsilon)
    ).astype(bf16)
    update_ref[...] = update
    widened = weight_ref[...].astype(f32)
    renewed = (
        widened - learning_rate * (update.astype(f32) + weight_decay * widened)
    ).astype(bf16)
    rows = (mine_ref[COLS:, :] + got_ref[COLS:, :]).astype(bf16)
    part = lax.dot_general(rows, renewed, (((1,), (1,)), ((), ())), preferred_element_type=f32)
    out_ref[...] = part.reshape(16, ROWS, COLS)


def step(table, mine, got, one, one_got, two, two_got, weight):
    vmem = pl.BlockSpec(memory_space=pltpu.VMEM)
    return pl.pallas_call(
        step_kernel,
        out_shape=(
            jax.ShapeDtypeStruct((COLS, FEAT), bf16),
            jax.ShapeDtypeStruct((16, ROWS, COLS), f32),
        ),
        in_specs=[pl.BlockSpec(memory_space=pltpu.SMEM)] + [vmem] * 7,
        out_specs=(vmem, vmem),
        compiler_params=pltpu.CompilerParams(vmem_limit_bytes=32 * 2**20),
        name="step",
    )(table, mine, got, one, one_got, two, two_got, weight)


def local(
    activations,
    cotangent,
    weight,
    moment_one,
    moment_two,
    queries,
    cache_keys,
    cache_values,
    new_keys,
    new_values,
    lengths,
    token_ids,
):
    g = lax.axis_index("group")
    p = lax.axis_index("dp")
    q = lax.axis_index("tensor")
    flat = (g * 16 + p) * 16 + q
    table = lax.dynamic_slice_in_dim(jnp.asarray(device_table()), flat, 1, 0)[0]

    payload = attend(
        (q >> 1).reshape(1),
        activations[0],
        queries,
        cache_keys,
        cache_values,
        new_keys,
        new_values,
        lengths,
        token_ids.T,
    )
    relay = permute(payload, along_z(2, 1, 0))
    up = [payload, permute(payload, along_y(1, 1))]
    down = [permute(payload, along_y(-1, 1, 0))]

    cut = lax.dynamic_slice_in_dim(cotangent[0], q * COLS, COLS, 1).T
    own = permute(cut, cot_transposed)

    other = permute(relay, along_z(2, 0, 0))
    for _ in range(2):
        up.append(permute(up[-1], along_y(1, 1)))
    for _ in range(3):
        down.append(permute(down[-1], along_y(-1, 0)))

    parts = [own] + [permute(own, along_zl(flip)) for flip in (1, 2, 3)]
    pair = jnp.stack(
        [
            jnp.where(
                table[s] == 0,
                parts[0],
                jnp.where(table[s] == 1, parts[1], jnp.where(table[s] == 2, parts[2], parts[3])),
            )
            for s in (1, 2)
        ]
    )
    pairs = (
        pair,
        permute(pair, along_x(-1)),
        permute(pair, along_x(2)),
        permute(pair, along_x(1)),
    )

    other_up = [permute(other, along_y(1, 0, 1))]
    other_down = [other, permute(other, along_y(-1, 0))]
    for _ in range(3):
        other_up.append(permute(other_up[-1], along_y(1, 1)))
    for _ in range(2):
        other_down.append(permute(other_down[-1], along_y(-1, 0)))

    one, two = moment_one[0].T, moment_two[0].T
    one_got = permute(one, to_rollout)
    two_got = permute(two, to_rollout)

    mine = gradient(table, down + other_down, up + other_up, pairs, (one_got, two_got))
    got = permute(mine, other_core)
    update, partial = step(table, mine, got, one, one_got, two, two_got, weight.T)

    shares = lax.all_to_all(partial, "tensor", split_axis=0, concat_axis=0, tiled=True)
    summed = jnp.sum(shares, axis=0).astype(bf16)
    block = permute(summed, transposed)
    spread = jnp.broadcast_to(block[None], (16, ROWS, COLS))
    gathered = lax.all_to_all(spread, "tensor", split_axis=0, concat_axis=0, tiled=True)
    decoded = gathered.transpose(1, 0, 2).reshape(STEPS, ROWS // STEPS, D)
    return (update.T, decoded)


def solution(mesh):
    return jax.shard_map(
        local,
        mesh=mesh,
        in_specs=(
            P("group", "dp", "tensor"),
            P("group", "dp", None),
            P("tensor", "dp"),
            P("group", "tensor", "dp"),
            P("group", "tensor", "dp"),
            P(None, "dp", "tensor"),
            P("dp", None, None),
            P("dp", None, None),
            P(None, "dp", None),
            P(None, "dp", None),
            P("dp"),
            P(None, "dp"),
        ),
        out_specs=(P("tensor", "dp"), P(None, "dp", None)),
        check_vma=False,
    )
```

```python
import math

import jax
import jax.numpy as jnp
import numpy as np
from jax import lax
from jax.experimental import pallas as pl
from jax.experimental.pallas import tpu as pltpu
from jax.sharding import Mesh
from jax.sharding import PartitionSpec as P

D = 5120
KVH = 8
HD = 128
EOS = 151645
STEPS = 4
CACHE = 256

learning_rate = 0.0003
weight_decay = 0.1
beta_one = 0.9
beta_two = 0.95
first_bias = 1.0 - 0.9**10
second_bias = 1.0 - 0.95**10
epsilon = 1e-08

AXES = ("group", "y", "z_hi", "z_lo", "x")
SHAPE = (2, 8, 2, 4, 4)
DP, TENSOR = ("y", "z_hi"), ("z_lo", "x")
TOK = 256
FEAT = 512
COLS = 320
ROWS = 8
PAD = 16
f32, bf16 = jnp.float32, jnp.bfloat16


def permute(value, target):
    pairs = []
    for flat, place in enumerate(np.ndindex(*SHAPE)):
        to = target(*place)
        if to is not None:
            pairs.append((flat, int(np.ravel_multi_index(to, SHAPE))))
    return lax.ppermute(value, AXES, pairs)


def keeper(zh, x):
    return int((x & 1) == zh)


def to_partner(g, y, zh, zl, x):
    return (0, y, 1 - zh, zl, x) if g == 1 else None


def transposed(g, y, zh, zl, x):
    return (g, zl * 2 + (x >> 1), x & 1, y >> 1, (y & 1) * 2 + zh)


def cot_transposed(g, *place):
    _, y, zh, zl, x = transposed(g, *place)
    return (keeper(zh, x), y, zh, zl, x) if g == 1 else None


def along_zl(flip):
    return lambda g, y, zh, zl, x: (g, y, zh, zl ^ flip, x) if g == keeper(zh, x) else None


def along_x(step):
    return lambda g, y, zh, zl, x: (g, y, zh, zl, (x + step) % 4) if g == keeper(zh, x) else None


def other_core(g, y, zh, zl, x):
    return (1 - g, y, zh, zl, x)


def to_rollout(g, y, zh, zl, x):
    return (0, y, zh, zl, x) if g == 1 else None


FLIPS = (0, 3, 1, 2)


def device_table():
    table = np.zeros((512, 32), np.int32)
    for flat, (g, y, zh, zl, x) in enumerate(np.ndindex(*SHAPE)):
        token_zh = zh if g == 1 else 1 - zh
        table[flat, 0] = g
        table[flat, 1] = token_zh
        for n in range(8):
            table[flat, 8 + n] = (2 * (n & 1) + token_zh - x) % 4
            table[flat, 16 + n] = FLIPS.index(zl ^ (n >> 1))
    return table


def attend_kernel(
    head_ref, lengths_ref, ids_ref, q_ref, k_ref, v_ref, nk_ref, nv_ref, out_ref, q_rows, nk_rows, nv_rows
):
    for t in range(STEPS):
        place = slice(2 * t, 2 * t + 2)
        q_rows[place, :] = q_ref[t].astype(f32)
        nk_rows[place, :] = nk_ref[t].astype(f32)
        nv_rows[place, :] = nv_ref[t].astype(f32)
    queries = q_rows[...]
    query = jnp.concatenate(
        [queries[:, h * HD : (h + 1) * HD] for h in range(4)], axis=0
    ).astype(bf16)
    keys = k_ref[...].reshape(2 * CACHE, HD)
    values = v_ref[...].reshape(2 * CACHE, HD)
    fresh_keys = nk_rows[...].astype(bf16)
    fresh_values = nv_rows[...].astype(bf16)
    scale = 1.0 / math.sqrt(HD)
    nt = (((1,), (1,)), ((), ()))
    cache_scores = lax.dot_general(query, keys, nt, preferred_element_type=f32) * scale
    step_scores = lax.dot_general(query, fresh_keys, nt, preferred_element_type=f32) * scale
    count = 4 * ROWS

    def place(width):
        place_row = lax.broadcasted_iota(jnp.int32, (count, width), 0) & (ROWS - 1)
        place_key = lax.broadcasted_iota(jnp.int32, (count, width), 1)
        return place_row >> 1, place_row & 1, place_key

    step, row, key = place(2 * CACHE)
    length = jnp.where(row == 0, lengths_ref[0], lengths_ref[1])
    cache_valid = ((key >> 8) == row) & ((key & (CACHE - 1)) < length)
    step, row, key = place(ROWS)
    step_valid = ((key & 1) == row) & ((key >> 1) <= step)
    cache_scores = jnp.where(cache_valid, cache_scores, -jnp.inf)
    step_scores = jnp.where(step_valid, step_scores, -jnp.inf)
    peak = jnp.maximum(
        jnp.max(cache_scores, axis=-1, keepdims=True), jnp.max(step_scores, axis=-1, keepdims=True)
    )
    cache_exp = jnp.exp(cache_scores - peak)
    step_exp = jnp.exp(step_scores - peak)
    denominator = jnp.sum(cache_exp, axis=-1, keepdims=True) + jnp.sum(
        step_exp, axis=-1, keepdims=True
    )
    cache_probs = (cache_exp / denominator).astype(bf16)
    step_probs = (step_exp / denominator).astype(bf16)
    nn = (((1,), (0,)), ((), ()))
    mixed = lax.dot_general(cache_probs, values, nn, preferred_element_type=f32)
    mixed = mixed + lax.dot_general(step_probs, fresh_values, nn, preferred_element_type=f32)
    step, row, _ = place(HD)
    dead = jnp.zeros((count, HD), jnp.int32)
    for u in range(STEPS - 1):
        for r in range(2):
            ended = (ids_ref[r, u] == EOS).astype(jnp.int32)
            dead = dead + jnp.where((row == r) & (step > u), ended, 0)
    mixed = jnp.where(dead == 0, mixed, 0.0)
    flat = jnp.concatenate([mixed[h * ROWS : (h + 1) * ROWS] for h in range(4)], axis=1)
    out_ref[...] = jnp.concatenate([flat, jnp.zeros_like(flat)], axis=0).astype(bf16)


def attend(head, queries, cache_keys, cache_values, new_keys, new_values, lengths, ids):
    whole = lambda *shape: pl.BlockSpec(shape, lambda i, *_: (0,) * len(shape))
    cache = pl.BlockSpec((2, CACHE, HD), lambda i, m, *_: (0, m[0], 0))
    fresh = pl.BlockSpec((STEPS, 2, HD), lambda i, m, *_: (0, 0, m[0]))
    return pl.pallas_call(
        attend_kernel,
        out_shape=jax.ShapeDtypeStruct((PAD, FEAT), bf16),
        grid_spec=pltpu.PrefetchScalarGridSpec(
            num_scalar_prefetch=3,
            grid=(1,),
            in_specs=[whole(STEPS, 2, FEAT), cache, cache, fresh, fresh],
            out_specs=whole(PAD, FEAT),
            scratch_shapes=[
                pltpu.VMEM((ROWS, FEAT), f32),
                pltpu.VMEM((ROWS, HD), f32),
                pltpu.VMEM((ROWS, HD), f32),
            ],
        ),
        name="attend",
    )(head, lengths, ids, queries, cache_keys, cache_values, new_keys, new_values)


def base_kernel(table_ref, act_ref, act_got, rows_ref, rows_got, out_ref):
    @pl.when(table_ref[0] == 1)
    def _():
        out_ref[:TOK, :] = act_ref[...]
        out_ref[TOK:, :] = rows_ref[...]

    @pl.when(table_ref[0] == 0)
    def _():
        out_ref[:TOK, :] = act_got[...]
        out_ref[TOK:, :] = rows_got[...]


def base_of(table, *parts):
    vmem = pl.BlockSpec(memory_space=pltpu.VMEM)
    return pl.pallas_call(
        base_kernel,
        out_shape=jax.ShapeDtypeStruct((TOK + PAD, FEAT), bf16),
        in_specs=[pl.BlockSpec(memory_space=pltpu.SMEM)] + [vmem] * 4,
        out_specs=vmem,
        name="base",
    )(table, *parts)


def gradient_kernel(table_ref, chunks_ref, *refs):
    blocks, (out_ref, chunk_rows, block_rows, row_tiles, sems) = refs[:4], refs[-5:]
    act_copies = [
        pltpu.make_async_copy(
            chunks_ref.at[n, :TOK], chunk_rows.at[pl.ds(n * TOK, TOK)], sems.at[n]
        )
        for n in range(8)
    ]
    row_copies = [
        pltpu.make_async_copy(chunks_ref.at[n, TOK:], row_tiles.at[n], sems.at[16 + n])
        for n in range(8)
    ]
    for n in range(8):
        act_copies[n].start()
        for b in range(4):

            @pl.when(table_ref[8 + n] == b)
            def _():
                pltpu.make_async_copy(
                    blocks[b].at[table_ref[16 + n]],
                    block_rows.at[:, pl.ds(n * TOK, TOK)],
                    sems.at[8 + n],
                ).start()

        row_copies[n].start()
    out_ref[COLS:, :] = jnp.zeros((16 * ROWS, FEAT), f32)
    for half in range(2):
        for n in range(4 * half, 4 * half + 4):
            act_copies[n].wait()
            pltpu.make_async_copy(
                blocks[0].at[0], block_rows.at[:, pl.ds(n * TOK, TOK)], sems.at[8 + n]
            ).wait()
        span = pl.ds(half * 4 * TOK, 4 * TOK)
        part = jnp.dot(block_rows[:, span], chunk_rows[span, :], preferred_element_type=f32)
        if half == 0:
            out_ref[:COLS, :] = part
        else:
            out_ref[:COLS, :] += part
    for n in range(8):
        row_copies[n].wait()
        place = pl.multiple_of(COLS + (2 * n + table_ref[1]) * ROWS, ROWS)
        out_ref[pl.ds(place, ROWS), :] = row_tiles[n].astype(f32)[:ROWS]


def gradient(table, chunks, blocks, others):
    hbm = pl.BlockSpec(memory_space=pl.ANY)
    operands = (chunks, *blocks, *others)
    return pl.pallas_call(
        gradient_kernel,
        out_shape=jax.ShapeDtypeStruct((COLS + 16 * ROWS, FEAT), f32),
        in_specs=[pl.BlockSpec(memory_space=pltpu.SMEM)] + [hbm] * len(operands),
        out_specs=pl.BlockSpec(memory_space=pltpu.VMEM),
        scratch_shapes=[
            pltpu.VMEM((8 * TOK, FEAT), bf16),
            pltpu.VMEM((COLS, 8 * TOK), bf16),
            pltpu.VMEM((8, PAD, FEAT), bf16),
            pltpu.SemaphoreType.DMA((24,)),
        ],
        compiler_params=pltpu.CompilerParams(vmem_limit_bytes=32 * 2**20),
        cost_estimate=pl.CostEstimate(
            flops=2 * 8 * TOK * COLS * FEAT, bytes_accessed=6 * 2**20, transcendentals=0
        ),
        name="gradient",
    )(table, *operands)


def step_kernel(
    table_ref, mine_ref, got_ref, one_ref, one_got, two_ref, two_got, weight_ref, update_ref, out_ref
):
    learner = table_ref[0] == 1
    grad = mine_ref[:COLS, :] + got_ref[:COLS, :]
    moment_one = jnp.where(learner, one_ref[...], one_got[...])
    moment_two = jnp.where(learner, two_ref[...], two_got[...])
    first_moment = beta_one * moment_one + (1.0 - beta_one) * grad
    second_moment = beta_two * moment_two + (1.0 - beta_two) * grad * grad
    update = (
        first_moment / first_bias / (jnp.sqrt(second_moment / second_bias) + epsilon)
    ).astype(bf16)
    update_ref[...] = update
    widened = weight_ref[...].astype(f32)
    renewed = (
        widened - learning_rate * (update.astype(f32) + weight_decay * widened)
    ).astype(bf16)
    rows = (mine_ref[COLS:, :] + got_ref[COLS:, :]).astype(bf16)
    part = lax.dot_general(rows, renewed, (((1,), (1,)), ((), ())), preferred_element_type=f32)
    out_ref[...] = part.reshape(16, ROWS, COLS)


def step(table, mine, got, one, one_got, two, two_got, weight):
    vmem = pl.BlockSpec(memory_space=pltpu.VMEM)
    return pl.pallas_call(
        step_kernel,
        out_shape=(
            jax.ShapeDtypeStruct((COLS, FEAT), bf16),
            jax.ShapeDtypeStruct((16, ROWS, COLS), f32),
        ),
        in_specs=[pl.BlockSpec(memory_space=pltpu.SMEM)] + [vmem] * 7,
        out_specs=(vmem, vmem),
        compiler_params=pltpu.CompilerParams(vmem_limit_bytes=32 * 2**20),
        name="step",
    )(table, mine, got, one, one_got, two, two_got, weight)


def local(
    activations,
    cotangent,
    weight,
    moment_one,
    moment_two,
    queries,
    cache_keys,
    cache_values,
    new_keys,
    new_values,
    lengths,
    token_ids,
):
    flat, q = lax.axis_index(AXES), lax.axis_index(TENSOR)
    table = lax.dynamic_slice_in_dim(jnp.asarray(device_table()), flat, 1, 0)[0]

    act = activations[0]
    act_got = permute(act, to_partner)
    rows = attend(
        (q >> 1).reshape(1),
        queries,
        cache_keys,
        cache_values,
        new_keys,
        new_values,
        lengths,
        token_ids.T,
    )
    rows_got = permute(rows, to_partner)
    base = base_of(table, act, act_got, rows, rows_got)
    chunks = lax.all_gather(base, "y", axis=0)

    cut = lax.dynamic_slice_in_dim(cotangent[0], q * COLS, COLS, 1).T
    own = permute(cut, cot_transposed)
    two_blocks = jnp.stack([own, permute(own, along_zl(3))])
    four = jnp.concatenate([two_blocks, permute(two_blocks, along_zl(1))], axis=0)
    blocks = (
        four,
        permute(four, along_x(-1)),
        permute(four, along_x(2)),
        permute(four, along_x(1)),
    )

    one, two = moment_one[0].T, moment_two[0].T
    one_got = permute(one, to_rollout)
    two_got = permute(two, to_rollout)

    mine = gradient(table, chunks, blocks, (one_got, two_got))
    got = permute(mine, other_core)
    update, partial = step(table, mine, got, one, one_got, two, two_got, weight.T)

    shares = lax.all_to_all(partial, TENSOR, split_axis=0, concat_axis=0, tiled=True)
    summed = jnp.sum(shares, axis=0).astype(bf16)
    block = permute(summed, transposed)
    spread = jnp.broadcast_to(block[None], (16, ROWS, COLS))
    gathered = lax.all_to_all(spread, TENSOR, split_axis=0, concat_axis=0, tiled=True)
    decoded = gathered.transpose(1, 0, 2).reshape(STEPS, ROWS // STEPS, D)
    return (update.T, decoded)


def solution(mesh):
    fine = Mesh(mesh.devices.reshape(SHAPE), AXES)
    return jax.shard_map(
        local,
        mesh=fine,
        in_specs=(
            P("group", DP, TENSOR),
            P("group", DP, None),
            P(TENSOR, DP),
            P("group", TENSOR, DP),
            P("group", TENSOR, DP),
            P(None, DP, TENSOR),
            P(DP, None, None),
            P(DP, None, None),
            P(None, DP, None),
            P(None, DP, None),
            P(DP),
            P(None, DP),
        ),
        out_specs=(P(TENSOR, DP), P(None, DP, None)),
        check_vma=False,
    )
```

```python
import math

import jax
import jax.numpy as jnp
import numpy as np
from jax import lax
from jax.experimental import pallas as pl
from jax.experimental.pallas import tpu as pltpu
from jax.sharding import Mesh
from jax.sharding import PartitionSpec as P

D = 5120
KVH = 8
HD = 128
EOS = 151645
STEPS = 4
CACHE = 256

learning_rate = 0.0003
weight_decay = 0.1
beta_one = 0.9
beta_two = 0.95
first_bias = 1.0 - 0.9**10
second_bias = 1.0 - 0.95**10
epsilon = 1e-08

AXES = ("group", "y", "z_hi", "z_lo", "x")
SHAPE = (2, 8, 2, 4, 4)
DP, TENSOR = ("y", "z_hi"), ("z_lo", "x")
TOK = 256
HALF = 128
FEAT = 512
COLS = 320
ROWS = 8
PAD = 16
f32, bf16 = jnp.float32, jnp.bfloat16


def permute(value, target):
    pairs = []
    for flat, place in enumerate(np.ndindex(*SHAPE)):
        to = target(*place)
        if to is not None:
            pairs.append((flat, int(np.ravel_multi_index(to, SHAPE))))
    return lax.ppermute(value, AXES, pairs)


def to_partner(g, y, zh, zl, x):
    return (g, y, 1 - zh, zl, x)


def along_y(step):
    return lambda g, y, zh, zl, x: (g, (y + step) % 8, zh, zl, x)


def transposed(g, y, zh, zl, x):
    return (g, zl * 2 + (x >> 1), x & 1, y >> 1, (y & 1) * 2 + zh)


def cot_transposed(core):
    return lambda g, *place: (core, *transposed(g, *place)[1:]) if g == 1 else None


def along_zl(flip):
    return lambda g, y, zh, zl, x: (g, y, zh, zl ^ flip, x)


def along_x(step):
    return lambda g, y, zh, zl, x: (g, y, zh, zl, (x + step) % 4)


def other_core(g, y, zh, zl, x):
    return (1 - g, y, zh, zl, x)


def to_rollout(g, y, zh, zl, x):
    return (0, y, zh, zl, x) if g == 1 else None


HOPS = (0, 1, 2, 3, 4, -1, -2, -3)
FLIPS = (0, 3, 1, 2)


def device_table():
    table = np.zeros((512, 64), np.int32)
    for flat, (g, y, zh, zl, x) in enumerate(np.ndindex(*SHAPE)):
        start = (zl * 4 + x) * COLS
        table[flat, :3] = g, start // 128, start % 128
        for n, hop in enumerate(HOPS):
            for other in range(2):
                block_y, block_zh = (y - hop) % 8, zh ^ other
                at = n * 2 + other
                table[flat, 16 + at] = block_y * 2 + block_zh
                table[flat, 32 + at] = (2 * (block_y & 1) + block_zh - x) % 4
                table[flat, 48 + at] = FLIPS.index(zl ^ (block_y >> 1))
    return table


def attend_kernel(
    head_ref, lengths_ref, ids_ref, q_ref, k_ref, v_ref, nk_ref, nv_ref, out_ref, q_rows, nk_rows, nv_rows
):
    for t in range(STEPS):
        place = slice(2 * t, 2 * t + 2)
        q_rows[place, :] = q_ref[t].astype(f32)
        nk_rows[place, :] = nk_ref[t].astype(f32)
        nv_rows[place, :] = nv_ref[t].astype(f32)
    queries = q_rows[...]
    query = jnp.concatenate(
        [queries[:, h * HD : (h + 1) * HD] for h in range(4)], axis=0
    ).astype(bf16)
    keys = k_ref[...].reshape(2 * CACHE, HD)
    values = v_ref[...].reshape(2 * CACHE, HD)
    fresh_keys = nk_rows[...].astype(bf16)
    fresh_values = nv_rows[...].astype(bf16)
    scale = 1.0 / math.sqrt(HD)
    nt = (((1,), (1,)), ((), ()))
    cache_scores = lax.dot_general(query, keys, nt, preferred_element_type=f32) * scale
    step_scores = lax.dot_general(query, fresh_keys, nt, preferred_element_type=f32) * scale
    count = 4 * ROWS

    def place(width):
        place_row = lax.broadcasted_iota(jnp.int32, (count, width), 0) & (ROWS - 1)
        place_key = lax.broadcasted_iota(jnp.int32, (count, width), 1)
        return place_row >> 1, place_row & 1, place_key

    step, row, key = place(2 * CACHE)
    length = jnp.where(row == 0, lengths_ref[0], lengths_ref[1])
    cache_valid = ((key >> 8) == row) & ((key & (CACHE - 1)) < length)
    step, row, key = place(ROWS)
    step_valid = ((key & 1) == row) & ((key >> 1) <= step)
    cache_scores = jnp.where(cache_valid, cache_scores, -jnp.inf)
    step_scores = jnp.where(step_valid, step_scores, -jnp.inf)
    peak = jnp.maximum(
        jnp.max(cache_scores, axis=-1, keepdims=True), jnp.max(step_scores, axis=-1, keepdims=True)
    )
    cache_exp = jnp.exp(cache_scores - peak)
    step_exp = jnp.exp(step_scores - peak)
    denominator = jnp.sum(cache_exp, axis=-1, keepdims=True) + jnp.sum(
        step_exp, axis=-1, keepdims=True
    )
    cache_probs = (cache_exp / denominator).astype(bf16)
    step_probs = (step_exp / denominator).astype(bf16)
    nn = (((1,), (0,)), ((), ()))
    mixed = lax.dot_general(cache_probs, values, nn, preferred_element_type=f32)
    mixed = mixed + lax.dot_general(step_probs, fresh_values, nn, preferred_element_type=f32)
    step, row, _ = place(HD)
    dead = jnp.zeros((count, HD), jnp.int32)
    for u in range(STEPS - 1):
        for r in range(2):
            ended = (ids_ref[r, u] == EOS).astype(jnp.int32)
            dead = dead + jnp.where((row == r) & (step > u), ended, 0)
    mixed = jnp.where(dead == 0, mixed, 0.0)
    flat = jnp.concatenate([mixed[h * ROWS : (h + 1) * ROWS] for h in range(4)], axis=1)
    out_ref[...] = jnp.concatenate([flat, jnp.zeros_like(flat)], axis=0).astype(bf16)


def attend(head, queries, cache_keys, cache_values, new_keys, new_values, lengths, ids):
    whole = lambda *shape: pl.BlockSpec(shape, lambda i, *_: (0,) * len(shape))
    cache = pl.BlockSpec((2, CACHE, HD), lambda i, m, *_: (0, m[0], 0))
    fresh = pl.BlockSpec((STEPS, 2, HD), lambda i, m, *_: (0, 0, m[0]))
    return pl.pallas_call(
        attend_kernel,
        out_shape=jax.ShapeDtypeStruct((PAD, FEAT), bf16),
        grid_spec=pltpu.PrefetchScalarGridSpec(
            num_scalar_prefetch=3,
            grid=(1,),
            in_specs=[whole(STEPS, 2, FEAT), cache, cache, fresh, fresh],
            out_specs=whole(PAD, FEAT),
            scratch_shapes=[
                pltpu.VMEM((ROWS, FEAT), f32),
                pltpu.VMEM((ROWS, HD), f32),
                pltpu.VMEM((ROWS, HD), f32),
            ],
        ),
        name="attend",
    )(head, lengths, ids, queries, cache_keys, cache_values, new_keys, new_values)


VMEM = pl.BlockSpec(memory_space=pltpu.VMEM)
SMEM = pl.BlockSpec(memory_space=pltpu.SMEM)
HBM = pl.BlockSpec(memory_space=pl.ANY)


def half_kernel(table_ref, act_ref, act_got, rows_ref, out_ref):
    @pl.when(table_ref[0] == 1)
    def _():
        out_ref[:HALF, :] = act_ref[:HALF, :]

    @pl.when(table_ref[0] == 0)
    def _():
        out_ref[:HALF, :] = act_got[HALF:, :]

    out_ref[HALF:, :] = rows_ref[...]


def half_of(table, *parts):
    return pl.pallas_call(
        half_kernel,
        out_shape=jax.ShapeDtypeStruct((HALF + PAD, FEAT), bf16),
        in_specs=[SMEM] + [VMEM] * 3,
        out_specs=VMEM,
        name="half",
    )(table, *parts)


def base_kernel(mine_ref, got_ref, out_ref):
    out_ref[:HALF, :] = mine_ref[:HALF, :]
    out_ref[HALF:TOK, :] = got_ref[:HALF, :]
    rows = [ref[HALF:, :].astype(f32)[:ROWS] for ref in (mine_ref, got_ref)]
    out_ref[TOK:, :] = jnp.concatenate(rows, axis=0).astype(bf16)


def base_of(*parts):
    return pl.pallas_call(
        base_kernel,
        out_shape=jax.ShapeDtypeStruct((TOK + PAD, FEAT), bf16),
        in_specs=[VMEM] * 2,
        out_specs=VMEM,
        name="base",
    )(*parts)


def cut_kernel(table_ref, cot_ref, one_ref, two_ref, window, turned, sem):
    start = pl.multiple_of(table_ref[1] * 128, 128)
    copy = pltpu.make_async_copy(cot_ref.at[:, pl.ds(start, 384)], window, sem)
    copy.start()
    copy.wait()
    turned[...] = window[...].astype(f32).T
    place = pl.ds(pl.multiple_of(table_ref[2], 64), COLS)
    one_ref[...] = turned[place, :HALF].astype(bf16)
    two_ref[...] = turned[place, HALF:].astype(bf16)


def cut_of(table, cot):
    shape = jax.ShapeDtypeStruct((COLS, HALF), bf16)
    return pl.pallas_call(
        cut_kernel,
        out_shape=(shape, shape),
        in_specs=[SMEM, HBM],
        out_specs=(VMEM, VMEM),
        scratch_shapes=[
            pltpu.VMEM((TOK, 384), bf16),
            pltpu.VMEM((384, TOK), f32),
            pltpu.SemaphoreType.DMA(()),
        ],
        name="cut",
    )(table, cot)


def gradient_kernel(table_ref, *refs):
    chunks, blocks, (out_ref, rows_ref) = refs[:8], refs[8:12], refs[-7:-5]
    chunk_rows, block_tiles, block_rows, row_tiles, sems = refs[-5:]
    copies = [
        pltpu.make_async_copy(blocks[b], block_tiles.at[b], sems.at[b]) for b in range(4)
    ]
    act_copies = [
        pltpu.make_async_copy(
            chunks[n].at[:TOK], chunk_rows.at[pl.ds(n * TOK, TOK)], sems.at[4 + n]
        )
        for n in range(8)
    ]
    row_copies = [
        pltpu.make_async_copy(chunks[n].at[TOK:], row_tiles.at[n], sems.at[12 + n])
        for n in range(8)
    ]
    for copy in copies + act_copies + row_copies:
        copy.start()
    for copy in copies:
        copy.wait()
    for at in range(16):
        block_rows[:, at * HALF : (at + 1) * HALF] = block_tiles[
            table_ref[32 + at], table_ref[48 + at]
        ]
    for half in range(2):
        for n in range(4 * half, 4 * half + 4):
            act_copies[n].wait()
        span = pl.ds(half * 4 * TOK, 4 * TOK)
        part = jnp.dot(block_rows[:, span], chunk_rows[span, :], preferred_element_type=f32)
        if half == 0:
            out_ref[...] = part
        else:
            out_ref[...] += part
    for n in range(8):
        row_copies[n].wait()
        rows = row_tiles[n].astype(f32)
        for other in range(2):
            place = pl.multiple_of(table_ref[16 + 2 * n + other] * ROWS, ROWS)
            rows_ref[pl.ds(place, ROWS), :] = rows[other * ROWS : (other + 1) * ROWS]


def gradient(table, chunks, blocks, others):
    operands = (*chunks, *blocks, *others)
    return pl.pallas_call(
        gradient_kernel,
        out_shape=(
            jax.ShapeDtypeStruct((COLS, FEAT), f32),
            jax.ShapeDtypeStruct((16 * ROWS, FEAT), f32),
        ),
        in_specs=[SMEM] + [HBM] * len(operands),
        out_specs=(VMEM, VMEM),
        scratch_shapes=[
            pltpu.VMEM((8 * TOK, FEAT), bf16),
            pltpu.VMEM((4, 4, COLS, HALF), bf16),
            pltpu.VMEM((COLS, 8 * TOK), bf16),
            pltpu.VMEM((8, PAD, FEAT), bf16),
            pltpu.SemaphoreType.DMA((20,)),
        ],
        compiler_params=pltpu.CompilerParams(vmem_limit_bytes=32 * 2**20),
        cost_estimate=pl.CostEstimate(
            flops=2 * 8 * TOK * COLS * FEAT, bytes_accessed=6 * 2**20, transcendentals=0
        ),
        name="gradient",
    )(table, *operands)


def step_kernel(
    table_ref, mine_ref, got_ref, rows_ref, one_ref, one_got, two_ref, two_got, weight_ref, update_ref, out_ref
):
    learner = table_ref[0] == 1
    grad = mine_ref[...] + got_ref[...]
    moment_one = jnp.where(learner, one_ref[...], one_got[...])
    moment_two = jnp.where(learner, two_ref[...], two_got[...])
    first_moment = beta_one * moment_one + (1.0 - beta_one) * grad
    second_moment = beta_two * moment_two + (1.0 - beta_two) * grad * grad
    update = (
        first_moment / first_bias / (jnp.sqrt(second_moment / second_bias) + epsilon)
    ).astype(bf16)
    update_ref[...] = update
    widened = weight_ref[...].astype(f32)
    renewed = (
        widened - learning_rate * (update.astype(f32) + weight_decay * widened)
    ).astype(bf16)
    rows = rows_ref[...].astype(bf16)
    part = lax.dot_general(rows, renewed, (((1,), (1,)), ((), ())), preferred_element_type=f32)
    out_ref[...] = part.reshape(16, ROWS, COLS)


def step(table, mine, got, rows, one, one_got, two, two_got, weight):
    return pl.pallas_call(
        step_kernel,
        out_shape=(
            jax.ShapeDtypeStruct((COLS, FEAT), bf16),
            jax.ShapeDtypeStruct((16, ROWS, COLS), f32),
        ),
        in_specs=[SMEM] + [VMEM] * 8,
        out_specs=(VMEM, VMEM),
        compiler_params=pltpu.CompilerParams(vmem_limit_bytes=32 * 2**20),
        name="step",
    )(table, mine, got, rows, one, one_got, two, two_got, weight)


def local(
    activations,
    cotangent,
    weight,
    moment_one,
    moment_two,
    queries,
    cache_keys,
    cache_values,
    new_keys,
    new_values,
    lengths,
    token_ids,
):
    flat, q = lax.axis_index(AXES), lax.axis_index(TENSOR)
    table = lax.dynamic_slice_in_dim(jnp.asarray(device_table()), flat, 1, 0)[0]

    act = activations[0]
    act_got = permute(act, to_rollout)
    rows = attend(
        (q >> 1).reshape(1),
        queries,
        cache_keys,
        cache_values,
        new_keys,
        new_values,
        lengths,
        token_ids.T,
    )
    half = half_of(table, act, act_got, rows)
    base = base_of(half, permute(half, to_partner))

    cut_one, cut_two = cut_of(table, cotangent[0])
    own = permute(cut_one, cot_transposed(1)), permute(cut_two, cot_transposed(0))

    up, down = [base], [base]
    up.append(permute(base, along_y(1)))
    down.append(permute(base, along_y(-1)))

    own_one, own_two, _ = lax.optimization_barrier((*own, base))
    own = jnp.where(table[0] == 1, own_one, own_two)
    two_blocks = jnp.stack([own, permute(own, along_zl(3))])
    up.append(permute(up[-1], along_y(1)))
    down.append(permute(down[-1], along_y(-1)))
    four = jnp.concatenate([two_blocks, permute(two_blocks, along_zl(1))], axis=0)
    blocks = (
        four,
        permute(four, along_x(-1)),
        permute(four, along_x(2)),
        permute(four, along_x(1)),
    )
    up.append(permute(up[-1], along_y(1)))
    down.append(permute(down[-1], along_y(-1)))
    up.append(permute(up[-1], along_y(1)))
    chunks = up + down[1:]

    one, two = moment_one[0].T, moment_two[0].T
    one_tied, two_tied, _ = lax.optimization_barrier((one, two, base))
    one_got = permute(one_tied, to_rollout)
    two_got = permute(two_tied, to_rollout)

    mine, all_rows = gradient(table, chunks, blocks, (one_got, two_got))
    got = permute(mine, other_core)
    update, partial = step(table, mine, got, all_rows, one, one_got, two, two_got, weight.T)

    shares = lax.all_to_all(partial, TENSOR, split_axis=0, concat_axis=0, tiled=True)
    summed = jnp.sum(shares, axis=0).astype(bf16)
    block = permute(summed, transposed)
    spread = jnp.broadcast_to(block[None], (16, ROWS, COLS))
    gathered = lax.all_to_all(spread, TENSOR, split_axis=0, concat_axis=0, tiled=True)
    decoded = gathered.transpose(1, 0, 2).reshape(STEPS, ROWS // STEPS, D)
    return (update.T, decoded)


def solution(mesh):
    fine = Mesh(mesh.devices.reshape(SHAPE), AXES)
    return jax.shard_map(
        local,
        mesh=fine,
        in_specs=(
            P("group", DP, TENSOR),
            P("group", DP, None),
            P(TENSOR, DP),
            P("group", TENSOR, DP),
            P("group", TENSOR, DP),
            P(None, DP, TENSOR),
            P(DP, None, None),
            P(DP, None, None),
            P(None, DP, None),
            P(None, DP, None),
            P(DP),
            P(None, DP),
        ),
        out_specs=(P(TENSOR, DP), P(None, DP, None)),
        check_vma=False,
    )
```

```python
import math

import jax
import jax.numpy as jnp
import numpy as np
from jax import lax
from jax.experimental import pallas as pl
from jax.experimental.pallas import tpu as pltpu
from jax.sharding import Mesh
from jax.sharding import PartitionSpec as P

D = 5120
KVH = 8
HD = 128
EOS = 151645
STEPS = 4
CACHE = 256

learning_rate = 0.0003
weight_decay = 0.1
beta_one = 0.9
beta_two = 0.95
first_bias = 1.0 - 0.9**10
second_bias = 1.0 - 0.95**10
epsilon = 1e-08

AXES = ("group", "y", "z_hi", "z_lo", "x")
SHAPE = (2, 8, 2, 4, 4)
DP, TENSOR = ("y", "z_hi"), ("z_lo", "x")
TOK = 256
FEAT = 512
COLS = 320
ROWS = 8
PAD = 16
f32, bf16 = jnp.float32, jnp.bfloat16


def permute(value, target):
    pairs = []
    for flat, place in enumerate(np.ndindex(*SHAPE)):
        to = target(*place)
        if to is not None:
            pairs.append((flat, int(np.ravel_multi_index(to, SHAPE))))
    return lax.ppermute(value, AXES, pairs)


def on_learner(y, block_y):
    return (y - block_y) % 8 in (1, 2, 3, 4)


def keeper(y, zl, x):
    return int(on_learner(y, 2 * zl + (x >> 1)))


def half_to_partner(g, y, zh, zl, x):
    z = (zh * 4 + zl + (2 if g == 1 else -2)) % 8
    return (g, y, z // 4, z % 4, x)


def round_y(g, y, zh, zl, x):
    return (g, (y + (1 if g == 1 else -1)) % 8, zh, zl, x)


def last_round_y(g, y, zh, zl, x):
    return (g, (y + 1) % 8, zh, zl, x) if g == 1 else None


def transposed(g, y, zh, zl, x):
    return (g, zl * 2 + (x >> 1), x & 1, y >> 1, (y & 1) * 2 + zh)


def cot_transposed(g, *place):
    _, y, zh, zl, x = transposed(g, *place)
    return (keeper(y, zl, x), y, zh, zl, x) if g == 1 else None


def along_zl(flip):
    return lambda g, y, zh, zl, x: (g, y, zh, zl ^ flip, x) if g == keeper(y, zl, x) else None


def along_x(step):
    return lambda g, y, zh, zl, x: (g, y, zh, zl, (x + step) % 4)


def other_core(g, y, zh, zl, x):
    return (1 - g, y, zh, zl, x)


def to_rollout(g, y, zh, zl, x):
    return (0, y, zh, zl, x) if g == 1 else None


CHUNKS = (
    ((0, -1), (0, -2), (0, -3), (1, -1), (1, -2), (1, -3), (0, 0), (1, 0)),
    ((0, 1), (0, 2), (0, 3), (1, 1), (1, 2), (1, 3), (0, 4), (1, 4)),
)


def device_table():
    table = np.zeros((512, 32), np.int32)
    for flat, (g, y, zh, zl, x) in enumerate(np.ndindex(*SHAPE)):
        kept = [[z for z in range(4) if keeper(y, z, c) == g] for c in range(4)]
        start = (zl * 4 + x) * COLS
        table[flat, :3] = g, start // 128, start % 128
        table[flat, 3:5] = [z ^ zl for z in kept[x]]
        for n, (other, hop) in enumerate(CHUNKS[g]):
            block_y, block_zh = (y - hop) % 8, zh ^ other
            block_x = 2 * (block_y & 1) + block_zh
            table[flat, 8 + n] = block_y * 2 + block_zh
            table[flat, 16 + n] = (block_x - x) % 4
            table[flat, 24 + n] = kept[block_x].index(block_y >> 1)
    return table


def attend_kernel(
    head_ref, lengths_ref, ids_ref, q_ref, k_ref, v_ref, nk_ref, nv_ref, out_ref, q_rows, nk_rows, nv_rows
):
    for t in range(STEPS):
        place = slice(2 * t, 2 * t + 2)
        q_rows[place, :] = q_ref[t].astype(f32)
        nk_rows[place, :] = nk_ref[t].astype(f32)
        nv_rows[place, :] = nv_ref[t].astype(f32)
    queries = q_rows[...]
    query = jnp.concatenate(
        [queries[:, h * HD : (h + 1) * HD] for h in range(4)], axis=0
    ).astype(bf16)
    keys = k_ref[...].reshape(2 * CACHE, HD)
    values = v_ref[...].reshape(2 * CACHE, HD)
    fresh_keys = nk_rows[...].astype(bf16)
    fresh_values = nv_rows[...].astype(bf16)
    scale = 1.0 / math.sqrt(HD)
    nt = (((1,), (1,)), ((), ()))
    cache_scores = lax.dot_general(query, keys, nt, preferred_element_type=f32) * scale
    step_scores = lax.dot_general(query, fresh_keys, nt, preferred_element_type=f32) * scale
    count = 4 * ROWS

    def place(width):
        place_row = lax.broadcasted_iota(jnp.int32, (count, width), 0) & (ROWS - 1)
        place_key = lax.broadcasted_iota(jnp.int32, (count, width), 1)
        return place_row >> 1, place_row & 1, place_key

    step, row, key = place(2 * CACHE)
    length = jnp.where(row == 0, lengths_ref[0], lengths_ref[1])
    cache_valid = ((key >> 8) == row) & ((key & (CACHE - 1)) < length)
    step, row, key = place(ROWS)
    step_valid = ((key & 1) == row) & ((key >> 1) <= step)
    cache_scores = jnp.where(cache_valid, cache_scores, -jnp.inf)
    step_scores = jnp.where(step_valid, step_scores, -jnp.inf)
    peak = jnp.maximum(
        jnp.max(cache_scores, axis=-1, keepdims=True), jnp.max(step_scores, axis=-1, keepdims=True)
    )
    cache_exp = jnp.exp(cache_scores - peak)
    step_exp = jnp.exp(step_scores - peak)
    denominator = jnp.sum(cache_exp, axis=-1, keepdims=True) + jnp.sum(
        step_exp, axis=-1, keepdims=True
    )
    cache_probs = (cache_exp / denominator).astype(bf16)
    step_probs = (step_exp / denominator).astype(bf16)
    nn = (((1,), (0,)), ((), ()))
    mixed = lax.dot_general(cache_probs, values, nn, preferred_element_type=f32)
    mixed = mixed + lax.dot_general(step_probs, fresh_values, nn, preferred_element_type=f32)
    step, row, _ = place(HD)
    dead = jnp.zeros((count, HD), jnp.int32)
    for u in range(STEPS - 1):
        for r in range(2):
            ended = (ids_ref[r, u] == EOS).astype(jnp.int32)
            dead = dead + jnp.where((row == r) & (step > u), ended, 0)
    mixed = jnp.where(dead == 0, mixed, 0.0)
    flat = jnp.concatenate([mixed[h * ROWS : (h + 1) * ROWS] for h in range(4)], axis=1)
    out_ref[...] = jnp.concatenate([flat, jnp.zeros_like(flat)], axis=0).astype(bf16)


def attend(head, queries, cache_keys, cache_values, new_keys, new_values, lengths, ids):
    whole = lambda *shape: pl.BlockSpec(shape, lambda i, *_: (0,) * len(shape))
    cache = pl.BlockSpec((2, CACHE, HD), lambda i, m, *_: (0, m[0], 0))
    fresh = pl.BlockSpec((STEPS, 2, HD), lambda i, m, *_: (0, 0, m[0]))
    return pl.pallas_call(
        attend_kernel,
        out_shape=jax.ShapeDtypeStruct((PAD, FEAT), bf16),
        grid_spec=pltpu.PrefetchScalarGridSpec(
            num_scalar_prefetch=3,
            grid=(1,),
            in_specs=[whole(STEPS, 2, FEAT), cache, cache, fresh, fresh],
            out_specs=whole(PAD, FEAT),
            scratch_shapes=[
                pltpu.VMEM((ROWS, FEAT), f32),
                pltpu.VMEM((ROWS, HD), f32),
                pltpu.VMEM((ROWS, HD), f32),
            ],
        ),
        name="attend",
    )(head, lengths, ids, queries, cache_keys, cache_values, new_keys, new_values)


VMEM = pl.BlockSpec(memory_space=pltpu.VMEM)
SMEM = pl.BlockSpec(memory_space=pltpu.SMEM)
HBM = pl.BlockSpec(memory_space=pl.ANY)


def payload_kernel(table_ref, act_ref, act_got, rows_ref, out_ref):
    @pl.when(table_ref[0] == 1)
    def _():
        out_ref[:TOK, :] = act_ref[...]

    @pl.when(table_ref[0] == 0)
    def _():
        out_ref[:TOK, :] = act_got[...]

    out_ref[TOK:, :] = rows_ref[...]


def payload_of(table, *parts):
    return pl.pallas_call(
        payload_kernel,
        out_shape=jax.ShapeDtypeStruct((TOK + PAD, FEAT), bf16),
        in_specs=[SMEM] + [VMEM] * 3,
        out_specs=VMEM,
        name="payload",
    )(table, *parts)


def cut_kernel(table_ref, cot_ref, out_ref, window, turned, sem):
    start = pl.multiple_of(table_ref[1] * 128, 128)
    copy = pltpu.make_async_copy(cot_ref.at[:, pl.ds(start, 384)], window, sem)
    copy.start()
    copy.wait()
    turned[...] = window[...].astype(f32).T
    place = pl.ds(pl.multiple_of(table_ref[2], 64), COLS)
    out_ref[...] = turned[place, :].astype(bf16)


def cut_of(table, cot):
    return pl.pallas_call(
        cut_kernel,
        out_shape=jax.ShapeDtypeStruct((COLS, TOK), bf16),
        in_specs=[SMEM, HBM],
        out_specs=VMEM,
        scratch_shapes=[
            pltpu.VMEM((TOK, 384), bf16),
            pltpu.VMEM((384, TOK), f32),
            pltpu.SemaphoreType.DMA(()),
        ],
        name="cut",
    )(table, cot)


def gradient_kernel(table_ref, *refs):
    chunks, lasts, pairs, out_ref = refs[:6], (refs[6:8], refs[8:10]), refs[10:14], refs[-6]
    chunk_rows, pair_tiles, block_rows, row_tiles, sems = refs[-5:]

    def copies_of(n, ref):
        return (
            pltpu.make_async_copy(
                ref.at[:TOK], chunk_rows.at[pl.ds(n * TOK, TOK)], sems.at[4 + n]
            ),
            pltpu.make_async_copy(ref.at[TOK:], row_tiles.at[n], sems.at[12 + n]),
        )

    pair_copies = [
        pltpu.make_async_copy(pairs[b], pair_tiles.at[b], sems.at[b]) for b in range(4)
    ]
    for copy in pair_copies:
        copy.start()
    for n in range(6):
        for copy in copies_of(n, chunks[n]):
            copy.start()
    for side in range(2):

        @pl.when(table_ref[0] == side)
        def _():
            for n in range(2):
                for copy in copies_of(6 + n, lasts[side][n]):
                    copy.start()

    out_ref[COLS:, :] = jnp.zeros((16 * ROWS, FEAT), f32)
    for copy in pair_copies:
        copy.wait()
    for n in range(8):
        block_rows[:, n * TOK : (n + 1) * TOK] = pair_tiles[table_ref[16 + n], table_ref[24 + n]]
    waits = [copies_of(n, chunks[n] if n < 6 else lasts[0][n - 6]) for n in range(8)]
    for half in range(2):
        for n in range(4 * half, 4 * half + 4):
            waits[n][0].wait()
        span = pl.ds(half * 4 * TOK, 4 * TOK)
        part = jnp.dot(block_rows[:, span], chunk_rows[span, :], preferred_element_type=f32)
        if half == 0:
            out_ref[:COLS, :] = part
        else:
            out_ref[:COLS, :] += part
    for n in range(8):
        waits[n][1].wait()
        place = pl.multiple_of(COLS + table_ref[8 + n] * ROWS, ROWS)
        out_ref[pl.ds(place, ROWS), :] = row_tiles[n].astype(f32)[:ROWS]


def gradient(table, chunks, rollout_lasts, learner_lasts, pairs):
    operands = (*chunks, *rollout_lasts, *learner_lasts, *pairs)
    return pl.pallas_call(
        gradient_kernel,
        out_shape=jax.ShapeDtypeStruct((COLS + 16 * ROWS, FEAT), f32),
        in_specs=[SMEM] + [HBM] * len(operands),
        out_specs=VMEM,
        scratch_shapes=[
            pltpu.VMEM((8 * TOK, FEAT), bf16),
            pltpu.VMEM((4, 2, COLS, TOK), bf16),
            pltpu.VMEM((COLS, 8 * TOK), bf16),
            pltpu.VMEM((8, PAD, FEAT), bf16),
            pltpu.SemaphoreType.DMA((20,)),
        ],
        compiler_params=pltpu.CompilerParams(vmem_limit_bytes=32 * 2**20),
        cost_estimate=pl.CostEstimate(
            flops=2 * 8 * TOK * COLS * FEAT, bytes_accessed=6 * 2**20, transcendentals=0
        ),
        name="gradient",
    )(table, *operands)


def step_kernel(
    table_ref, mine_ref, got_ref, one_ref, one_got, two_ref, two_got, weight_ref, update_ref, out_ref
):
    learner = table_ref[0] == 1
    grad = mine_ref[:COLS, :] + got_ref[:COLS, :]
    moment_one = jnp.where(learner, one_ref[...], one_got[...])
    moment_two = jnp.where(learner, two_ref[...], two_got[...])
    first_moment = beta_one * moment_one + (1.0 - beta_one) * grad
    second_moment = beta_two * moment_two + (1.0 - beta_two) * grad * grad
    update = (
        first_moment / first_bias / (jnp.sqrt(second_moment / second_bias) + epsilon)
    ).astype(bf16)
    update_ref[...] = update
    widened = weight_ref[...].astype(f32)
    renewed = (
        widened - learning_rate * (update.astype(f32) + weight_decay * widened)
    ).astype(bf16)
    rows = (mine_ref[COLS:, :] + got_ref[COLS:, :]).astype(bf16)
    part = lax.dot_general(rows, renewed, (((1,), (1,)), ((), ())), preferred_element_type=f32)
    out_ref[...] = part.reshape(16, ROWS, COLS)


def step(table, mine, got, one, one_got, two, two_got, weight):
    return pl.pallas_call(
        step_kernel,
        out_shape=(
            jax.ShapeDtypeStruct((COLS, FEAT), bf16),
            jax.ShapeDtypeStruct((16, ROWS, COLS), f32),
        ),
        in_specs=[SMEM] + [VMEM] * 7,
        out_specs=(VMEM, VMEM),
        compiler_params=pltpu.CompilerParams(vmem_limit_bytes=32 * 2**20),
        name="step",
    )(table, mine, got, one, one_got, two, two_got, weight)


def local(
    activations,
    cotangent,
    weight,
    moment_one,
    moment_two,
    queries,
    cache_keys,
    cache_values,
    new_keys,
    new_values,
    lengths,
    token_ids,
):
    flat, q = lax.axis_index(AXES), lax.axis_index(TENSOR)
    table = lax.dynamic_slice_in_dim(jnp.asarray(device_table()), flat, 1, 0)[0]

    act = activations[0]
    act_got = permute(act, to_rollout)
    rows = attend(
        (q >> 1).reshape(1),
        queries,
        cache_keys,
        cache_values,
        new_keys,
        new_values,
        lengths,
        token_ids.T,
    )
    payload = payload_of(table, act, act_got, rows)
    relay = permute(payload, half_to_partner)
    ring = [payload, permute(payload, round_y)]

    cut = cut_of(table, cotangent[0])
    own = permute(cut, cot_transposed)

    relay, _, _ = lax.optimization_barrier((relay, ring[1], cut))
    other = permute(relay, half_to_partner)
    ring.append(permute(ring[1], round_y))
    one, two = moment_one[0].T, moment_two[0].T
    one_tied, two_tied, _ = lax.optimization_barrier((one, two, relay))
    one_got = permute(one_tied, to_rollout)
    two_got = permute(two_tied, to_rollout)

    other, one_got, two_got, own, ring[2] = lax.optimization_barrier(
        (other, one_got, two_got, own, ring[2])
    )
    other_ring = [other, permute(other, round_y)]
    ring.append(permute(ring[2], round_y))
    parts = [own] + [permute(own, along_zl(flip)) for flip in (1, 2, 3)]
    other_ring[1], ring[3], *parts = lax.optimization_barrier((other_ring[1], ring[3], *parts))
    pair = jnp.stack(
        [
            jnp.where(
                table[s] == 0,
                parts[0],
                jnp.where(table[s] == 1, parts[1], jnp.where(table[s] == 2, parts[2], parts[3])),
            )
            for s in (3, 4)
        ]
    )
    other_ring.append(permute(other_ring[1], round_y))
    ring.append(permute(ring[3], last_round_y))
    pairs = [pair] + [permute(pair, along_x(step)) for step in (-1, 2, 1)]
    other_ring[2], ring[4], pair = lax.optimization_barrier((other_ring[2], ring[4], pair))
    other_ring.append(permute(other_ring[2], round_y))
    other_ring[3], *pairs = lax.optimization_barrier((other_ring[3], *pairs))
    other_ring.append(permute(other_ring[3], last_round_y))

    mine = gradient(
        table,
        ring[1:4] + other_ring[1:4],
        (ring[0], other_ring[0]),
        (ring[4], other_ring[4]),
        pairs,
    )
    got = permute(mine, other_core)
    update, partial = step(table, mine, got, one, one_got, two, two_got, weight.T)

    shares = lax.all_to_all(partial, TENSOR, split_axis=0, concat_axis=0, tiled=True)
    summed = jnp.sum(shares, axis=0).astype(bf16)
    block = permute(summed, transposed)
    spread = jnp.broadcast_to(block[None], (16, ROWS, COLS))
    gathered = lax.all_to_all(spread, TENSOR, split_axis=0, concat_axis=0, tiled=True)
    decoded = gathered.transpose(1, 0, 2).reshape(STEPS, ROWS // STEPS, D)
    return (update.T, decoded)


def solution(mesh):
    fine = Mesh(mesh.devices.reshape(SHAPE), AXES)
    return jax.shard_map(
        local,
        mesh=fine,
        in_specs=(
            P("group", DP, TENSOR),
            P("group", DP, None),
            P(TENSOR, DP),
            P("group", TENSOR, DP),
            P("group", TENSOR, DP),
            P(None, DP, TENSOR),
            P(DP, None, None),
            P(DP, None, None),
            P(None, DP, None),
            P(None, DP, None),
            P(DP),
            P(None, DP),
        ),
        out_specs=(P(TENSOR, DP), P(None, DP, None)),
        check_vma=False,
    )
```

```python
import math

import jax
import jax.numpy as jnp
import numpy as np
from jax import lax
from jax.experimental import pallas as pl
from jax.experimental.pallas import tpu as pltpu
from jax.sharding import Mesh
from jax.sharding import PartitionSpec as P

D = 5120
KVH = 8
HD = 128
EOS = 151645
STEPS = 4
CACHE = 256

learning_rate = 0.0003
weight_decay = 0.1
beta_one = 0.9
beta_two = 0.95
first_bias = 1.0 - 0.9**10
second_bias = 1.0 - 0.95**10
epsilon = 1e-08

AXES = ("group", "y", "z_hi", "z_lo", "x")
SHAPE = (2, 8, 2, 4, 4)
DP, TENSOR = ("y", "z_hi"), ("z_lo", "x")
TOK = 256
HALF = 128
FEAT = 512
COLS = 320
PART = 80
ROWS = 8
PAD = 16
f32, bf16 = jnp.float32, jnp.bfloat16


def permute(value, target):
    pairs = []
    for flat, place in enumerate(np.ndindex(*SHAPE)):
        to = target(*place)
        if to is not None:
            pairs.append((flat, int(np.ravel_multi_index(to, SHAPE))))
    return lax.ppermute(value, AXES, pairs)


def gather(value, axes):
    return lax.all_to_all(value, axes, split_axis=0, concat_axis=0, tiled=True)


def to_partner(g, y, zh, zl, x):
    return (g, y, 1 - zh, zl, x)


def transposed(g, y, zh, zl, x):
    return (g, zl * 2 + (x >> 1), x & 1, y >> 1, (y & 1) * 2 + zh)


def other_core(g, y, zh, zl, x):
    return (1 - g, y, zh, zl, x)


def to_rollout(g, y, zh, zl, x):
    return (0, y, zh, zl, x) if g == 1 else None


def attend_kernel(
    head_ref, lengths_ref, ids_ref, q_ref, k_ref, v_ref, nk_ref, nv_ref, out_ref, q_rows, nk_rows, nv_rows
):
    for t in range(STEPS):
        place = slice(2 * t, 2 * t + 2)
        q_rows[place, :] = q_ref[t].astype(f32)
        nk_rows[place, :] = nk_ref[t].astype(f32)
        nv_rows[place, :] = nv_ref[t].astype(f32)
    queries = q_rows[...]
    query = jnp.concatenate(
        [queries[:, h * HD : (h + 1) * HD] for h in range(4)], axis=0
    ).astype(bf16)
    keys = k_ref[...].reshape(2 * CACHE, HD)
    values = v_ref[...].reshape(2 * CACHE, HD)
    fresh_keys = nk_rows[...].astype(bf16)
    fresh_values = nv_rows[...].astype(bf16)
    scale = 1.0 / math.sqrt(HD)
    nt = (((1,), (1,)), ((), ()))
    cache_scores = lax.dot_general(query, keys, nt, preferred_element_type=f32) * scale
    step_scores = lax.dot_general(query, fresh_keys, nt, preferred_element_type=f32) * scale
    count = 4 * ROWS

    def place(width):
        place_row = lax.broadcasted_iota(jnp.int32, (count, width), 0) & (ROWS - 1)
        place_key = lax.broadcasted_iota(jnp.int32, (count, width), 1)
        return place_row >> 1, place_row & 1, place_key

    step, row, key = place(2 * CACHE)
    length = jnp.where(row == 0, lengths_ref[0], lengths_ref[1])
    cache_valid = ((key >> 8) == row) & ((key & (CACHE - 1)) < length)
    step, row, key = place(ROWS)
    step_valid = ((key & 1) == row) & ((key >> 1) <= step)
    cache_scores = jnp.where(cache_valid, cache_scores, -jnp.inf)
    step_scores = jnp.where(step_valid, step_scores, -jnp.inf)
    peak = jnp.maximum(
        jnp.max(cache_scores, axis=-1, keepdims=True), jnp.max(step_scores, axis=-1, keepdims=True)
    )
    cache_exp = jnp.exp(cache_scores - peak)
    step_exp = jnp.exp(step_scores - peak)
    denominator = jnp.sum(cache_exp, axis=-1, keepdims=True) + jnp.sum(
        step_exp, axis=-1, keepdims=True
    )
    cache_probs = (cache_exp / denominator).astype(bf16)
    step_probs = (step_exp / denominator).astype(bf16)
    nn = (((1,), (0,)), ((), ()))
    mixed = lax.dot_general(cache_probs, values, nn, preferred_element_type=f32)
    mixed = mixed + lax.dot_general(step_probs, fresh_values, nn, preferred_element_type=f32)
    step, row, _ = place(HD)
    dead = jnp.zeros((count, HD), jnp.int32)
    for u in range(STEPS - 1):
        for r in range(2):
            ended = (ids_ref[r, u] == EOS).astype(jnp.int32)
            dead = dead + jnp.where((row == r) & (step > u), ended, 0)
    mixed = jnp.where(dead == 0, mixed, 0.0)
    flat = jnp.concatenate([mixed[h * ROWS : (h + 1) * ROWS] for h in range(4)], axis=1)
    out_ref[...] = jnp.concatenate([flat, jnp.zeros_like(flat)], axis=0).astype(bf16)


def attend(head, queries, cache_keys, cache_values, new_keys, new_values, lengths, ids):
    whole = lambda *shape: pl.BlockSpec(shape, lambda i, *_: (0,) * len(shape))
    cache = pl.BlockSpec((2, CACHE, HD), lambda i, m, *_: (0, m[0], 0))
    fresh = pl.BlockSpec((STEPS, 2, HD), lambda i, m, *_: (0, 0, m[0]))
    return pl.pallas_call(
        attend_kernel,
        out_shape=jax.ShapeDtypeStruct((PAD, FEAT), bf16),
        grid_spec=pltpu.PrefetchScalarGridSpec(
            num_scalar_prefetch=3,
            grid=(1,),
            in_specs=[whole(STEPS, 2, FEAT), cache, cache, fresh, fresh],
            out_specs=whole(PAD, FEAT),
            scratch_shapes=[
                pltpu.VMEM((ROWS, FEAT), f32),
                pltpu.VMEM((ROWS, HD), f32),
                pltpu.VMEM((ROWS, HD), f32),
            ],
        ),
        name="attend",
    )(head, lengths, ids, queries, cache_keys, cache_values, new_keys, new_values)


VMEM = pl.BlockSpec(memory_space=pltpu.VMEM)
SMEM = pl.BlockSpec(memory_space=pltpu.SMEM)
HBM = pl.BlockSpec(memory_space=pl.ANY)


def half_kernel(place_ref, act_ref, act_got, rows_ref, out_ref, spread_ref):
    @pl.when(place_ref[0] == 1)
    def _():
        out_ref[:HALF, :] = act_ref[:HALF, :]

    @pl.when(place_ref[0] == 0)
    def _():
        out_ref[:HALF, :] = act_got[HALF:, :]

    out_ref[HALF:, :] = rows_ref[...]
    for n in range(8):
        spread_ref[n] = out_ref[...]


def half_of(place, *parts):
    return pl.pallas_call(
        half_kernel,
        out_shape=(
            jax.ShapeDtypeStruct((HALF + PAD, FEAT), bf16),
            jax.ShapeDtypeStruct((8, HALF + PAD, FEAT), bf16),
        ),
        in_specs=[SMEM] + [VMEM] * 3,
        out_specs=(VMEM, VMEM),
        name="half",
    )(place, *parts)


def cut_kernel(place_ref, cot_ref, cot_got, out_ref, rows, turned, sem):
    @pl.when(place_ref[0] == 1)
    def _():
        pltpu.make_async_copy(cot_ref.at[:HALF], rows, sem).start()

    @pl.when(place_ref[0] == 0)
    def _():
        pltpu.make_async_copy(cot_got, rows, sem).start()

    pltpu.make_async_copy(cot_got, rows, sem).wait()
    for n in range(D // HALF):
        span = slice(n * HALF, (n + 1) * HALF)
        turned[span, :] = rows[:, span].astype(f32).T
    for n in range(16):
        start = pl.multiple_of(n * COLS + place_ref[4] * PART, 16)
        out_ref[n] = turned[pl.ds(start, PART), :].astype(bf16)


def cut_of(place, cot, cot_got):
    return pl.pallas_call(
        cut_kernel,
        out_shape=jax.ShapeDtypeStruct((16, PART, HALF), bf16),
        in_specs=[SMEM, HBM, HBM],
        out_specs=VMEM,
        scratch_shapes=[
            pltpu.VMEM((HALF, D), bf16),
            pltpu.VMEM((D, HALF), f32),
            pltpu.SemaphoreType.DMA(()),
        ],
        compiler_params=pltpu.CompilerParams(vmem_limit_bytes=32 * 2**20),
        name="cut",
    )(place, cot, cot_got)


def gradient_kernel(place_ref, own_ref, other_ref, blocks_ref, *refs):
    out_ref, rows_ref, chunk_rows, row_tiles, block_tiles, block_rows, sems = refs[-7:]
    sides = (own_ref, other_ref)
    copies = [pltpu.make_async_copy(blocks_ref, block_tiles, sems.at[0])]
    for n, ref in enumerate(sides):
        copies.append(
            pltpu.make_async_copy(ref.at[:, :HALF], chunk_rows.at[n], sems.at[1 + n])
        )
    for n, ref in enumerate(sides):
        copies.append(pltpu.make_async_copy(ref.at[:, HALF:], row_tiles.at[n], sems.at[3 + n]))
    for copy in copies:
        copy.start()
    copies[0].wait()
    z_hi = place_ref[2]
    for n in range(2):
        for y in range(8):
            span = slice((n * 8 + y) * HALF, (n * 8 + y + 1) * HALF)
            block = 2 * y + (z_hi if n == 0 else 1 - z_hi)
            for x in range(4):
                block_rows[x * PART : (x + 1) * PART, span] = block_tiles[x, block]
    for n in range(2):
        copies[1 + n].wait()
        span = slice(n * 8 * HALF, (n + 1) * 8 * HALF)
        part = jnp.dot(
            block_rows[:, span],
            chunk_rows[n].reshape(8 * HALF, FEAT),
            preferred_element_type=f32,
        )
        if n == 0:
            out_ref[...] = part
        else:
            out_ref[...] += part
    for n in range(2):
        copies[3 + n].wait()
        for y in range(8):
            block = 2 * y + (z_hi if n == 0 else 1 - z_hi)
            place = pl.multiple_of(block * ROWS, ROWS)
            rows_ref[pl.ds(place, ROWS), :] = row_tiles[n, y].astype(f32)[:ROWS]


def gradient(place, own, other, blocks, others):
    operands = (own, other, blocks, *others)
    return pl.pallas_call(
        gradient_kernel,
        out_shape=(
            jax.ShapeDtypeStruct((COLS, FEAT), f32),
            jax.ShapeDtypeStruct((16 * ROWS, FEAT), f32),
        ),
        in_specs=[SMEM] + [HBM] * len(operands),
        out_specs=(VMEM, VMEM),
        scratch_shapes=[
            pltpu.VMEM((2, 8, HALF, FEAT), bf16),
            pltpu.VMEM((2, 8, PAD, FEAT), bf16),
            pltpu.VMEM((4, 16, PART, HALF), bf16),
            pltpu.VMEM((COLS, 16 * HALF), bf16),
            pltpu.SemaphoreType.DMA((5,)),
        ],
        compiler_params=pltpu.CompilerParams(vmem_limit_bytes=32 * 2**20),
        cost_estimate=pl.CostEstimate(
            flops=2 * 8 * TOK * COLS * FEAT, bytes_accessed=6 * 2**20, transcendentals=0
        ),
        name="gradient",
    )(place, *operands)


def step_kernel(
    table_ref, mine_ref, got_ref, rows_ref, one_ref, one_got, two_ref, two_got, weight_ref, update_ref, out_ref
):
    learner = table_ref[0] == 1
    grad = mine_ref[...] + got_ref[...]
    moment_one = jnp.where(learner, one_ref[...], one_got[...])
    moment_two = jnp.where(learner, two_ref[...], two_got[...])
    first_moment = beta_one * moment_one + (1.0 - beta_one) * grad
    second_moment = beta_two * moment_two + (1.0 - beta_two) * grad * grad
    update = (
        first_moment / first_bias / (jnp.sqrt(second_moment / second_bias) + epsilon)
    ).astype(bf16)
    update_ref[...] = update
    widened = weight_ref[...].astype(f32)
    renewed = (
        widened - learning_rate * (update.astype(f32) + weight_decay * widened)
    ).astype(bf16)
    rows = rows_ref[...].astype(bf16)
    part = lax.dot_general(rows, renewed, (((1,), (1,)), ((), ())), preferred_element_type=f32)
    out_ref[...] = part.reshape(16, ROWS, COLS)


def step(table, mine, got, rows, one, one_got, two, two_got, weight):
    return pl.pallas_call(
        step_kernel,
        out_shape=(
            jax.ShapeDtypeStruct((COLS, FEAT), bf16),
            jax.ShapeDtypeStruct((16, ROWS, COLS), f32),
        ),
        in_specs=[SMEM] + [VMEM] * 8,
        out_specs=(VMEM, VMEM),
        compiler_params=pltpu.CompilerParams(vmem_limit_bytes=32 * 2**20),
        name="step",
    )(table, mine, got, rows, one, one_got, two, two_got, weight)


def local(
    activations,
    cotangent,
    weight,
    moment_one,
    moment_two,
    queries,
    cache_keys,
    cache_values,
    new_keys,
    new_values,
    lengths,
    token_ids,
):
    q = lax.axis_index(TENSOR)
    place = jnp.stack([lax.axis_index(axis) for axis in AXES]).astype(jnp.int32)

    act, cot = activations[0], cotangent[0]
    act_got = permute(act, to_rollout)
    cot_got = permute(cot[HALF:], to_rollout)
    rows = attend(
        (q >> 1).reshape(1),
        queries,
        cache_keys,
        cache_values,
        new_keys,
        new_values,
        lengths,
        token_ids.T,
    )
    half, spread = half_of(place, act, act_got, rows)
    own = gather(spread, "y")
    half_got = permute(half, to_partner)
    other = gather(jnp.broadcast_to(half_got[None], (8, HALF + PAD, FEAT)), "y")

    cut = cut_of(place, cot, cot_got)
    parts = gather(cut, DP)
    blocks = gather(jnp.broadcast_to(parts[None], (4, 16, PART, HALF)), "x")

    one, two = moment_one[0].T, moment_two[0].T
    one_tied, two_tied, _ = lax.optimization_barrier((one, two, half))
    one_got = permute(one_tied, to_rollout)
    two_got = permute(two_tied, to_rollout)

    mine, all_rows = gradient(place, own, other, blocks, (one_got, two_got))
    got = permute(mine, other_core)
    update, partial = step(place, mine, got, all_rows, one, one_got, two, two_got, weight.T)

    shares = gather(partial, TENSOR)
    summed = jnp.sum(shares, axis=0).astype(bf16)
    block = permute(summed, transposed)
    spread = jnp.broadcast_to(block[None], (16, ROWS, COLS))
    gathered = gather(spread, TENSOR)
    decoded = gathered.transpose(1, 0, 2).reshape(STEPS, ROWS // STEPS, D)
    return (update.T, decoded)


def solution(mesh):
    fine = Mesh(mesh.devices.reshape(SHAPE), AXES)
    return jax.shard_map(
        local,
        mesh=fine,
        in_specs=(
            P("group", DP, TENSOR),
            P("group", DP, None),
            P(TENSOR, DP),
            P("group", TENSOR, DP),
            P("group", TENSOR, DP),
            P(None, DP, TENSOR),
            P(DP, None, None),
            P(DP, None, None),
            P(None, DP, None),
            P(None, DP, None),
            P(DP),
            P(None, DP),
        ),
        out_specs=(P(TENSOR, DP), P(None, DP, None)),
        check_vma=False,
    )
```

```python
import math

import jax
import jax.numpy as jnp
import numpy as np
from jax import lax
from jax.experimental import pallas as pl
from jax.experimental.pallas import tpu as pltpu
from jax.sharding import Mesh
from jax.sharding import PartitionSpec as P

D = 5120
KVH = 8
HD = 128
EOS = 151645
STEPS = 4
CACHE = 256

learning_rate = 0.0003
weight_decay = 0.1
beta_one = 0.9
beta_two = 0.95
first_bias = 1.0 - 0.9**10
second_bias = 1.0 - 0.95**10
epsilon = 1e-08

AXES = ("group", "y", "z_hi", "z_lo", "x")
SHAPE = (2, 8, 2, 4, 4)
DP, TENSOR = ("y", "z_hi"), ("z_lo", "x")
TOK = 256
HALF = 128
FEAT = 512
COLS = 320
ROWS = 8
PAD = 16
f32, bf16 = jnp.float32, jnp.bfloat16


def permute(value, target):
    pairs = []
    for flat, place in enumerate(np.ndindex(*SHAPE)):
        to = target(*place)
        if to is not None:
            pairs.append((flat, int(np.ravel_multi_index(to, SHAPE))))
    return lax.ppermute(value, AXES, pairs)


def to_partner(g, y, zh, zl, x):
    return (g, y, 1 - zh, zl, x)


def along_y(step):
    return lambda g, y, zh, zl, x: (g, (y + (step if g == 1 else -step)) % 8, zh, zl, x)


def transposed(g, y, zh, zl, x):
    return (g, zl * 2 + (x >> 1), x & 1, y >> 1, (y & 1) * 2 + zh)


def cot_transposed(core):
    return lambda g, *place: (core, *transposed(g, *place)[1:]) if g == 1 else None


def along_zl(flip):
    return lambda g, y, zh, zl, x: (g, y, zh, zl ^ flip, x)


def along_x(step):
    return lambda g, y, zh, zl, x: (g, y, zh, zl, (x + (step if g == 1 else -step)) % 4)


def other_core(g, y, zh, zl, x):
    return (1 - g, y, zh, zl, x)


def to_rollout(g, y, zh, zl, x):
    return (0, y, zh, zl, x) if g == 1 else None


HOPS = (0, 1, 2, 3, 4, -1, -2, -3)
FLIPS = (0, 3, 1, 2)


def attend_kernel(
    head_ref, lengths_ref, ids_ref, q_ref, k_ref, v_ref, nk_ref, nv_ref, out_ref, q_rows, nk_rows, nv_rows
):
    for t in range(STEPS):
        place = slice(2 * t, 2 * t + 2)
        q_rows[place, :] = q_ref[t].astype(f32)
        nk_rows[place, :] = nk_ref[t].astype(f32)
        nv_rows[place, :] = nv_ref[t].astype(f32)
    queries = q_rows[...]
    query = jnp.concatenate(
        [queries[:, h * HD : (h + 1) * HD] for h in range(4)], axis=0
    ).astype(bf16)
    keys = k_ref[...].reshape(2 * CACHE, HD)
    values = v_ref[...].reshape(2 * CACHE, HD)
    fresh_keys = nk_rows[...].astype(bf16)
    fresh_values = nv_rows[...].astype(bf16)
    scale = 1.0 / math.sqrt(HD)
    nt = (((1,), (1,)), ((), ()))
    cache_scores = lax.dot_general(query, keys, nt, preferred_element_type=f32) * scale
    step_scores = lax.dot_general(query, fresh_keys, nt, preferred_element_type=f32) * scale
    count = 4 * ROWS

    def place(width):
        place_row = lax.broadcasted_iota(jnp.int32, (count, width), 0) & (ROWS - 1)
        place_key = lax.broadcasted_iota(jnp.int32, (count, width), 1)
        return place_row >> 1, place_row & 1, place_key

    step, row, key = place(2 * CACHE)
    length = jnp.where(row == 0, lengths_ref[0], lengths_ref[1])
    cache_valid = ((key >> 8) == row) & ((key & (CACHE - 1)) < length)
    step, row, key = place(ROWS)
    step_valid = ((key & 1) == row) & ((key >> 1) <= step)
    cache_scores = jnp.where(cache_valid, cache_scores, -jnp.inf)
    step_scores = jnp.where(step_valid, step_scores, -jnp.inf)
    peak = jnp.maximum(
        jnp.max(cache_scores, axis=-1, keepdims=True), jnp.max(step_scores, axis=-1, keepdims=True)
    )
    cache_exp = jnp.exp(cache_scores - peak)
    step_exp = jnp.exp(step_scores - peak)
    denominator = jnp.sum(cache_exp, axis=-1, keepdims=True) + jnp.sum(
        step_exp, axis=-1, keepdims=True
    )
    cache_probs = (cache_exp / denominator).astype(bf16)
    step_probs = (step_exp / denominator).astype(bf16)
    nn = (((1,), (0,)), ((), ()))
    mixed = lax.dot_general(cache_probs, values, nn, preferred_element_type=f32)
    mixed = mixed + lax.dot_general(step_probs, fresh_values, nn, preferred_element_type=f32)
    step, row, _ = place(HD)
    dead = jnp.zeros((count, HD), jnp.int32)
    for u in range(STEPS - 1):
        for r in range(2):
            ended = (ids_ref[r, u] == EOS).astype(jnp.int32)
            dead = dead + jnp.where((row == r) & (step > u), ended, 0)
    mixed = jnp.where(dead == 0, mixed, 0.0)
    flat = jnp.concatenate([mixed[h * ROWS : (h + 1) * ROWS] for h in range(4)], axis=1)
    out_ref[...] = jnp.concatenate([flat, jnp.zeros_like(flat)], axis=0).astype(bf16)


def attend(head, queries, cache_keys, cache_values, new_keys, new_values, lengths, ids):
    whole = lambda *shape: pl.BlockSpec(shape, lambda i, *_: (0,) * len(shape))
    cache = pl.BlockSpec((2, CACHE, HD), lambda i, m, *_: (0, m[0], 0))
    fresh = pl.BlockSpec((STEPS, 2, HD), lambda i, m, *_: (0, 0, m[0]))
    return pl.pallas_call(
        attend_kernel,
        out_shape=jax.ShapeDtypeStruct((PAD, FEAT), bf16),
        grid_spec=pltpu.PrefetchScalarGridSpec(
            num_scalar_prefetch=3,
            grid=(1,),
            in_specs=[whole(STEPS, 2, FEAT), cache, cache, fresh, fresh],
            out_specs=whole(PAD, FEAT),
            scratch_shapes=[
                pltpu.VMEM((ROWS, FEAT), f32),
                pltpu.VMEM((ROWS, HD), f32),
                pltpu.VMEM((ROWS, HD), f32),
            ],
        ),
        name="attend",
    )(head, lengths, ids, queries, cache_keys, cache_values, new_keys, new_values)


VMEM = pl.BlockSpec(memory_space=pltpu.VMEM)
SMEM = pl.BlockSpec(memory_space=pltpu.SMEM)
HBM = pl.BlockSpec(memory_space=pl.ANY)


def half_kernel(place_ref, act_ref, act_got, rows_ref, out_ref):
    @pl.when(place_ref[0] == 1)
    def _():
        out_ref[:HALF, :] = act_ref[:HALF, :]

    @pl.when(place_ref[0] == 0)
    def _():
        out_ref[:HALF, :] = act_got[HALF:, :]

    out_ref[HALF:, :] = rows_ref[...]


def half_of(place, *parts):
    return pl.pallas_call(
        half_kernel,
        out_shape=jax.ShapeDtypeStruct((HALF + PAD, FEAT), bf16),
        in_specs=[SMEM] + [VMEM] * 3,
        out_specs=VMEM,
        name="half",
    )(place, *parts)


def base_kernel(mine_ref, got_ref, *refs):
    out_ref = refs[-1]
    out_ref[:HALF, :] = mine_ref[:HALF, :]
    out_ref[HALF:TOK, :] = got_ref[:HALF, :]
    rows = [ref[HALF:, :].astype(f32)[:ROWS] for ref in (mine_ref, got_ref)]
    out_ref[TOK:, :] = jnp.concatenate(rows, axis=0).astype(bf16)


def base_of(parts, others):
    return pl.pallas_call(
        base_kernel,
        out_shape=jax.ShapeDtypeStruct((TOK + PAD, FEAT), bf16),
        in_specs=[VMEM] * 2 + [HBM] * len(others),
        out_specs=VMEM,
        name="base",
    )(*parts, *others)


def cut_kernel(place_ref, cot_ref, one_ref, two_ref, window, turned, sem):
    q = place_ref[3] * 4 + place_ref[4]
    start = pl.multiple_of(((q * 5) >> 1) * 128, 128)
    copy = pltpu.make_async_copy(cot_ref.at[:, pl.ds(start, 384)], window, sem)
    copy.start()
    copy.wait()
    turned[...] = window[...].astype(f32).T
    place = pl.ds(pl.multiple_of((q & 1) * 64, 64), COLS)
    one_ref[...] = turned[place, :HALF].astype(bf16)
    two_ref[...] = turned[place, HALF:].astype(bf16)


def cut_of(place, cot):
    shape = jax.ShapeDtypeStruct((COLS, HALF), bf16)
    return pl.pallas_call(
        cut_kernel,
        out_shape=(shape, shape),
        in_specs=[SMEM, HBM],
        out_specs=(VMEM, VMEM),
        scratch_shapes=[
            pltpu.VMEM((TOK, 384), bf16),
            pltpu.VMEM((384, TOK), f32),
            pltpu.SemaphoreType.DMA(()),
        ],
        name="cut",
    )(place, cot)


def gradient_kernel(place_ref, *refs):
    chunks, blocks, (out_ref, rows_ref) = refs[:8], refs[8:12], refs[-7:-5]
    chunk_rows, block_tiles, block_rows, row_tiles, sems = refs[-5:]
    copies = [
        pltpu.make_async_copy(blocks[b], block_tiles.at[b], sems.at[b]) for b in range(4)
    ]
    act_copies = [
        pltpu.make_async_copy(
            chunks[n].at[:TOK], chunk_rows.at[pl.ds(n * TOK, TOK)], sems.at[4 + n]
        )
        for n in range(8)
    ]
    row_copies = [
        pltpu.make_async_copy(chunks[n].at[TOK:], row_tiles.at[n], sems.at[12 + n])
        for n in range(8)
    ]
    for copy in copies + act_copies + row_copies:
        copy.start()
    for copy in copies:
        copy.wait()
    side, y, z_hi, z_lo, x = (place_ref[n] for n in range(5))
    places = []
    for at in range(16):
        hop, block_zh = HOPS[at // 2], (z_hi if at % 2 == 0 else 1 - z_hi)
        block_y = jnp.where(side == 1, y - hop, y + hop) & 7
        source = 2 * (block_y & 1) + block_zh - x
        source = jnp.where(side == 1, -source, source) & 3
        flip = z_lo ^ (block_y >> 1)
        slot = sum(jnp.where(flip == f, n, 0) for n, f in enumerate(FLIPS))
        block_rows[:, at * HALF : (at + 1) * HALF] = block_tiles[source, slot]
        places.append(2 * block_y + block_zh)
    for half in range(2):
        for n in range(4 * half, 4 * half + 4):
            act_copies[n].wait()
        span = pl.ds(half * 4 * TOK, 4 * TOK)
        part = jnp.dot(block_rows[:, span], chunk_rows[span, :], preferred_element_type=f32)
        if half == 0:
            out_ref[...] = part
        else:
            out_ref[...] += part
    for n in range(8):
        row_copies[n].wait()
        rows = row_tiles[n].astype(f32)
        for other in range(2):
            place = pl.multiple_of(places[2 * n + other] * ROWS, ROWS)
            rows_ref[pl.ds(place, ROWS), :] = rows[other * ROWS : (other + 1) * ROWS]


def gradient(place, chunks, blocks, others):
    operands = (*chunks, *blocks, *others)
    return pl.pallas_call(
        gradient_kernel,
        out_shape=(
            jax.ShapeDtypeStruct((COLS, FEAT), f32),
            jax.ShapeDtypeStruct((16 * ROWS, FEAT), f32),
        ),
        in_specs=[SMEM] + [HBM] * len(operands),
        out_specs=(VMEM, VMEM),
        scratch_shapes=[
            pltpu.VMEM((8 * TOK, FEAT), bf16),
            pltpu.VMEM((4, 4, COLS, HALF), bf16),
            pltpu.VMEM((COLS, 8 * TOK), bf16),
            pltpu.VMEM((8, PAD, FEAT), bf16),
            pltpu.SemaphoreType.DMA((20,)),
        ],
        compiler_params=pltpu.CompilerParams(vmem_limit_bytes=32 * 2**20),
        cost_estimate=pl.CostEstimate(
            flops=2 * 8 * TOK * COLS * FEAT, bytes_accessed=6 * 2**20, transcendentals=0
        ),
        name="gradient",
    )(place, *operands)


def step_kernel(
    place_ref, mine_ref, got_ref, rows_ref, one_ref, one_got, two_ref, two_got, weight_ref, update_ref, out_ref
):
    learner = place_ref[0] == 1
    grad = mine_ref[...] + got_ref[...]
    moment_one = jnp.where(learner, one_ref[...], one_got[...])
    moment_two = jnp.where(learner, two_ref[...], two_got[...])
    first_moment = beta_one * moment_one + (1.0 - beta_one) * grad
    second_moment = beta_two * moment_two + (1.0 - beta_two) * grad * grad
    update = (
        first_moment / first_bias / (jnp.sqrt(second_moment / second_bias) + epsilon)
    ).astype(bf16)
    update_ref[...] = update
    widened = weight_ref[...].astype(f32)
    renewed = (
        widened - learning_rate * (update.astype(f32) + weight_decay * widened)
    ).astype(bf16)
    rows = rows_ref[...].astype(bf16)
    part = lax.dot_general(rows, renewed, (((1,), (1,)), ((), ())), preferred_element_type=f32)
    out_ref[...] = part.reshape(16, ROWS, COLS)


def step(place, mine, got, rows, one, one_got, two, two_got, weight):
    return pl.pallas_call(
        step_kernel,
        out_shape=(
            jax.ShapeDtypeStruct((COLS, FEAT), bf16),
            jax.ShapeDtypeStruct((16, ROWS, COLS), f32),
        ),
        in_specs=[SMEM] + [VMEM] * 8,
        out_specs=(VMEM, VMEM),
        compiler_params=pltpu.CompilerParams(vmem_limit_bytes=32 * 2**20),
        name="step",
    )(place, mine, got, rows, one, one_got, two, two_got, weight)


def local(
    activations,
    cotangent,
    weight,
    moment_one,
    moment_two,
    queries,
    cache_keys,
    cache_values,
    new_keys,
    new_values,
    lengths,
    token_ids,
):
    q = lax.axis_index(TENSOR)
    place = jnp.stack([lax.axis_index(axis) for axis in AXES]).astype(jnp.int32)

    act = activations[0]
    act_got = permute(act, to_rollout)
    rows = attend(
        (q >> 1).reshape(1),
        queries,
        cache_keys,
        cache_values,
        new_keys,
        new_values,
        lengths,
        token_ids.T,
    )
    half = half_of(place, act, act_got, rows)
    half_got = permute(half, to_partner)

    cut_one, cut_two = cut_of(place, cotangent[0])
    own_one = permute(cut_one, cot_transposed(1))
    own_two = permute(cut_two, cot_transposed(0))

    one, two = moment_one[0].T, moment_two[0].T
    one_tied, two_tied, _, _ = lax.optimization_barrier((one, two, cut_one, half))
    one_got = permute(one_tied, to_rollout)
    two_got = permute(two_tied, to_rollout)
    base = base_of((half, half_got), (one_got, two_got, cut_one, cut_two))

    first, second = [base], [base]
    first.append(permute(base, along_y(1)))
    second.append(permute(base, along_y(-1)))
    own_one, own_two, first[1] = lax.optimization_barrier((own_one, own_two, first[1]))
    first.append(permute(first[1], along_y(1)))
    own = jnp.where(place[0] == 1, own_one, own_two)
    two_blocks = jnp.stack([own, permute(own, along_zl(3))])
    two_blocks, second[1] = lax.optimization_barrier((two_blocks, second[1]))
    second.append(permute(second[1], along_y(-1)))
    two_got_blocks = permute(two_blocks, along_zl(1))
    two_got_blocks, first[2] = lax.optimization_barrier((two_got_blocks, first[2]))
    first.append(permute(first[2], along_y(1)))
    four = jnp.concatenate([two_blocks, two_got_blocks], axis=0)
    four, second[2] = lax.optimization_barrier((four, second[2]))
    second.append(permute(second[2], along_y(-1)))
    blocks = [four] + [permute(four, along_x(step)) for step in (1, 2, -1)]
    blocks[1], first[3] = lax.optimization_barrier((blocks[1], first[3]))
    first.append(permute(first[3], along_y(1)))
    chunks = first + second[1:]

    mine, all_rows = gradient(place, chunks, blocks, ())
    got = permute(mine, other_core)
    update, partial = step(place, mine, got, all_rows, one, one_got, two, two_got, weight.T)

    shares = lax.all_to_all(partial, TENSOR, split_axis=0, concat_axis=0, tiled=True)
    summed = jnp.sum(shares, axis=0).astype(bf16)
    block = permute(summed, transposed)
    spread = jnp.broadcast_to(block[None], (16, ROWS, COLS))
    gathered = lax.all_to_all(spread, TENSOR, split_axis=0, concat_axis=0, tiled=True)
    decoded = gathered.transpose(1, 0, 2).reshape(STEPS, ROWS // STEPS, D)
    return (update.T, decoded)


def solution(mesh):
    fine = Mesh(mesh.devices.reshape(SHAPE), AXES)
    return jax.shard_map(
        local,
        mesh=fine,
        in_specs=(
            P("group", DP, TENSOR),
            P("group", DP, None),
            P(TENSOR, DP),
            P("group", TENSOR, DP),
            P("group", TENSOR, DP),
            P(None, DP, TENSOR),
            P(DP, None, None),
            P(DP, None, None),
            P(None, DP, None),
            P(None, DP, None),
            P(DP),
            P(None, DP),
        ),
        out_specs=(P(TENSOR, DP), P(None, DP, None)),
        check_vma=False,
    )
```

```python
import math

import jax
import jax.numpy as jnp
import numpy as np
from jax import lax
from jax.experimental import pallas as pl
from jax.experimental.pallas import tpu as pltpu
from jax.sharding import Mesh
from jax.sharding import PartitionSpec as P

D = 5120
KVH = 8
HD = 128
EOS = 151645
STEPS = 4
CACHE = 256

learning_rate = 0.0003
weight_decay = 0.1
beta_one = 0.9
beta_two = 0.95
first_bias = 1.0 - 0.9**10
second_bias = 1.0 - 0.95**10
epsilon = 1e-08

AXES = ("group", "y", "z_hi", "z_lo", "x")
SHAPE = (2, 8, 2, 4, 4)
DP, TENSOR = ("y", "z_hi"), ("z_lo", "x")
TOK = 256
HALF = 128
FEAT = 512
COLS = 320
ROWS = 8
PAD = 16
f32, bf16 = jnp.float32, jnp.bfloat16


def permute(value, target):
    pairs = []
    for flat, place in enumerate(np.ndindex(*SHAPE)):
        to = target(*place)
        if to is not None:
            pairs.append((flat, int(np.ravel_multi_index(to, SHAPE))))
    return lax.ppermute(value, AXES, pairs)


def gather(value, axes):
    return lax.all_to_all(value, axes, split_axis=0, concat_axis=0, tiled=True)


def to_partner(g, y, zh, zl, x):
    return (g, y, 1 - zh, zl, x)


def along_y(step):
    return lambda g, y, zh, zl, x: (g, (y + (step if g == 1 else -step)) % 8, zh, zl, x)


def transposed(g, y, zh, zl, x):
    return (g, zl * 2 + (x >> 1), x & 1, y >> 1, (y & 1) * 2 + zh)


def cot_transposed(core):
    return lambda g, *place: (core, *transposed(g, *place)[1:]) if g == 1 else None


def other_core(g, y, zh, zl, x):
    return (1 - g, y, zh, zl, x)


def to_rollout(g, y, zh, zl, x):
    return (0, y, zh, zl, x) if g == 1 else None


HOPS = (0, 1, 2, 3, 4, -1, -2, -3)


def attend_kernel(
    head_ref, lengths_ref, ids_ref, q_ref, k_ref, v_ref, nk_ref, nv_ref, out_ref, q_rows, nk_rows, nv_rows
):
    for t in range(STEPS):
        place = slice(2 * t, 2 * t + 2)
        q_rows[place, :] = q_ref[t].astype(f32)
        nk_rows[place, :] = nk_ref[t].astype(f32)
        nv_rows[place, :] = nv_ref[t].astype(f32)
    queries = q_rows[...]
    query = jnp.concatenate(
        [queries[:, h * HD : (h + 1) * HD] for h in range(4)], axis=0
    ).astype(bf16)
    keys = k_ref[...].reshape(2 * CACHE, HD)
    values = v_ref[...].reshape(2 * CACHE, HD)
    fresh_keys = nk_rows[...].astype(bf16)
    fresh_values = nv_rows[...].astype(bf16)
    scale = 1.0 / math.sqrt(HD)
    nt = (((1,), (1,)), ((), ()))
    cache_scores = lax.dot_general(query, keys, nt, preferred_element_type=f32) * scale
    step_scores = lax.dot_general(query, fresh_keys, nt, preferred_element_type=f32) * scale
    count = 4 * ROWS

    def place(width):
        place_row = lax.broadcasted_iota(jnp.int32, (count, width), 0) & (ROWS - 1)
        place_key = lax.broadcasted_iota(jnp.int32, (count, width), 1)
        return place_row >> 1, place_row & 1, place_key

    step, row, key = place(2 * CACHE)
    length = jnp.where(row == 0, lengths_ref[0], lengths_ref[1])
    cache_valid = ((key >> 8) == row) & ((key & (CACHE - 1)) < length)
    step, row, key = place(ROWS)
    step_valid = ((key & 1) == row) & ((key >> 1) <= step)
    cache_scores = jnp.where(cache_valid, cache_scores, -jnp.inf)
    step_scores = jnp.where(step_valid, step_scores, -jnp.inf)
    peak = jnp.maximum(
        jnp.max(cache_scores, axis=-1, keepdims=True), jnp.max(step_scores, axis=-1, keepdims=True)
    )
    cache_exp = jnp.exp(cache_scores - peak)
    step_exp = jnp.exp(step_scores - peak)
    denominator = jnp.sum(cache_exp, axis=-1, keepdims=True) + jnp.sum(
        step_exp, axis=-1, keepdims=True
    )
    cache_probs = (cache_exp / denominator).astype(bf16)
    step_probs = (step_exp / denominator).astype(bf16)
    nn = (((1,), (0,)), ((), ()))
    mixed = lax.dot_general(cache_probs, values, nn, preferred_element_type=f32)
    mixed = mixed + lax.dot_general(step_probs, fresh_values, nn, preferred_element_type=f32)
    step, row, _ = place(HD)
    dead = jnp.zeros((count, HD), jnp.int32)
    for u in range(STEPS - 1):
        for r in range(2):
            ended = (ids_ref[r, u] == EOS).astype(jnp.int32)
            dead = dead + jnp.where((row == r) & (step > u), ended, 0)
    mixed = jnp.where(dead == 0, mixed, 0.0)
    flat = jnp.concatenate([mixed[h * ROWS : (h + 1) * ROWS] for h in range(4)], axis=1)
    out_ref[...] = jnp.concatenate([flat, jnp.zeros_like(flat)], axis=0).astype(bf16)


def attend(head, queries, cache_keys, cache_values, new_keys, new_values, lengths, ids):
    whole = lambda *shape: pl.BlockSpec(shape, lambda i, *_: (0,) * len(shape))
    cache = pl.BlockSpec((2, CACHE, HD), lambda i, m, *_: (0, m[0], 0))
    fresh = pl.BlockSpec((STEPS, 2, HD), lambda i, m, *_: (0, 0, m[0]))
    return pl.pallas_call(
        attend_kernel,
        out_shape=jax.ShapeDtypeStruct((PAD, FEAT), bf16),
        grid_spec=pltpu.PrefetchScalarGridSpec(
            num_scalar_prefetch=3,
            grid=(1,),
            in_specs=[whole(STEPS, 2, FEAT), cache, cache, fresh, fresh],
            out_specs=whole(PAD, FEAT),
            scratch_shapes=[
                pltpu.VMEM((ROWS, FEAT), f32),
                pltpu.VMEM((ROWS, HD), f32),
                pltpu.VMEM((ROWS, HD), f32),
            ],
        ),
        name="attend",
    )(head, lengths, ids, queries, cache_keys, cache_values, new_keys, new_values)


VMEM = pl.BlockSpec(memory_space=pltpu.VMEM)
SMEM = pl.BlockSpec(memory_space=pltpu.SMEM)
HBM = pl.BlockSpec(memory_space=pl.ANY)


def half_kernel(place_ref, act_ref, act_got, rows_ref, out_ref):
    @pl.when(place_ref[0] == 1)
    def _():
        out_ref[:HALF, :] = act_ref[:HALF, :]

    @pl.when(place_ref[0] == 0)
    def _():
        out_ref[:HALF, :] = act_got[HALF:, :]

    out_ref[HALF:, :] = rows_ref[...]


def half_of(place, *parts):
    return pl.pallas_call(
        half_kernel,
        out_shape=jax.ShapeDtypeStruct((HALF + PAD, FEAT), bf16),
        in_specs=[SMEM] + [VMEM] * 3,
        out_specs=VMEM,
        name="half",
    )(place, *parts)


def base_kernel(mine_ref, got_ref, *refs):
    out_ref = refs[-1]
    out_ref[:HALF, :] = mine_ref[:HALF, :]
    out_ref[HALF:TOK, :] = got_ref[:HALF, :]
    rows = [ref[HALF:, :].astype(f32)[:ROWS] for ref in (mine_ref, got_ref)]
    out_ref[TOK:, :] = jnp.concatenate(rows, axis=0).astype(bf16)


def base_of(parts, others):
    return pl.pallas_call(
        base_kernel,
        out_shape=jax.ShapeDtypeStruct((TOK + PAD, FEAT), bf16),
        in_specs=[VMEM] * 2 + [HBM] * len(others),
        out_specs=VMEM,
        name="base",
    )(*parts, *others)


def cut_kernel(place_ref, cot_ref, one_ref, two_ref, window, turned, sem):
    q = place_ref[3] * 4 + place_ref[4]
    start = pl.multiple_of(((q * 5) >> 1) * 128, 128)
    copy = pltpu.make_async_copy(cot_ref.at[:, pl.ds(start, 384)], window, sem)
    copy.start()
    copy.wait()
    turned[...] = window[...].astype(f32).T
    place = pl.ds(pl.multiple_of((q & 1) * 64, 64), COLS)
    one_ref[...] = turned[place, :HALF].astype(bf16)
    two_ref[...] = turned[place, HALF:].astype(bf16)


def cut_of(place, cot):
    shape = jax.ShapeDtypeStruct((COLS, HALF), bf16)
    return pl.pallas_call(
        cut_kernel,
        out_shape=(shape, shape),
        in_specs=[SMEM, HBM],
        out_specs=(VMEM, VMEM),
        scratch_shapes=[
            pltpu.VMEM((TOK, 384), bf16),
            pltpu.VMEM((384, TOK), f32),
            pltpu.SemaphoreType.DMA(()),
        ],
        name="cut",
    )(place, cot)


def gradient_kernel(place_ref, *refs):
    chunks, blocks, (out_ref, rows_ref) = refs[:8], refs[8], refs[-7:-5]
    chunk_rows, block_tiles, block_rows, row_tiles, sems = refs[-5:]
    block_copy = pltpu.make_async_copy(blocks, block_tiles, sems.at[0])
    act_copies = [
        pltpu.make_async_copy(
            chunks[n].at[:TOK], chunk_rows.at[pl.ds(n * TOK, TOK)], sems.at[4 + n]
        )
        for n in range(8)
    ]
    row_copies = [
        pltpu.make_async_copy(chunks[n].at[TOK:], row_tiles.at[n], sems.at[12 + n])
        for n in range(8)
    ]
    for copy in [block_copy] + act_copies + row_copies:
        copy.start()
    block_copy.wait()
    side, y, z_hi = (place_ref[n] for n in range(3))
    places = []
    for at in range(16):
        hop, block_zh = HOPS[at // 2], (z_hi if at % 2 == 0 else 1 - z_hi)
        block = 2 * (jnp.where(side == 1, y - hop, y + hop) & 7) + block_zh
        block_rows[:, at * HALF : (at + 1) * HALF] = block_tiles[block]
        places.append(block)
    for half in range(2):
        for n in range(4 * half, 4 * half + 4):
            act_copies[n].wait()
        span = pl.ds(half * 4 * TOK, 4 * TOK)
        part = jnp.dot(block_rows[:, span], chunk_rows[span, :], preferred_element_type=f32)
        if half == 0:
            out_ref[...] = part
        else:
            out_ref[...] += part
    for n in range(8):
        row_copies[n].wait()
        rows = row_tiles[n].astype(f32)
        for other in range(2):
            place = pl.multiple_of(places[2 * n + other] * ROWS, ROWS)
            rows_ref[pl.ds(place, ROWS), :] = rows[other * ROWS : (other + 1) * ROWS]


def gradient(place, chunks, blocks, others):
    operands = (*chunks, blocks, *others)
    return pl.pallas_call(
        gradient_kernel,
        out_shape=(
            jax.ShapeDtypeStruct((COLS, FEAT), f32),
            jax.ShapeDtypeStruct((16 * ROWS, FEAT), f32),
        ),
        in_specs=[SMEM] + [HBM] * len(operands),
        out_specs=(VMEM, VMEM),
        scratch_shapes=[
            pltpu.VMEM((8 * TOK, FEAT), bf16),
            pltpu.VMEM((16, COLS, HALF), bf16),
            pltpu.VMEM((COLS, 8 * TOK), bf16),
            pltpu.VMEM((8, PAD, FEAT), bf16),
            pltpu.SemaphoreType.DMA((20,)),
        ],
        compiler_params=pltpu.CompilerParams(vmem_limit_bytes=32 * 2**20),
        cost_estimate=pl.CostEstimate(
            flops=2 * 8 * TOK * COLS * FEAT, bytes_accessed=6 * 2**20, transcendentals=0
        ),
        name="gradient",
    )(place, *operands)


def step_kernel(
    place_ref, mine_ref, got_ref, rows_ref, one_ref, one_got, two_ref, two_got, weight_ref, update_ref, out_ref
):
    learner = place_ref[0] == 1
    grad = mine_ref[...] + got_ref[...]
    moment_one = jnp.where(learner, one_ref[...], one_got[...])
    moment_two = jnp.where(learner, two_ref[...], two_got[...])
    first_moment = beta_one * moment_one + (1.0 - beta_one) * grad
    second_moment = beta_two * moment_two + (1.0 - beta_two) * grad * grad
    update = (
        first_moment / first_bias / (jnp.sqrt(second_moment / second_bias) + epsilon)
    ).astype(bf16)
    update_ref[...] = update
    widened = weight_ref[...].astype(f32)
    renewed = (
        widened - learning_rate * (update.astype(f32) + weight_decay * widened)
    ).astype(bf16)
    rows = rows_ref[...].astype(bf16)
    part = lax.dot_general(rows, renewed, (((1,), (1,)), ((), ())), preferred_element_type=f32)
    out_ref[...] = part.reshape(16, ROWS, COLS)


def step(place, mine, got, rows, one, one_got, two, two_got, weight):
    return pl.pallas_call(
        step_kernel,
        out_shape=(
            jax.ShapeDtypeStruct((COLS, FEAT), bf16),
            jax.ShapeDtypeStruct((16, ROWS, COLS), f32),
        ),
        in_specs=[SMEM] + [VMEM] * 8,
        out_specs=(VMEM, VMEM),
        compiler_params=pltpu.CompilerParams(vmem_limit_bytes=32 * 2**20),
        name="step",
    )(place, mine, got, rows, one, one_got, two, two_got, weight)


def local(
    activations,
    cotangent,
    weight,
    moment_one,
    moment_two,
    queries,
    cache_keys,
    cache_values,
    new_keys,
    new_values,
    lengths,
    token_ids,
):
    q = lax.axis_index(TENSOR)
    place = jnp.stack([lax.axis_index(axis) for axis in AXES]).astype(jnp.int32)

    act = activations[0]
    act_got = permute(act, to_rollout)
    cut_one, cut_two = cut_of(place, cotangent[0])
    own_one = permute(cut_one, cot_transposed(1))
    own_two = permute(cut_two, cot_transposed(0))
    rows = attend(
        (q >> 1).reshape(1),
        queries,
        cache_keys,
        cache_values,
        new_keys,
        new_values,
        lengths,
        token_ids.T,
    )
    half = half_of(place, act, act_got, rows)
    half_tied, _ = lax.optimization_barrier((half, cut_one))
    half_got = permute(half_tied, to_partner)
    own_one, own_two, half_got = lax.optimization_barrier((own_one, own_two, half_got))
    own = jnp.where(place[0] == 1, own_one, own_two)
    own_spread = jnp.broadcast_to(own[None], (16, COLS, HALF))
    blocks = gather(own_spread, TENSOR)
    base = base_of((half, half_got), (own_spread,))
    first, second = [base], [base]
    for n in range(3):
        first.append(permute(first[n], along_y(1)))
        second.append(permute(second[n], along_y(-1)))
        first[n + 1], second[n + 1] = lax.optimization_barrier((first[n + 1], second[n + 1]))
    one, two = moment_one[0].T, moment_two[0].T
    one_tied, two_tied, first[3] = lax.optimization_barrier((one, two, first[3]))
    first.append(permute(first[3], along_y(1)))
    one_got = permute(one_tied, to_rollout)
    two_got = permute(two_tied, to_rollout)
    chunks = first + second[1:]

    mine, all_rows = gradient(place, chunks, blocks, (one_got, two_got))
    got = permute(mine, other_core)
    update, partial = step(place, mine, got, all_rows, one, one_got, two, two_got, weight.T)

    shares = gather(partial, TENSOR)
    summed = jnp.sum(shares, axis=0).astype(bf16)
    block = permute(summed, transposed)
    spread = jnp.broadcast_to(block[None], (16, ROWS, COLS))
    gathered = gather(spread, TENSOR)
    decoded = gathered.transpose(1, 0, 2).reshape(STEPS, ROWS // STEPS, D)
    return (update.T, decoded)


def solution(mesh):
    fine = Mesh(mesh.devices.reshape(SHAPE), AXES)
    return jax.shard_map(
        local,
        mesh=fine,
        in_specs=(
            P("group", DP, TENSOR),
            P("group", DP, None),
            P(TENSOR, DP),
            P("group", TENSOR, DP),
            P("group", TENSOR, DP),
            P(None, DP, TENSOR),
            P(DP, None, None),
            P(DP, None, None),
            P(None, DP, None),
            P(None, DP, None),
            P(DP),
            P(None, DP),
        ),
        out_specs=(P(TENSOR, DP), P(None, DP, None)),
        check_vma=False,
    )
```

```python
import math

import jax
import jax.numpy as jnp
import numpy as np
from jax import lax
from jax.experimental import pallas as pl
from jax.experimental.pallas import tpu as pltpu
from jax.sharding import Mesh
from jax.sharding import PartitionSpec as P

D = 5120
KVH = 8
HD = 128
EOS = 151645
STEPS = 4
CACHE = 256

learning_rate = 0.0003
weight_decay = 0.1
beta_one = 0.9
beta_two = 0.95
first_bias = 1.0 - 0.9**10
second_bias = 1.0 - 0.95**10
epsilon = 1e-08

AXES = ("group", "y", "z_hi", "z_lo", "x")
SHAPE = (2, 8, 2, 4, 4)
DP, TENSOR = ("y", "z_hi"), ("z_lo", "x")
TOK = 256
HALF = 128
FEAT = 512
COLS = 320
ROWS = 8
PAD = 16
f32, bf16 = jnp.float32, jnp.bfloat16


def permute(value, target):
    pairs = []
    for flat, place in enumerate(np.ndindex(*SHAPE)):
        to = target(*place)
        if to is not None:
            pairs.append((flat, int(np.ravel_multi_index(to, SHAPE))))
    return lax.ppermute(value, AXES, pairs)


def gather(value, axes):
    return lax.all_to_all(value, axes, split_axis=0, concat_axis=0, tiled=True)


def to_partner(g, y, zh, zl, x):
    return (g, y, 1 - zh, zl, x)


def along_y(step):
    return lambda g, y, zh, zl, x: (g, (y + (step if g == 1 else -step)) % 8, zh, zl, x)


def transposed(g, y, zh, zl, x):
    return (g, zl * 2 + (x >> 1), x & 1, y >> 1, (y & 1) * 2 + zh)


def cot_transposed(core):
    return lambda g, *place: (core, *transposed(g, *place)[1:]) if g == 1 else None


def along_x(step):
    return lambda g, y, zh, zl, x: (g, y, zh, zl, (x + (step if g == 1 else -step)) % 4)


def to_learner(g, y, zh, zl, x):
    return (1, y, zh, zl, x) if g == 0 else None


def to_rollout(g, y, zh, zl, x):
    return (0, y, zh, zl, x) if g == 1 else None


HOPS = (0, 1, 2, 3, 4, -1, -2, -3)


SMALL = pltpu.CompilerParams(vmem_limit_bytes=6 * 2**20)


def attend_kernel(
    head_ref, lengths_ref, ids_ref, q_ref, k_ref, v_ref, nk_ref, nv_ref, out_ref, q_rows, nk_rows, nv_rows
):
    for t in range(STEPS):
        place = slice(2 * t, 2 * t + 2)
        q_rows[place, :] = q_ref[t].astype(f32)
        nk_rows[place, :] = nk_ref[t].astype(f32)
        nv_rows[place, :] = nv_ref[t].astype(f32)
    queries = q_rows[...]
    query = jnp.concatenate(
        [queries[:, h * HD : (h + 1) * HD] for h in range(4)], axis=0
    ).astype(bf16)
    keys = k_ref[...].reshape(2 * CACHE, HD)
    values = v_ref[...].reshape(2 * CACHE, HD)
    fresh_keys = nk_rows[...].astype(bf16)
    fresh_values = nv_rows[...].astype(bf16)
    scale = 1.0 / math.sqrt(HD)
    nt = (((1,), (1,)), ((), ()))
    cache_scores = lax.dot_general(query, keys, nt, preferred_element_type=f32) * scale
    step_scores = lax.dot_general(query, fresh_keys, nt, preferred_element_type=f32) * scale
    count = 4 * ROWS

    def place(width):
        place_row = lax.broadcasted_iota(jnp.int32, (count, width), 0) & (ROWS - 1)
        place_key = lax.broadcasted_iota(jnp.int32, (count, width), 1)
        return place_row >> 1, place_row & 1, place_key

    step, row, key = place(2 * CACHE)
    length = jnp.where(row == 0, lengths_ref[0], lengths_ref[1])
    cache_valid = ((key >> 8) == row) & ((key & (CACHE - 1)) < length)
    step, row, key = place(ROWS)
    step_valid = ((key & 1) == row) & ((key >> 1) <= step)
    cache_scores = jnp.where(cache_valid, cache_scores, -jnp.inf)
    step_scores = jnp.where(step_valid, step_scores, -jnp.inf)
    peak = jnp.maximum(
        jnp.max(cache_scores, axis=-1, keepdims=True), jnp.max(step_scores, axis=-1, keepdims=True)
    )
    cache_exp = jnp.exp(cache_scores - peak)
    step_exp = jnp.exp(step_scores - peak)
    denominator = jnp.sum(cache_exp, axis=-1, keepdims=True) + jnp.sum(
        step_exp, axis=-1, keepdims=True
    )
    cache_probs = (cache_exp / denominator).astype(bf16)
    step_probs = (step_exp / denominator).astype(bf16)
    nn = (((1,), (0,)), ((), ()))
    mixed = lax.dot_general(cache_probs, values, nn, preferred_element_type=f32)
    mixed = mixed + lax.dot_general(step_probs, fresh_values, nn, preferred_element_type=f32)
    step, row, _ = place(HD)
    dead = jnp.zeros((count, HD), jnp.int32)
    for u in range(STEPS - 1):
        for r in range(2):
            ended = (ids_ref[r, u] == EOS).astype(jnp.int32)
            dead = dead + jnp.where((row == r) & (step > u), ended, 0)
    mixed = jnp.where(dead == 0, mixed, 0.0)
    flat = jnp.concatenate([mixed[h * ROWS : (h + 1) * ROWS] for h in range(4)], axis=1)
    out_ref[...] = jnp.concatenate([flat, jnp.zeros_like(flat)], axis=0).astype(bf16)


def attend(head, queries, cache_keys, cache_values, new_keys, new_values, lengths, ids):
    whole = lambda *shape: pl.BlockSpec(shape, lambda i, *_: (0,) * len(shape))
    cache = pl.BlockSpec((2, CACHE, HD), lambda i, m, *_: (0, m[0], 0))
    fresh = pl.BlockSpec((STEPS, 2, HD), lambda i, m, *_: (0, 0, m[0]))
    return pl.pallas_call(
        attend_kernel,
        out_shape=jax.ShapeDtypeStruct((PAD, FEAT), bf16),
        grid_spec=pltpu.PrefetchScalarGridSpec(
            num_scalar_prefetch=3,
            grid=(1,),
            in_specs=[whole(STEPS, 2, FEAT), cache, cache, fresh, fresh],
            out_specs=whole(PAD, FEAT),
            scratch_shapes=[
                pltpu.VMEM((ROWS, FEAT), f32),
                pltpu.VMEM((ROWS, HD), f32),
                pltpu.VMEM((ROWS, HD), f32),
            ],
        ),
        compiler_params=SMALL,
        name="attend",
    )(head, lengths, ids, queries, cache_keys, cache_values, new_keys, new_values)


VMEM = pl.BlockSpec(memory_space=pltpu.VMEM)
SMEM = pl.BlockSpec(memory_space=pltpu.SMEM)
HBM = pl.BlockSpec(memory_space=pl.ANY)


def half_kernel(place_ref, act_ref, act_got, rows_ref, out_ref):
    @pl.when(place_ref[0] == 1)
    def _():
        out_ref[:HALF, :] = act_ref[:HALF, :]

    @pl.when(place_ref[0] == 0)
    def _():
        out_ref[:HALF, :] = act_got[HALF:, :]

    out_ref[HALF:, :] = rows_ref[...]


def half_of(place, *parts):
    return pl.pallas_call(
        half_kernel,
        out_shape=jax.ShapeDtypeStruct((HALF + PAD, FEAT), bf16),
        in_specs=[SMEM] + [VMEM] * 3,
        out_specs=VMEM,
        compiler_params=SMALL,
        name="half",
    )(place, *parts)


def base_kernel(mine_ref, got_ref, *refs):
    out_ref = refs[-1]
    out_ref[:HALF, :] = mine_ref[:HALF, :]
    out_ref[HALF:TOK, :] = got_ref[:HALF, :]
    rows = [ref[HALF:, :].astype(f32)[:ROWS] for ref in (mine_ref, got_ref)]
    out_ref[TOK:, :] = jnp.concatenate(rows, axis=0).astype(bf16)


def base_of(parts, others):
    return pl.pallas_call(
        base_kernel,
        out_shape=jax.ShapeDtypeStruct((TOK + PAD, FEAT), bf16),
        in_specs=[VMEM] * 2 + [HBM] * len(others),
        out_specs=VMEM,
        compiler_params=SMALL,
        name="base",
    )(*parts, *others)


def cut_kernel(place_ref, cot_ref, one_ref, two_ref, window, turned, sem):
    q = place_ref[3] * 4 + place_ref[4]
    start = pl.multiple_of(((q * 5) >> 1) * 128, 128)
    copy = pltpu.make_async_copy(cot_ref.at[:, pl.ds(start, 384)], window, sem)
    copy.start()
    copy.wait()
    turned[...] = window[...].astype(f32).T
    place = pl.ds(pl.multiple_of((q & 1) * 64, 64), COLS)
    one_ref[...] = turned[place, :HALF].astype(bf16)
    two_ref[...] = turned[place, HALF:].astype(bf16)


def cut_of(place, cot):
    shape = jax.ShapeDtypeStruct((COLS, HALF), bf16)
    return pl.pallas_call(
        cut_kernel,
        out_shape=(shape, shape),
        in_specs=[SMEM, HBM],
        out_specs=(VMEM, VMEM),
        scratch_shapes=[
            pltpu.VMEM((TOK, 384), bf16),
            pltpu.VMEM((384, TOK), f32),
            pltpu.SemaphoreType.DMA(()),
        ],
        compiler_params=SMALL,
        name="cut",
    )(place, cot)


def gradient_kernel(place_ref, *refs):
    chunks, blocks, (out_ref, rows_ref, block_rows) = refs[:8], refs[8:12], refs[12:]
    side, y, z_hi, x = (place_ref[n] for n in (0, 1, 2, 4))
    for n, hop in enumerate(HOPS):
        block_y = jnp.where(side == 1, y - hop, y + hop) & 7
        rows = chunks[n][TOK:, :].astype(f32)
        for other in range(2):
            block_zh = z_hi if other == 0 else 1 - z_hi
            span = slice(other * HALF, (other + 1) * HALF)
            source = 2 * (block_y & 1) + block_zh - x
            source = jnp.where(side == 1, -source, source) & 3
            block = blocks[0][block_y >> 1]
            for m in range(1, 4):
                block = jnp.where(source == m, blocks[m][block_y >> 1], block)
            block_rows[:, span] = block
            place = pl.multiple_of((2 * block_y + block_zh) * ROWS, ROWS)
            rows_ref[pl.ds(place, ROWS), :] = rows[other * ROWS : (other + 1) * ROWS]
        part = jnp.dot(block_rows[...], chunks[n][:TOK, :], preferred_element_type=f32)
        if n == 0:
            out_ref[...] = part
        else:
            out_ref[...] += part


def gradient(place, chunks, blocks):
    return pl.pallas_call(
        gradient_kernel,
        out_shape=(
            jax.ShapeDtypeStruct((COLS, FEAT), f32),
            jax.ShapeDtypeStruct((16 * ROWS, FEAT), f32),
        ),
        in_specs=[SMEM] + [VMEM] * 12,
        out_specs=(VMEM, VMEM),
        scratch_shapes=[pltpu.VMEM((COLS, TOK), bf16)],
        compiler_params=pltpu.CompilerParams(vmem_limit_bytes=12 * 2**20),
        cost_estimate=pl.CostEstimate(
            flops=2 * 8 * TOK * COLS * FEAT, bytes_accessed=6 * 2**20, transcendentals=0
        ),
        name="gradient",
    )(place, *chunks, *blocks)


def adam_kernel(mine_ref, got_ref, one_ref, two_ref, out_ref):
    grad = mine_ref[...] + got_ref[...]
    first_moment = beta_one * one_ref[...] + (1.0 - beta_one) * grad
    second_moment = beta_two * two_ref[...] + (1.0 - beta_two) * grad * grad
    out_ref[...] = (
        first_moment / first_bias / (jnp.sqrt(second_moment / second_bias) + epsilon)
    ).astype(bf16)


def adam(*operands):
    return pl.pallas_call(
        adam_kernel,
        out_shape=jax.ShapeDtypeStruct((COLS, FEAT), bf16),
        in_specs=[VMEM] * 4,
        out_specs=VMEM,
        compiler_params=pltpu.CompilerParams(vmem_limit_bytes=12 * 2**20),
        name="adam",
    )(*operands)


def step_kernel(place_ref, update_ref, update_got, rows_ref, weight_ref, taken_ref, out_ref):
    update = jnp.where(place_ref[0] == 1, update_ref[...], update_got[...])
    taken_ref[...] = update
    widened = weight_ref[...].astype(f32)
    renewed = (
        widened - learning_rate * (update.astype(f32) + weight_decay * widened)
    ).astype(bf16)
    rows = rows_ref[...].astype(bf16)
    part = lax.dot_general(rows, renewed, (((1,), (1,)), ((), ())), preferred_element_type=f32)
    out_ref[...] = part.reshape(16, ROWS, COLS)


def step(place, *operands):
    return pl.pallas_call(
        step_kernel,
        out_shape=(
            jax.ShapeDtypeStruct((COLS, FEAT), bf16),
            jax.ShapeDtypeStruct((16, ROWS, COLS), f32),
        ),
        in_specs=[SMEM] + [VMEM] * 4,
        out_specs=(VMEM, VMEM),
        compiler_params=pltpu.CompilerParams(vmem_limit_bytes=12 * 2**20),
        name="step",
    )(place, *operands)


def local(
    activations,
    cotangent,
    weight,
    moment_one,
    moment_two,
    queries,
    cache_keys,
    cache_values,
    new_keys,
    new_values,
    lengths,
    token_ids,
):
    q = lax.axis_index(TENSOR)
    place = jnp.stack([lax.axis_index(axis) for axis in AXES]).astype(jnp.int32)

    act = activations[0]
    act_got = permute(act, to_rollout)
    cut_one, cut_two = cut_of(place, cotangent[0])
    own_one = permute(cut_one, cot_transposed(1))
    own_two = permute(cut_two, cot_transposed(0))
    rows = attend(
        (q >> 1).reshape(1),
        queries,
        cache_keys,
        cache_values,
        new_keys,
        new_values,
        lengths,
        token_ids.T,
    )
    half = half_of(place, act, act_got, rows)
    own = jnp.where(place[0] == 1, own_one, own_two)
    half_tied, own = lax.optimization_barrier((half, own))
    half_got = permute(half_tied, to_partner)
    line = gather(jnp.broadcast_to(own[None], (4, COLS, HALF)), "z_lo")
    base = base_of((half, half_got), (line,))
    first = [permute(base, along_y(1))]
    second = [permute(base, along_y(-1))]
    line_tied, ahead, back = lax.optimization_barrier((line, first[0], second[0]))
    first.append(permute(ahead, along_y(1)))
    second.append(permute(back, along_y(-1)))
    blocks = [line] + [permute(line_tied, along_x(step)) for step in (1, 2, -1)]
    ahead, back, *_ = lax.optimization_barrier((first[1], second[1], blocks[1]))
    first.append(permute(ahead, along_y(1)))
    second.append(permute(back, along_y(-1)))
    ahead, _ = lax.optimization_barrier((first[2], blocks[2]))
    first.append(permute(ahead, along_y(1)))
    chunks = [base] + first + second

    mine, all_rows = gradient(place, chunks, blocks)
    got = permute(mine, to_learner)
    update = adam(mine, got, moment_one[0].T, moment_two[0].T)
    update_got = permute(update, to_rollout)
    update, partial = step(place, update, update_got, all_rows, weight.T)

    shares = gather(partial, TENSOR)
    summed = jnp.sum(shares, axis=0).astype(bf16)
    block = permute(summed, transposed)
    spread = jnp.broadcast_to(block[None], (16, ROWS, COLS))
    gathered = gather(spread, TENSOR)
    decoded = gathered.transpose(1, 0, 2).reshape(STEPS, ROWS // STEPS, D)
    return (update.T, decoded)


def solution(mesh):
    fine = Mesh(mesh.devices.reshape(SHAPE), AXES)
    return jax.shard_map(
        local,
        mesh=fine,
        in_specs=(
            P("group", DP, TENSOR),
            P("group", DP, None),
            P(TENSOR, DP),
            P("group", TENSOR, DP),
            P("group", TENSOR, DP),
            P(None, DP, TENSOR),
            P(DP, None, None),
            P(DP, None, None),
            P(None, DP, None),
            P(None, DP, None),
            P(DP),
            P(None, DP),
        ),
        out_specs=(P(TENSOR, DP), P(None, DP, None)),
        check_vma=False,
    )
```

```python
import math

import jax
import jax.numpy as jnp
import numpy as np
from jax import lax
from jax.experimental import pallas as pl
from jax.experimental.pallas import tpu as pltpu
from jax.sharding import Mesh
from jax.sharding import PartitionSpec as P

D = 5120
KVH = 8
HD = 128
EOS = 151645
STEPS = 4
CACHE = 256

learning_rate = 0.0003
weight_decay = 0.1
beta_one = 0.9
beta_two = 0.95
first_bias = 1.0 - 0.9**10
second_bias = 1.0 - 0.95**10
epsilon = 1e-08

AXES = ("group", "y", "z_hi", "z_lo", "x")
SHAPE = (2, 8, 2, 4, 4)
DP, TENSOR = ("y", "z_hi"), ("z_lo", "x")
TOK = 256
HALF = 128
FEAT = 512
COLS = 320
ROWS = 8
PAD = 16
f32, bf16 = jnp.float32, jnp.bfloat16


def permute(value, target):
    pairs = []
    for flat, place in enumerate(np.ndindex(*SHAPE)):
        to = target(*place)
        if to is not None:
            pairs.append((flat, int(np.ravel_multi_index(to, SHAPE))))
    return lax.ppermute(value, AXES, pairs)


def gather(value, axes):
    return lax.all_to_all(value, axes, split_axis=0, concat_axis=0, tiled=True)


def to_partner(g, y, zh, zl, x):
    return (g, y, 1 - zh, zl, x)


def along_y(step):
    return lambda g, y, zh, zl, x: (g, (y + (step if g == 1 else -step)) % 8, zh, zl, x)


def transposed(g, y, zh, zl, x):
    return (g, zl * 2 + (x >> 1), x & 1, y >> 1, (y & 1) * 2 + zh)


def shift_of(z_lo, x):
    return 4 * (z_lo >> 1) + x - 3


def cot_shifted(core):
    def target(g, y, zh, zl, x):
        return (core, (y - shift_of(zl, x)) % 8, zh ^ (zl & 1), zl, x) if g == 1 else None

    return target


def along_x(step):
    return lambda g, y, zh, zl, x: (g, y, zh, zl, (x + (step if g == 1 else -step)) % 4)


def to_learner(g, y, zh, zl, x):
    return (1, y, zh, zl, x) if g == 0 else None


def to_rollout(g, y, zh, zl, x):
    return (0, y, zh, zl, x) if g == 1 else None


HOPS = (0, 1, 2, 3, 4, -1, -2, -3)


SMALL = pltpu.CompilerParams(vmem_limit_bytes=6 * 2**20)


def attend_kernel(
    head_ref, lengths_ref, ids_ref, q_ref, k_ref, v_ref, nk_ref, nv_ref, out_ref, q_rows, nk_rows, nv_rows
):
    for t in range(STEPS):
        place = slice(2 * t, 2 * t + 2)
        q_rows[place, :] = q_ref[t].astype(f32)
        nk_rows[place, :] = nk_ref[t].astype(f32)
        nv_rows[place, :] = nv_ref[t].astype(f32)
    queries = q_rows[...]
    query = jnp.concatenate(
        [queries[:, h * HD : (h + 1) * HD] for h in range(4)], axis=0
    ).astype(bf16)
    keys = k_ref[...].reshape(2 * CACHE, HD)
    values = v_ref[...].reshape(2 * CACHE, HD)
    fresh_keys = nk_rows[...].astype(bf16)
    fresh_values = nv_rows[...].astype(bf16)
    scale = 1.0 / math.sqrt(HD)
    nt = (((1,), (1,)), ((), ()))
    cache_scores = lax.dot_general(query, keys, nt, preferred_element_type=f32) * scale
    step_scores = lax.dot_general(query, fresh_keys, nt, preferred_element_type=f32) * scale
    count = 4 * ROWS

    def place(width):
        place_row = lax.broadcasted_iota(jnp.int32, (count, width), 0) & (ROWS - 1)
        place_key = lax.broadcasted_iota(jnp.int32, (count, width), 1)
        return place_row >> 1, place_row & 1, place_key

    step, row, key = place(2 * CACHE)
    length = jnp.where(row == 0, lengths_ref[0], lengths_ref[1])
    cache_valid = ((key >> 8) == row) & ((key & (CACHE - 1)) < length)
    step, row, key = place(ROWS)
    step_valid = ((key & 1) == row) & ((key >> 1) <= step)
    cache_scores = jnp.where(cache_valid, cache_scores, -jnp.inf)
    step_scores = jnp.where(step_valid, step_scores, -jnp.inf)
    peak = jnp.maximum(
        jnp.max(cache_scores, axis=-1, keepdims=True), jnp.max(step_scores, axis=-1, keepdims=True)
    )
    cache_exp = jnp.exp(cache_scores - peak)
    step_exp = jnp.exp(step_scores - peak)
    denominator = jnp.sum(cache_exp, axis=-1, keepdims=True) + jnp.sum(
        step_exp, axis=-1, keepdims=True
    )
    cache_probs = (cache_exp / denominator).astype(bf16)
    step_probs = (step_exp / denominator).astype(bf16)
    nn = (((1,), (0,)), ((), ()))
    mixed = lax.dot_general(cache_probs, values, nn, preferred_element_type=f32)
    mixed = mixed + lax.dot_general(step_probs, fresh_values, nn, preferred_element_type=f32)
    step, row, _ = place(HD)
    dead = jnp.zeros((count, HD), jnp.int32)
    for u in range(STEPS - 1):
        for r in range(2):
            ended = (ids_ref[r, u] == EOS).astype(jnp.int32)
            dead = dead + jnp.where((row == r) & (step > u), ended, 0)
    mixed = jnp.where(dead == 0, mixed, 0.0)
    flat = jnp.concatenate([mixed[h * ROWS : (h + 1) * ROWS] for h in range(4)], axis=1)
    out_ref[...] = jnp.concatenate([flat, jnp.zeros_like(flat)], axis=0).astype(bf16)


def attend(head, queries, cache_keys, cache_values, new_keys, new_values, lengths, ids):
    whole = lambda *shape: pl.BlockSpec(shape, lambda i, *_: (0,) * len(shape))
    cache = pl.BlockSpec((2, CACHE, HD), lambda i, m, *_: (0, m[0], 0))
    fresh = pl.BlockSpec((STEPS, 2, HD), lambda i, m, *_: (0, 0, m[0]))
    return pl.pallas_call(
        attend_kernel,
        out_shape=jax.ShapeDtypeStruct((PAD, FEAT), bf16),
        grid_spec=pltpu.PrefetchScalarGridSpec(
            num_scalar_prefetch=3,
            grid=(1,),
            in_specs=[whole(STEPS, 2, FEAT), cache, cache, fresh, fresh],
            out_specs=whole(PAD, FEAT),
            scratch_shapes=[
                pltpu.VMEM((ROWS, FEAT), f32),
                pltpu.VMEM((ROWS, HD), f32),
                pltpu.VMEM((ROWS, HD), f32),
            ],
        ),
        compiler_params=SMALL,
        name="attend",
    )(head, lengths, ids, queries, cache_keys, cache_values, new_keys, new_values)


VMEM = pl.BlockSpec(memory_space=pltpu.VMEM)
SMEM = pl.BlockSpec(memory_space=pltpu.SMEM)
HBM = pl.BlockSpec(memory_space=pl.ANY)


def half_kernel(place_ref, act_ref, act_got, rows_ref, out_ref):
    @pl.when(place_ref[0] == 1)
    def _():
        out_ref[:HALF, :] = act_ref[:HALF, :]

    @pl.when(place_ref[0] == 0)
    def _():
        out_ref[:HALF, :] = act_got[HALF:, :]

    out_ref[HALF:, :] = rows_ref[...]


def half_of(place, *parts):
    return pl.pallas_call(
        half_kernel,
        out_shape=jax.ShapeDtypeStruct((HALF + PAD, FEAT), bf16),
        in_specs=[SMEM] + [VMEM] * 3,
        out_specs=VMEM,
        compiler_params=SMALL,
        name="half",
    )(place, *parts)


def base_kernel(mine_ref, got_ref, *refs):
    out_ref = refs[-1]
    out_ref[:HALF, :] = mine_ref[:HALF, :]
    out_ref[HALF:TOK, :] = got_ref[:HALF, :]
    rows = [ref[HALF:, :].astype(f32)[:ROWS] for ref in (mine_ref, got_ref)]
    out_ref[TOK:, :] = jnp.concatenate(rows, axis=0).astype(bf16)


def base_of(parts, others):
    return pl.pallas_call(
        base_kernel,
        out_shape=jax.ShapeDtypeStruct((TOK + PAD, FEAT), bf16),
        in_specs=[VMEM] * 2 + [HBM] * len(others),
        out_specs=VMEM,
        compiler_params=SMALL,
        name="base",
    )(*parts, *others)


def cut_kernel(place_ref, cot_ref, one_ref, two_ref, window, turned, sem):
    z_lo = place_ref[3]
    q = 2 * ((place_ref[1] - shift_of(z_lo, place_ref[4])) & 7) + (place_ref[2] ^ (z_lo & 1))
    start = pl.multiple_of(((q * 5) >> 1) * 128, 128)
    copy = pltpu.make_async_copy(cot_ref.at[:, pl.ds(start, 384)], window, sem)
    copy.start()
    copy.wait()
    turned[...] = window[...].astype(f32).T
    place = pl.ds(pl.multiple_of((q & 1) * 64, 64), COLS)
    one_ref[...] = turned[place, :HALF].astype(bf16)
    two_ref[...] = turned[place, HALF:].astype(bf16)


def cut_of(place, cot):
    shape = jax.ShapeDtypeStruct((COLS, HALF), bf16)
    return pl.pallas_call(
        cut_kernel,
        out_shape=(shape, shape),
        in_specs=[SMEM, HBM],
        out_specs=(VMEM, VMEM),
        scratch_shapes=[
            pltpu.VMEM((TOK, 384), bf16),
            pltpu.VMEM((384, TOK), f32),
            pltpu.SemaphoreType.DMA(()),
        ],
        compiler_params=SMALL,
        name="cut",
    )(place, cot)


def gradient_kernel(place_ref, *refs):
    chunks, blocks, (out_ref, rows_ref, block_rows) = refs[:8], refs[8:12], refs[12:]
    side, y, z_hi, x = (place_ref[n] for n in (0, 1, 2, 4))
    for n, hop in enumerate(HOPS):
        shift = jnp.where(side == 1, 4 if hop == 4 else -hop, hop)
        block_y = (y + shift) & 7
        rows = chunks[n][TOK:, :].astype(f32)
        for other in range(2):
            block_zh = z_hi if other == 0 else 1 - z_hi
            span = slice(other * HALF, (other + 1) * HALF)
            z_lo = 2 * ((shift + 3) >> 2) + other
            source = (shift + 3) - x
            source = jnp.where(side == 1, -source, source) & 3
            block = blocks[0][z_lo]
            for m in range(1, 4):
                block = jnp.where(source == m, blocks[m][z_lo], block)
            block_rows[:, span] = block
            place = pl.multiple_of((2 * block_y + block_zh) * ROWS, ROWS)
            rows_ref[pl.ds(place, ROWS), :] = rows[other * ROWS : (other + 1) * ROWS]
        part = jnp.dot(block_rows[...], chunks[n][:TOK, :], preferred_element_type=f32)
        if n == 0:
            out_ref[...] = part
        else:
            out_ref[...] += part


def gradient(place, chunks, blocks):
    return pl.pallas_call(
        gradient_kernel,
        out_shape=(
            jax.ShapeDtypeStruct((COLS, FEAT), f32),
            jax.ShapeDtypeStruct((16 * ROWS, FEAT), f32),
        ),
        in_specs=[SMEM] + [VMEM] * 12,
        out_specs=(VMEM, VMEM),
        scratch_shapes=[pltpu.VMEM((COLS, TOK), bf16)],
        compiler_params=pltpu.CompilerParams(vmem_limit_bytes=12 * 2**20),
        cost_estimate=pl.CostEstimate(
            flops=2 * 8 * TOK * COLS * FEAT, bytes_accessed=6 * 2**20, transcendentals=0
        ),
        name="gradient",
    )(place, *chunks, *blocks)


def adam_kernel(mine_ref, got_ref, one_ref, two_ref, out_ref):
    grad = mine_ref[...] + got_ref[...]
    first_moment = beta_one * one_ref[...] + (1.0 - beta_one) * grad
    second_moment = beta_two * two_ref[...] + (1.0 - beta_two) * grad * grad
    out_ref[...] = (
        first_moment / first_bias / (jnp.sqrt(second_moment / second_bias) + epsilon)
    ).astype(bf16)


def adam(*operands):
    return pl.pallas_call(
        adam_kernel,
        out_shape=jax.ShapeDtypeStruct((COLS, FEAT), bf16),
        in_specs=[VMEM] * 4,
        out_specs=VMEM,
        compiler_params=pltpu.CompilerParams(vmem_limit_bytes=12 * 2**20),
        name="adam",
    )(*operands)


def step_kernel(place_ref, update_ref, update_got, rows_ref, weight_ref, taken_ref, out_ref):
    update = jnp.where(place_ref[0] == 1, update_ref[...], update_got[...])
    taken_ref[...] = update
    widened = weight_ref[...].astype(f32)
    renewed = (
        widened - learning_rate * (update.astype(f32) + weight_decay * widened)
    ).astype(bf16)
    rows = rows_ref[...].astype(bf16)
    part = lax.dot_general(rows, renewed, (((1,), (1,)), ((), ())), preferred_element_type=f32)
    out_ref[...] = part.reshape(16, ROWS, COLS)


def step(place, *operands):
    return pl.pallas_call(
        step_kernel,
        out_shape=(
            jax.ShapeDtypeStruct((COLS, FEAT), bf16),
            jax.ShapeDtypeStruct((16, ROWS, COLS), f32),
        ),
        in_specs=[SMEM] + [VMEM] * 4,
        out_specs=(VMEM, VMEM),
        compiler_params=pltpu.CompilerParams(vmem_limit_bytes=12 * 2**20),
        name="step",
    )(place, *operands)


def local(
    activations,
    cotangent,
    weight,
    moment_one,
    moment_two,
    queries,
    cache_keys,
    cache_values,
    new_keys,
    new_values,
    lengths,
    token_ids,
):
    q = lax.axis_index(TENSOR)
    place = jnp.stack([lax.axis_index(axis) for axis in AXES]).astype(jnp.int32)

    act = activations[0]
    act_got = permute(act, to_rollout)
    cut_one, cut_two = cut_of(place, cotangent[0])
    own_one = permute(cut_one, cot_shifted(1))
    own_two = permute(cut_two, cot_shifted(0))
    rows = attend(
        (q >> 1).reshape(1),
        queries,
        cache_keys,
        cache_values,
        new_keys,
        new_values,
        lengths,
        token_ids.T,
    )
    half = half_of(place, act, act_got, rows)
    own_one, own_two, _ = lax.optimization_barrier((own_one, own_two, half))
    own = jnp.where(place[0] == 1, own_one, own_two)
    own_spread = jnp.broadcast_to(own[None], (4, COLS, HALF))
    line = gather(own_spread, "z_lo")
    half_got = permute(half, to_partner)
    base = base_of((half, half_got), (own_spread,))
    first = [permute(base, along_y(1))]
    second = [permute(base, along_y(-1))]
    line_tied, ahead, back = lax.optimization_barrier((line, first[0], second[0]))
    first.append(permute(ahead, along_y(1)))
    second.append(permute(back, along_y(-1)))
    blocks = [line] + [permute(line_tied, along_x(step)) for step in (1, 2, -1)]
    ahead, back, *_ = lax.optimization_barrier((first[1], second[1], blocks[1]))
    first.append(permute(ahead, along_y(1)))
    second.append(permute(back, along_y(-1)))
    ahead, _ = lax.optimization_barrier((first[2], blocks[2]))
    first.append(permute(ahead, along_y(1)))
    chunks = [base] + first + second

    mine, all_rows = gradient(place, chunks, blocks)
    got = permute(mine, to_learner)
    update = adam(mine, got, moment_one[0].T, moment_two[0].T)
    update_got = permute(update, to_rollout)
    update, partial = step(place, update, update_got, all_rows, weight.T)

    shares = gather(partial, TENSOR)
    summed = jnp.sum(shares, axis=0).astype(bf16)
    block = permute(summed, transposed)
    spread = jnp.broadcast_to(block[None], (16, ROWS, COLS))
    gathered = gather(spread, TENSOR)
    decoded = gathered.transpose(1, 0, 2).reshape(STEPS, ROWS // STEPS, D)
    return (update.T, decoded)


def solution(mesh):
    fine = Mesh(mesh.devices.reshape(SHAPE), AXES)
    return jax.shard_map(
        local,
        mesh=fine,
        in_specs=(
            P("group", DP, TENSOR),
            P("group", DP, None),
            P(TENSOR, DP),
            P("group", TENSOR, DP),
            P("group", TENSOR, DP),
            P(None, DP, TENSOR),
            P(DP, None, None),
            P(DP, None, None),
            P(None, DP, None),
            P(None, DP, None),
            P(DP),
            P(None, DP),
        ),
        out_specs=(P(TENSOR, DP), P(None, DP, None)),
        check_vma=False,
    )
```

```python
import math

import jax
import jax.numpy as jnp
import numpy as np
from jax import lax
from jax.experimental import pallas as pl
from jax.experimental.pallas import tpu as pltpu
from jax.sharding import Mesh
from jax.sharding import PartitionSpec as P

D = 5120
KVH = 8
HD = 128
EOS = 151645
STEPS = 4
CACHE = 256

learning_rate = 0.0003
weight_decay = 0.1
beta_one = 0.9
beta_two = 0.95
first_bias = 1.0 - 0.9**10
second_bias = 1.0 - 0.95**10
epsilon = 1e-08

AXES = ("group", "y", "z_hi", "z_lo", "x")
SHAPE = (2, 8, 2, 4, 4)
DP, TENSOR = ("y", "z_hi"), ("z_lo", "x")
TOK = 256
HALF = 128
FEAT = 512
COLS = 320
PART = 80
ROWS = 8
PAD = 16
f32, bf16 = jnp.float32, jnp.bfloat16


def permute(value, target):
    pairs = []
    for flat, place in enumerate(np.ndindex(*SHAPE)):
        to = target(*place)
        if to is not None:
            pairs.append((flat, int(np.ravel_multi_index(to, SHAPE))))
    return lax.ppermute(value, AXES, pairs)


def gather(value, axes):
    return lax.all_to_all(value, axes, split_axis=0, concat_axis=0, tiled=True)


def along_y(step):
    return lambda g, y, zh, zl, x: (g, (y + (step if g == 1 else -step)) % 8, zh, zl, x)


def transposed(g, y, zh, zl, x):
    return (g, zl * 2 + (x >> 1), x & 1, y >> 1, (y & 1) * 2 + zh)


def shift_of(z_lo, x):
    return 4 * (z_lo >> 1) + x - 3


def cot_shifted(g, y, zh, zl, x):
    return (g, (y - shift_of(zl, x)) % 8, zh ^ (zl & 1), zl, x)


def along_zl(flip):
    return lambda g, y, zh, zl, x: (g, y, zh, zl ^ flip, x)


def along_x(step):
    return lambda g, y, zh, zl, x: (g, y, zh, zl, (x + (step if g == 1 else -step)) % 4)


def to_learner(g, y, zh, zl, x):
    return (1, y, zh, zl, x) if g == 0 else None


def to_rollout(g, y, zh, zl, x):
    return (0, y, zh, zl, x) if g == 1 else None


FLIPS = (0, 3, 1, 2)
HOPS = (0, 1, 2, 3, 4, -1, -2, -3)


SMALL = pltpu.CompilerParams(vmem_limit_bytes=6 * 2**20)


def attend_kernel(
    head_ref, lengths_ref, ids_ref, q_ref, k_ref, v_ref, nk_ref, nv_ref, out_ref, q_rows, nk_rows, nv_rows
):
    for t in range(STEPS):
        place = slice(2 * t, 2 * t + 2)
        q_rows[place, :] = q_ref[t].astype(f32)
        nk_rows[place, :] = nk_ref[t].astype(f32)
        nv_rows[place, :] = nv_ref[t].astype(f32)
    queries = q_rows[...]
    query = jnp.concatenate(
        [queries[:, h * HD : (h + 1) * HD] for h in range(4)], axis=0
    ).astype(bf16)
    keys = k_ref[...].reshape(2 * CACHE, HD)
    values = v_ref[...].reshape(2 * CACHE, HD)
    fresh_keys = nk_rows[...].astype(bf16)
    fresh_values = nv_rows[...].astype(bf16)
    scale = 1.0 / math.sqrt(HD)
    nt = (((1,), (1,)), ((), ()))
    cache_scores = lax.dot_general(query, keys, nt, preferred_element_type=f32) * scale
    step_scores = lax.dot_general(query, fresh_keys, nt, preferred_element_type=f32) * scale
    count = 4 * ROWS

    def place(width):
        place_row = lax.broadcasted_iota(jnp.int32, (count, width), 0) & (ROWS - 1)
        place_key = lax.broadcasted_iota(jnp.int32, (count, width), 1)
        return place_row >> 1, place_row & 1, place_key

    step, row, key = place(2 * CACHE)
    length = jnp.where(row == 0, lengths_ref[0], lengths_ref[1])
    cache_valid = ((key >> 8) == row) & ((key & (CACHE - 1)) < length)
    step, row, key = place(ROWS)
    step_valid = ((key & 1) == row) & ((key >> 1) <= step)
    cache_scores = jnp.where(cache_valid, cache_scores, -jnp.inf)
    step_scores = jnp.where(step_valid, step_scores, -jnp.inf)
    peak = jnp.maximum(
        jnp.max(cache_scores, axis=-1, keepdims=True), jnp.max(step_scores, axis=-1, keepdims=True)
    )
    cache_exp = jnp.exp(cache_scores - peak)
    step_exp = jnp.exp(step_scores - peak)
    denominator = jnp.sum(cache_exp, axis=-1, keepdims=True) + jnp.sum(
        step_exp, axis=-1, keepdims=True
    )
    cache_probs = (cache_exp / denominator).astype(bf16)
    step_probs = (step_exp / denominator).astype(bf16)
    nn = (((1,), (0,)), ((), ()))
    mixed = lax.dot_general(cache_probs, values, nn, preferred_element_type=f32)
    mixed = mixed + lax.dot_general(step_probs, fresh_values, nn, preferred_element_type=f32)
    step, row, _ = place(HD)
    dead = jnp.zeros((count, HD), jnp.int32)
    for u in range(STEPS - 1):
        for r in range(2):
            ended = (ids_ref[r, u] == EOS).astype(jnp.int32)
            dead = dead + jnp.where((row == r) & (step > u), ended, 0)
    mixed = jnp.where(dead == 0, mixed, 0.0)
    flat = jnp.concatenate([mixed[h * ROWS : (h + 1) * ROWS] for h in range(4)], axis=1)
    out_ref[...] = jnp.concatenate([flat, jnp.zeros_like(flat)], axis=0).astype(bf16)


def attend(head, queries, cache_keys, cache_values, new_keys, new_values, lengths, ids):
    whole = lambda *shape: pl.BlockSpec(shape, lambda i, *_: (0,) * len(shape))
    cache = pl.BlockSpec((2, CACHE, HD), lambda i, m, *_: (0, m[0], 0))
    fresh = pl.BlockSpec((STEPS, 2, HD), lambda i, m, *_: (0, 0, m[0]))
    return pl.pallas_call(
        attend_kernel,
        out_shape=jax.ShapeDtypeStruct((PAD, FEAT), bf16),
        grid_spec=pltpu.PrefetchScalarGridSpec(
            num_scalar_prefetch=3,
            grid=(1,),
            in_specs=[whole(STEPS, 2, FEAT), cache, cache, fresh, fresh],
            out_specs=whole(PAD, FEAT),
            scratch_shapes=[
                pltpu.VMEM((ROWS, FEAT), f32),
                pltpu.VMEM((ROWS, HD), f32),
                pltpu.VMEM((ROWS, HD), f32),
            ],
        ),
        compiler_params=SMALL,
        name="attend",
    )(head, lengths, ids, queries, cache_keys, cache_values, new_keys, new_values)


VMEM = pl.BlockSpec(memory_space=pltpu.VMEM)
SMEM = pl.BlockSpec(memory_space=pltpu.SMEM)
HBM = pl.BlockSpec(memory_space=pl.ANY)


def cut_kernel(place_ref, cot_ref, act_ref, one_ref, pack_ref, window, turned, sem):
    z_lo = place_ref[3]
    q = 2 * ((place_ref[1] - shift_of(z_lo, place_ref[4])) & 7) + (place_ref[2] ^ (z_lo & 1))
    start = pl.multiple_of(((q * 5) >> 1) * 128, 128)
    copy = pltpu.make_async_copy(cot_ref.at[:, pl.ds(start, 384)], window, sem)
    copy.start()
    pack_ref[:HALF, :] = act_ref[HALF:, :]
    copy.wait()
    turned[...] = window[...].astype(f32).T
    shift = pl.multiple_of((q & 1) * 64, 64)
    one_ref[...] = turned[pl.ds(shift, COLS), :HALF].astype(bf16)
    for n in range(4):
        place = pl.ds(pl.multiple_of(shift + n * PART, 16), PART)
        pack_ref[HALF:, n * HALF : (n + 1) * HALF] = turned[place, HALF:].astype(bf16)


def cut_of(place, cot, act):
    return pl.pallas_call(
        cut_kernel,
        out_shape=(
            jax.ShapeDtypeStruct((COLS, HALF), bf16),
            jax.ShapeDtypeStruct((HALF + PART, FEAT), bf16),
        ),
        in_specs=[SMEM, HBM, VMEM],
        out_specs=(VMEM, VMEM),
        scratch_shapes=[
            pltpu.VMEM((TOK, 384), bf16),
            pltpu.VMEM((384, TOK), f32),
            pltpu.SemaphoreType.DMA(()),
        ],
        compiler_params=SMALL,
        name="cut",
    )(place, cot, act)


def half_kernel(place_ref, act_ref, one_ref, pack_ref, rows_ref, cut_ref, out_ref):
    @pl.when(place_ref[0] == 1)
    def _():
        out_ref[0, :HALF, :] = act_ref[:HALF, :]
        cut_ref[...] = one_ref[...]

    @pl.when(place_ref[0] == 0)
    def _():
        out_ref[0, :HALF, :] = pack_ref[:HALF, :]
        for n in range(4):
            cut_ref[n * PART : (n + 1) * PART, :] = pack_ref[HALF:, n * HALF : (n + 1) * HALF]

    out_ref[0, HALF:, :] = rows_ref[...]
    out_ref[1] = out_ref[0]


def half_of(place, *parts):
    return pl.pallas_call(
        half_kernel,
        out_shape=(
            jax.ShapeDtypeStruct((COLS, HALF), bf16),
            jax.ShapeDtypeStruct((2, HALF + PAD, FEAT), bf16),
        ),
        in_specs=[SMEM] + [VMEM] * 4,
        out_specs=(VMEM, VMEM),
        compiler_params=SMALL,
        name="half",
    )(place, *parts)


def base_kernel(halves_ref, out_ref):
    for z_hi in range(2):
        out_ref[z_hi * HALF : (z_hi + 1) * HALF, :] = halves_ref[z_hi, :HALF, :]
    rows = [halves_ref[z_hi, HALF:, :].astype(f32)[:ROWS] for z_hi in range(2)]
    out_ref[TOK:, :] = jnp.concatenate(rows, axis=0).astype(bf16)


def base_of(halves):
    return pl.pallas_call(
        base_kernel,
        out_shape=jax.ShapeDtypeStruct((TOK + PAD, FEAT), bf16),
        in_specs=[VMEM],
        out_specs=VMEM,
        compiler_params=SMALL,
        name="base",
    )(halves)


def gradient_kernel(place_ref, *refs):
    chunks, blocks, (out_ref, rows_ref, block_rows) = refs[:8], refs[8:12], refs[12:]
    side, y, z_hi, own_z_lo, x = (place_ref[n] for n in range(5))
    for n, hop in enumerate(HOPS):
        shift = jnp.where(side == 1, 4 if hop == 4 else -hop, hop)
        block_y = (y + shift) & 7
        rows = chunks[n][TOK:, :].astype(f32)
        for block_zh in range(2):
            span = slice(block_zh * HALF, (block_zh + 1) * HALF)
            flip = own_z_lo ^ (2 * ((shift + 3) >> 2) + (z_hi ^ block_zh))
            slot = sum(jnp.where(flip == f, m, 0) for m, f in enumerate(FLIPS))
            source = (shift + 3) - x
            source = jnp.where(side == 1, -source, source) & 3
            block = blocks[0][slot]
            for m in range(1, 4):
                block = jnp.where(source == m, blocks[m][slot], block)
            block_rows[:, span] = block
            place = pl.multiple_of((2 * block_y + block_zh) * ROWS, ROWS)
            rows_ref[pl.ds(place, ROWS), :] = rows[block_zh * ROWS : (block_zh + 1) * ROWS]
        part = jnp.dot(block_rows[...], chunks[n][:TOK, :], preferred_element_type=f32)
        if n == 0:
            out_ref[...] = part
        else:
            out_ref[...] += part


def gradient(place, chunks, blocks):
    return pl.pallas_call(
        gradient_kernel,
        out_shape=(
            jax.ShapeDtypeStruct((COLS, FEAT), f32),
            jax.ShapeDtypeStruct((16 * ROWS, FEAT), f32),
        ),
        in_specs=[SMEM] + [VMEM] * 12,
        out_specs=(VMEM, VMEM),
        scratch_shapes=[pltpu.VMEM((COLS, TOK), bf16)],
        compiler_params=pltpu.CompilerParams(vmem_limit_bytes=12 * 2**20),
        cost_estimate=pl.CostEstimate(
            flops=2 * 8 * TOK * COLS * FEAT, bytes_accessed=6 * 2**20, transcendentals=0
        ),
        name="gradient",
    )(place, *chunks, *blocks)


def adam_kernel(mine_ref, got_ref, one_ref, two_ref, out_ref):
    grad = mine_ref[...] + got_ref[...]
    first_moment = beta_one * one_ref[...] + (1.0 - beta_one) * grad
    second_moment = beta_two * two_ref[...] + (1.0 - beta_two) * grad * grad
    out_ref[...] = (
        first_moment / first_bias / (jnp.sqrt(second_moment / second_bias) + epsilon)
    ).astype(bf16)


def adam(*operands):
    return pl.pallas_call(
        adam_kernel,
        out_shape=jax.ShapeDtypeStruct((COLS, FEAT), bf16),
        in_specs=[VMEM] * 4,
        out_specs=VMEM,
        compiler_params=pltpu.CompilerParams(vmem_limit_bytes=12 * 2**20),
        name="adam",
    )(*operands)


def step_kernel(place_ref, update_ref, update_got, rows_ref, weight_ref, taken_ref, out_ref):
    update = jnp.where(place_ref[0] == 1, update_ref[...], update_got[...])
    taken_ref[...] = update
    widened = weight_ref[...].astype(f32)
    renewed = (
        widened - learning_rate * (update.astype(f32) + weight_decay * widened)
    ).astype(bf16)
    rows = rows_ref[...].astype(bf16)
    part = lax.dot_general(rows, renewed, (((1,), (1,)), ((), ())), preferred_element_type=f32)
    out_ref[...] = part.reshape(16, ROWS, COLS)


def step(place, *operands):
    return pl.pallas_call(
        step_kernel,
        out_shape=(
            jax.ShapeDtypeStruct((COLS, FEAT), bf16),
            jax.ShapeDtypeStruct((16, ROWS, COLS), f32),
        ),
        in_specs=[SMEM] + [VMEM] * 4,
        out_specs=(VMEM, VMEM),
        compiler_params=pltpu.CompilerParams(vmem_limit_bytes=12 * 2**20),
        name="step",
    )(place, *operands)


def local(
    activations,
    cotangent,
    weight,
    moment_one,
    moment_two,
    queries,
    cache_keys,
    cache_values,
    new_keys,
    new_values,
    lengths,
    token_ids,
):
    q = lax.axis_index(TENSOR)
    place = jnp.stack([lax.axis_index(axis) for axis in AXES]).astype(jnp.int32)

    act = activations[0]
    cut_one, pack = cut_of(place, cotangent[0], act)
    pack_got = permute(pack, to_rollout)
    rows = attend(
        (q >> 1).reshape(1),
        queries,
        cache_keys,
        cache_values,
        new_keys,
        new_values,
        lengths,
        token_ids.T,
    )
    cut, halves = half_of(place, act, cut_one, pack_got, rows)
    own = permute(cut, cot_shifted)
    base = base_of(gather(halves, "z_hi"))
    two_blocks = jnp.stack([own, permute(own, along_zl(3))])
    line = jnp.concatenate([two_blocks, permute(two_blocks, along_zl(1))], axis=0)
    first = [permute(base, along_y(1))]
    second = [permute(base, along_y(-1))]
    line_tied, ahead, back = lax.optimization_barrier((line, first[0], second[0]))
    first.append(permute(ahead, along_y(1)))
    second.append(permute(back, along_y(-1)))
    blocks = [line] + [permute(line_tied, along_x(step)) for step in (1, 2, -1)]
    ahead, back, *_ = lax.optimization_barrier((first[1], second[1], blocks[1]))
    first.append(permute(ahead, along_y(1)))
    second.append(permute(back, along_y(-1)))
    ahead, _ = lax.optimization_barrier((first[2], blocks[2]))
    first.append(permute(ahead, along_y(1)))
    chunks = [base] + first + second

    mine, all_rows = gradient(place, chunks, blocks)
    got = permute(mine, to_learner)
    update = adam(mine, got, moment_one[0].T, moment_two[0].T)
    update_got = permute(update, to_rollout)
    update, partial = step(place, update, update_got, all_rows, weight.T)

    shares = gather(partial, TENSOR)
    summed = jnp.sum(shares, axis=0).astype(bf16)
    block = permute(summed, transposed)
    spread = jnp.broadcast_to(block[None], (16, ROWS, COLS))
    gathered = gather(spread, TENSOR)
    decoded = gathered.transpose(1, 0, 2).reshape(STEPS, ROWS // STEPS, D)
    return (update.T, decoded)


def solution(mesh):
    fine = Mesh(mesh.devices.reshape(SHAPE), AXES)
    return jax.shard_map(
        local,
        mesh=fine,
        in_specs=(
            P("group", DP, TENSOR),
            P("group", DP, None),
            P(TENSOR, DP),
            P("group", TENSOR, DP),
            P("group", TENSOR, DP),
            P(None, DP, TENSOR),
            P(DP, None, None),
            P(DP, None, None),
            P(None, DP, None),
            P(None, DP, None),
            P(DP),
            P(None, DP),
        ),
        out_specs=(P(TENSOR, DP), P(None, DP, None)),
        check_vma=False,
    )
```

```python
import math

import jax
import jax.numpy as jnp
import numpy as np
from jax import lax
from jax.experimental import pallas as pl
from jax.experimental.pallas import tpu as pltpu
from jax.sharding import Mesh
from jax.sharding import PartitionSpec as P

D = 5120
KVH = 8
HD = 128
EOS = 151645
STEPS = 4
CACHE = 256

learning_rate = 0.0003
weight_decay = 0.1
beta_one = 0.9
beta_two = 0.95
first_bias = 1.0 - 0.9**10
second_bias = 1.0 - 0.95**10
epsilon = 1e-08

AXES = ("group", "y", "z_hi", "z_lo", "x")
SHAPE = (2, 8, 2, 4, 4)
DP, TENSOR = ("y", "z_hi"), ("z_lo", "x")
TOK = 256
HALF = 128
FEAT = 512
COLS = 320
PART = 80
ROWS = 8
PAD = 16
f32, bf16 = jnp.float32, jnp.bfloat16


def permute(value, target):
    pairs = []
    for flat, place in enumerate(np.ndindex(*SHAPE)):
        to = target(*place)
        if to is not None:
            pairs.append((flat, int(np.ravel_multi_index(to, SHAPE))))
    return lax.ppermute(value, AXES, pairs)


def gather(value, axes):
    return lax.all_to_all(value, axes, split_axis=0, concat_axis=0, tiled=True)


def along_y(step):
    return lambda g, y, zh, zl, x: (g, (y + (step if g == 1 else -step)) % 8, zh, zl, x)


def shift_of(z_lo, x):
    return 4 * (z_lo >> 1) + x - 3


def cot_shifted(g, y, zh, zl, x):
    return (g, (y - shift_of(zl, x)) % 8, zh ^ (zl & 1), zl, x)


def rows_shifted(g, y, zh, zl, x):
    return (g, (y + shift_of(zl, x)) % 8, zh ^ (zl & 1), zl, x)


def along_zl(flip):
    return lambda g, y, zh, zl, x: (g, y, zh, zl ^ flip, x)


def along_x(step):
    return lambda g, y, zh, zl, x: (g, y, zh, zl, (x + (step if g == 1 else -step)) % 4)


def to_learner(g, y, zh, zl, x):
    return (1, y, zh, zl, x) if g == 0 else None


def to_rollout(g, y, zh, zl, x):
    return (0, y, zh, zl, x) if g == 1 else None


FLIPS = (0, 3, 1, 2)
HOPS = (0, 1, 2, 3, 4, -1, -2, -3)


SMALL = pltpu.CompilerParams(vmem_limit_bytes=6 * 2**20)


def attend_kernel(
    head_ref, lengths_ref, ids_ref, q_ref, k_ref, v_ref, nk_ref, nv_ref, out_ref, q_rows, nk_rows, nv_rows
):
    for t in range(STEPS):
        place = slice(2 * t, 2 * t + 2)
        q_rows[place, :] = q_ref[t].astype(f32)
        nk_rows[place, :] = nk_ref[t].astype(f32)
        nv_rows[place, :] = nv_ref[t].astype(f32)
    queries = q_rows[...]
    query = jnp.concatenate(
        [queries[:, h * HD : (h + 1) * HD] for h in range(4)], axis=0
    ).astype(bf16)
    keys = k_ref[...].reshape(2 * CACHE, HD)
    values = v_ref[...].reshape(2 * CACHE, HD)
    fresh_keys = nk_rows[...].astype(bf16)
    fresh_values = nv_rows[...].astype(bf16)
    scale = 1.0 / math.sqrt(HD)
    nt = (((1,), (1,)), ((), ()))
    cache_scores = lax.dot_general(query, keys, nt, preferred_element_type=f32) * scale
    step_scores = lax.dot_general(query, fresh_keys, nt, preferred_element_type=f32) * scale
    count = 4 * ROWS

    def place(width):
        place_row = lax.broadcasted_iota(jnp.int32, (count, width), 0) & (ROWS - 1)
        place_key = lax.broadcasted_iota(jnp.int32, (count, width), 1)
        return place_row >> 1, place_row & 1, place_key

    step, row, key = place(2 * CACHE)
    length = jnp.where(row == 0, lengths_ref[0], lengths_ref[1])
    cache_valid = ((key >> 8) == row) & ((key & (CACHE - 1)) < length)
    step, row, key = place(ROWS)
    step_valid = ((key & 1) == row) & ((key >> 1) <= step)
    cache_scores = jnp.where(cache_valid, cache_scores, -jnp.inf)
    step_scores = jnp.where(step_valid, step_scores, -jnp.inf)
    peak = jnp.maximum(
        jnp.max(cache_scores, axis=-1, keepdims=True), jnp.max(step_scores, axis=-1, keepdims=True)
    )
    cache_exp = jnp.exp(cache_scores - peak)
    step_exp = jnp.exp(step_scores - peak)
    denominator = jnp.sum(cache_exp, axis=-1, keepdims=True) + jnp.sum(
        step_exp, axis=-1, keepdims=True
    )
    cache_probs = (cache_exp / denominator).astype(bf16)
    step_probs = (step_exp / denominator).astype(bf16)
    nn = (((1,), (0,)), ((), ()))
    mixed = lax.dot_general(cache_probs, values, nn, preferred_element_type=f32)
    mixed = mixed + lax.dot_general(step_probs, fresh_values, nn, preferred_element_type=f32)
    step, row, _ = place(HD)
    dead = jnp.zeros((count, HD), jnp.int32)
    for u in range(STEPS - 1):
        for r in range(2):
            ended = (ids_ref[r, u] == EOS).astype(jnp.int32)
            dead = dead + jnp.where((row == r) & (step > u), ended, 0)
    mixed = jnp.where(dead == 0, mixed, 0.0)
    flat = jnp.concatenate([mixed[h * ROWS : (h + 1) * ROWS] for h in range(4)], axis=1)
    out_ref[...] = jnp.concatenate([flat, jnp.zeros_like(flat)], axis=0).astype(bf16)


def attend(head, queries, cache_keys, cache_values, new_keys, new_values, lengths, ids):
    whole = lambda *shape: pl.BlockSpec(shape, lambda i, *_: (0,) * len(shape))
    cache = pl.BlockSpec((2, CACHE, HD), lambda i, m, *_: (0, m[0], 0))
    fresh = pl.BlockSpec((STEPS, 2, HD), lambda i, m, *_: (0, 0, m[0]))
    return pl.pallas_call(
        attend_kernel,
        out_shape=jax.ShapeDtypeStruct((PAD, FEAT), bf16),
        grid_spec=pltpu.PrefetchScalarGridSpec(
            num_scalar_prefetch=3,
            grid=(1,),
            in_specs=[whole(STEPS, 2, FEAT), cache, cache, fresh, fresh],
            out_specs=whole(PAD, FEAT),
            scratch_shapes=[
                pltpu.VMEM((ROWS, FEAT), f32),
                pltpu.VMEM((ROWS, HD), f32),
                pltpu.VMEM((ROWS, HD), f32),
            ],
        ),
        compiler_params=SMALL,
        name="attend",
    )(head, lengths, ids, queries, cache_keys, cache_values, new_keys, new_values)


VMEM = pl.BlockSpec(memory_space=pltpu.VMEM)
SMEM = pl.BlockSpec(memory_space=pltpu.SMEM)
HBM = pl.BlockSpec(memory_space=pl.ANY)


def cut_kernel(place_ref, cot_ref, act_ref, one_ref, pack_ref, window, turned, sem):
    z_lo = place_ref[3]
    q = 2 * ((place_ref[1] - shift_of(z_lo, place_ref[4])) & 7) + (place_ref[2] ^ (z_lo & 1))
    start = pl.multiple_of(((q * 5) >> 1) * 128, 128)
    copy = pltpu.make_async_copy(cot_ref.at[:, pl.ds(start, 384)], window, sem)
    copy.start()
    pack_ref[:HALF, :] = act_ref[HALF:, :]
    copy.wait()
    turned[...] = window[...].astype(f32).T
    shift = pl.multiple_of((q & 1) * 64, 64)
    one_ref[...] = turned[pl.ds(shift, COLS), :HALF].astype(bf16)
    for n in range(4):
        place = pl.ds(pl.multiple_of(shift + n * PART, 16), PART)
        pack_ref[HALF:, n * HALF : (n + 1) * HALF] = turned[place, HALF:].astype(bf16)


def cut_of(place, cot, act):
    return pl.pallas_call(
        cut_kernel,
        out_shape=(
            jax.ShapeDtypeStruct((COLS, HALF), bf16),
            jax.ShapeDtypeStruct((HALF + PART, FEAT), bf16),
        ),
        in_specs=[SMEM, HBM, VMEM],
        out_specs=(VMEM, VMEM),
        scratch_shapes=[
            pltpu.VMEM((TOK, 384), bf16),
            pltpu.VMEM((384, TOK), f32),
            pltpu.SemaphoreType.DMA(()),
        ],
        compiler_params=SMALL,
        name="cut",
    )(place, cot, act)


def half_kernel(place_ref, act_ref, one_ref, pack_ref, rows_ref, cut_ref, out_ref):
    @pl.when(place_ref[0] == 1)
    def _():
        out_ref[0, :HALF, :] = act_ref[:HALF, :]
        cut_ref[...] = one_ref[...]

    @pl.when(place_ref[0] == 0)
    def _():
        out_ref[0, :HALF, :] = pack_ref[:HALF, :]
        for n in range(4):
            cut_ref[n * PART : (n + 1) * PART, :] = pack_ref[HALF:, n * HALF : (n + 1) * HALF]

    out_ref[0, HALF:, :] = rows_ref[...]
    out_ref[1] = out_ref[0]


def half_of(place, *parts):
    return pl.pallas_call(
        half_kernel,
        out_shape=(
            jax.ShapeDtypeStruct((COLS, HALF), bf16),
            jax.ShapeDtypeStruct((2, HALF + PAD, FEAT), bf16),
        ),
        in_specs=[SMEM] + [VMEM] * 4,
        out_specs=(VMEM, VMEM),
        compiler_params=SMALL,
        name="half",
    )(place, *parts)


def base_kernel(halves_ref, _, out_ref):
    for z_hi in range(2):
        out_ref[z_hi * HALF : (z_hi + 1) * HALF, :] = halves_ref[z_hi, :HALF, :]
    rows = [halves_ref[z_hi, HALF:, :].astype(f32)[:ROWS] for z_hi in range(2)]
    out_ref[TOK:, :] = jnp.concatenate(rows, axis=0).astype(bf16)


def base_of(halves, after):
    return pl.pallas_call(
        base_kernel,
        out_shape=jax.ShapeDtypeStruct((TOK + PAD, FEAT), bf16),
        in_specs=[VMEM, HBM],
        out_specs=VMEM,
        compiler_params=SMALL,
        name="base",
    )(halves, after)


def gradient_kernel(place_ref, *refs):
    chunks, blocks, (out_ref, rows_ref, block_rows) = refs[:8], refs[8:12], refs[12:]
    side, y, z_hi, own_z_lo, x = (place_ref[n] for n in range(5))
    for n, hop in enumerate(HOPS):
        shift = jnp.where(side == 1, 4 if hop == 4 else -hop, hop)
        block_y = (y + shift) & 7
        rows = chunks[n][TOK:, :].astype(f32)
        for block_zh in range(2):
            span = slice(block_zh * HALF, (block_zh + 1) * HALF)
            flip = own_z_lo ^ (2 * ((shift + 3) >> 2) + (z_hi ^ block_zh))
            slot = sum(jnp.where(flip == f, m, 0) for m, f in enumerate(FLIPS))
            source = (shift + 3) - x
            source = jnp.where(side == 1, -source, source) & 3
            block = blocks[0][slot]
            for m in range(1, 4):
                block = jnp.where(source == m, blocks[m][slot], block)
            block_rows[:, span] = block
            place = pl.multiple_of((2 * block_y + block_zh) * ROWS, ROWS)
            rows_ref[pl.ds(place, ROWS), :] = rows[block_zh * ROWS : (block_zh + 1) * ROWS]
        part = jnp.dot(block_rows[...], chunks[n][:TOK, :], preferred_element_type=f32)
        if n == 0:
            out_ref[...] = part
        else:
            out_ref[...] += part


def gradient(place, chunks, blocks):
    return pl.pallas_call(
        gradient_kernel,
        out_shape=(
            jax.ShapeDtypeStruct((COLS, FEAT), f32),
            jax.ShapeDtypeStruct((16 * ROWS, FEAT), f32),
        ),
        in_specs=[SMEM] + [VMEM] * 12,
        out_specs=(VMEM, VMEM),
        scratch_shapes=[pltpu.VMEM((COLS, TOK), bf16)],
        compiler_params=pltpu.CompilerParams(vmem_limit_bytes=12 * 2**20),
        cost_estimate=pl.CostEstimate(
            flops=2 * 8 * TOK * COLS * FEAT, bytes_accessed=6 * 2**20, transcendentals=0
        ),
        name="gradient",
    )(place, *chunks, *blocks)


def adam_kernel(mine_ref, got_ref, one_ref, two_ref, out_ref):
    grad = mine_ref[...] + got_ref[...]
    first_moment = beta_one * one_ref[...] + (1.0 - beta_one) * grad
    second_moment = beta_two * two_ref[...] + (1.0 - beta_two) * grad * grad
    out_ref[...] = (
        first_moment / first_bias / (jnp.sqrt(second_moment / second_bias) + epsilon)
    ).astype(bf16)


def adam(*operands):
    return pl.pallas_call(
        adam_kernel,
        out_shape=jax.ShapeDtypeStruct((COLS, FEAT), bf16),
        in_specs=[VMEM] * 4,
        out_specs=VMEM,
        compiler_params=pltpu.CompilerParams(vmem_limit_bytes=12 * 2**20),
        name="adam",
    )(*operands)


def step_kernel(
    place_ref, update_ref, update_got, rows_ref, weight_ref, taken_ref, out_ref, part_ref
):
    update = jnp.where(place_ref[0] == 1, update_ref[...], update_got[...])
    taken_ref[...] = update
    widened = weight_ref[...].astype(f32)
    renewed = (
        widened - learning_rate * (update.astype(f32) + weight_decay * widened)
    ).astype(bf16)
    rows = rows_ref[...].astype(bf16)
    part_ref[...] = lax.dot_general(
        rows, renewed, (((1,), (1,)), ((), ())), preferred_element_type=f32
    )
    for n in range(16):
        z_lo, x = divmod(n, 4)
        block = 2 * ((place_ref[1] + shift_of(z_lo, x)) & 7) + (place_ref[2] ^ (z_lo & 1))
        out_ref[n] = part_ref[pl.ds(pl.multiple_of(block * ROWS, ROWS), ROWS), :]


def step(place, *operands):
    return pl.pallas_call(
        step_kernel,
        out_shape=(
            jax.ShapeDtypeStruct((COLS, FEAT), bf16),
            jax.ShapeDtypeStruct((16, ROWS, COLS), f32),
        ),
        in_specs=[SMEM] + [VMEM] * 4,
        out_specs=(VMEM, VMEM),
        scratch_shapes=[pltpu.VMEM((16 * ROWS, COLS), f32)],
        compiler_params=pltpu.CompilerParams(vmem_limit_bytes=12 * 2**20),
        name="step",
    )(place, *operands)


def join_kernel(place_ref, blocks_ref, out_ref, pair):
    for y in range(8):
        shift = ((place_ref[1] - y + 3) & 7) - 3
        for z_hi in range(2):
            z_lo = 2 * ((shift + 3) >> 2) + (place_ref[2] ^ z_hi)
            block = blocks_ref[4 * z_lo + ((shift + 3) & 3)]
            pair[:, z_hi * COLS : (z_hi + 1) * COLS] = block.astype(f32)
        out_ref[:, y * 2 * COLS : (y + 1) * 2 * COLS] = pair[...].astype(bf16)


def join(place, blocks):
    return pl.pallas_call(
        join_kernel,
        out_shape=jax.ShapeDtypeStruct((ROWS, D), bf16),
        in_specs=[SMEM, VMEM],
        out_specs=VMEM,
        scratch_shapes=[pltpu.VMEM((ROWS, 2 * COLS), f32)],
        compiler_params=SMALL,
        name="join",
    )(place, blocks)


def local(
    activations,
    cotangent,
    weight,
    moment_one,
    moment_two,
    queries,
    cache_keys,
    cache_values,
    new_keys,
    new_values,
    lengths,
    token_ids,
):
    q = lax.axis_index(TENSOR)
    place = jnp.stack([lax.axis_index(axis) for axis in AXES]).astype(jnp.int32)

    act = activations[0]
    cut_one, pack = cut_of(place, cotangent[0], act)
    pack_got = permute(pack, to_rollout)
    rows = attend(
        (q >> 1).reshape(1),
        queries,
        cache_keys,
        cache_values,
        new_keys,
        new_values,
        lengths,
        token_ids.T,
    )
    cut, halves = half_of(place, act, cut_one, pack_got, rows)
    own = permute(cut, cot_shifted)
    base = base_of(gather(halves, "z_hi"), own)
    ahead = back = base
    first, second = [], []

    def round_y():
        first.append(permute(ahead, along_y(1)))
        second.append(permute(back, along_y(-1)))

    round_y()
    own, _ = lax.optimization_barrier((own, base))
    own_got = permute(own, along_zl(3))
    ahead, back, own_got = lax.optimization_barrier((first[0], second[0], own_got))
    round_y()
    two_blocks = jnp.stack([own, own_got])
    two_got = permute(two_blocks, along_zl(1))
    ahead, back, two_got = lax.optimization_barrier((first[1], second[1], two_got))
    round_y()
    line = jnp.concatenate([two_blocks, two_got], axis=0)
    blocks = [line] + [permute(line, along_x(step)) for step in (1, -1)]
    ahead, line_tied, *_ = lax.optimization_barrier((first[2], line, blocks[1]))
    first.append(permute(ahead, along_y(1)))
    blocks.insert(2, permute(line_tied, along_x(2)))
    chunks = [base] + first + second

    mine, all_rows = gradient(place, chunks, blocks)
    got = permute(mine, to_learner)
    update = adam(mine, got, moment_one[0].T, moment_two[0].T)
    update_got = permute(update, to_rollout)
    update, partial = step(place, update, update_got, all_rows, weight.T)

    shares = gather(partial, TENSOR)
    summed = jnp.sum(shares, axis=0).astype(bf16)
    block = permute(summed, rows_shifted)
    spread = jnp.broadcast_to(block[None], (16, ROWS, COLS))
    decoded = join(place, gather(spread, TENSOR)).reshape(STEPS, ROWS // STEPS, D)
    return (update.T, decoded)


def solution(mesh):
    fine = Mesh(mesh.devices.reshape(SHAPE), AXES)
    return jax.shard_map(
        local,
        mesh=fine,
        in_specs=(
            P("group", DP, TENSOR),
            P("group", DP, None),
            P(TENSOR, DP),
            P("group", TENSOR, DP),
            P("group", TENSOR, DP),
            P(None, DP, TENSOR),
            P(DP, None, None),
            P(DP, None, None),
            P(None, DP, None),
            P(None, DP, None),
            P(DP),
            P(None, DP),
        ),
        out_specs=(P(TENSOR, DP), P(None, DP, None)),
        check_vma=False,
    )
```

```python
import math

import jax
import jax.numpy as jnp
import numpy as np
from jax import lax
from jax.experimental import pallas as pl
from jax.experimental.pallas import tpu as pltpu
from jax.sharding import Mesh
from jax.sharding import PartitionSpec as P

D = 5120
KVH = 8
HD = 128
EOS = 151645
STEPS = 4
CACHE = 256

learning_rate = 0.0003
weight_decay = 0.1
beta_one = 0.9
beta_two = 0.95
first_bias = 1.0 - 0.9**10
second_bias = 1.0 - 0.95**10
epsilon = 1e-08

AXES = ("group", "y", "z_hi", "z_lo", "x")
SHAPE = (2, 8, 2, 4, 4)
DP, TENSOR = ("y", "z_hi"), ("z_lo", "x")
TOK = 256
HALF = 128
FEAT = 512
COLS = 320
PART = 80
ROWS = 8
PAD = 16
f32, bf16 = jnp.float32, jnp.bfloat16


def permute(value, target):
    pairs = []
    for flat, place in enumerate(np.ndindex(*SHAPE)):
        to = target(*place)
        if to is not None:
            pairs.append((flat, int(np.ravel_multi_index(to, SHAPE))))
    return lax.ppermute(value, AXES, pairs)


def gather(value, axes):
    return lax.all_to_all(value, axes, split_axis=0, concat_axis=0, tiled=True)


def along_y(step):
    return lambda g, y, zh, zl, x: (g, (y + (step if g == 1 else -step)) % 8, zh, zl, x)


def shift_of(z_lo, x):
    return 4 * (z_lo >> 1) + x - 3


def cot_shifted(g, y, zh, zl, x):
    return (g, (y - shift_of(zl, x)) % 8, zh ^ (zl & 1), zl, x)


def rows_shifted(g, y, zh, zl, x):
    return (g, (y + shift_of(zl, x)) % 8, zh ^ (zl & 1), zl, x)


def to_learner(g, y, zh, zl, x):
    return (1, y, zh, zl, x) if g == 0 else None


def to_rollout(g, y, zh, zl, x):
    return (0, y, zh, zl, x) if g == 1 else None


HOPS = (0, 1, 2, 3, 4, -1, -2, -3)


SMALL = pltpu.CompilerParams(vmem_limit_bytes=6 * 2**20)


def attend_kernel(
    head_ref, lengths_ref, ids_ref, q_ref, k_ref, v_ref, nk_ref, nv_ref, out_ref, q_rows, nk_rows, nv_rows
):
    for t in range(STEPS):
        place = slice(2 * t, 2 * t + 2)
        q_rows[place, :] = q_ref[t].astype(f32)
        nk_rows[place, :] = nk_ref[t].astype(f32)
        nv_rows[place, :] = nv_ref[t].astype(f32)
    queries = q_rows[...]
    query = jnp.concatenate(
        [queries[:, h * HD : (h + 1) * HD] for h in range(4)], axis=0
    ).astype(bf16)
    keys = k_ref[...].reshape(2 * CACHE, HD)
    values = v_ref[...].reshape(2 * CACHE, HD)
    fresh_keys = nk_rows[...].astype(bf16)
    fresh_values = nv_rows[...].astype(bf16)
    scale = 1.0 / math.sqrt(HD)
    nt = (((1,), (1,)), ((), ()))
    cache_scores = lax.dot_general(query, keys, nt, preferred_element_type=f32) * scale
    step_scores = lax.dot_general(query, fresh_keys, nt, preferred_element_type=f32) * scale
    count = 4 * ROWS

    def place(width):
        place_row = lax.broadcasted_iota(jnp.int32, (count, width), 0) & (ROWS - 1)
        place_key = lax.broadcasted_iota(jnp.int32, (count, width), 1)
        return place_row >> 1, place_row & 1, place_key

    step, row, key = place(2 * CACHE)
    length = jnp.where(row == 0, lengths_ref[0], lengths_ref[1])
    cache_valid = ((key >> 8) == row) & ((key & (CACHE - 1)) < length)
    step, row, key = place(ROWS)
    step_valid = ((key & 1) == row) & ((key >> 1) <= step)
    cache_scores = jnp.where(cache_valid, cache_scores, -jnp.inf)
    step_scores = jnp.where(step_valid, step_scores, -jnp.inf)
    peak = jnp.maximum(
        jnp.max(cache_scores, axis=-1, keepdims=True), jnp.max(step_scores, axis=-1, keepdims=True)
    )
    cache_exp = jnp.exp(cache_scores - peak)
    step_exp = jnp.exp(step_scores - peak)
    denominator = jnp.sum(cache_exp, axis=-1, keepdims=True) + jnp.sum(
        step_exp, axis=-1, keepdims=True
    )
    cache_probs = (cache_exp / denominator).astype(bf16)
    step_probs = (step_exp / denominator).astype(bf16)
    nn = (((1,), (0,)), ((), ()))
    mixed = lax.dot_general(cache_probs, values, nn, preferred_element_type=f32)
    mixed = mixed + lax.dot_general(step_probs, fresh_values, nn, preferred_element_type=f32)
    step, row, _ = place(HD)
    dead = jnp.zeros((count, HD), jnp.int32)
    for u in range(STEPS - 1):
        for r in range(2):
            ended = (ids_ref[r, u] == EOS).astype(jnp.int32)
            dead = dead + jnp.where((row == r) & (step > u), ended, 0)
    mixed = jnp.where(dead == 0, mixed, 0.0)
    flat = jnp.concatenate([mixed[h * ROWS : (h + 1) * ROWS] for h in range(4)], axis=1)
    out_ref[...] = jnp.concatenate([flat, jnp.zeros_like(flat)], axis=0).astype(bf16)


def attend(head, queries, cache_keys, cache_values, new_keys, new_values, lengths, ids):
    whole = lambda *shape: pl.BlockSpec(shape, lambda i, *_: (0,) * len(shape))
    cache = pl.BlockSpec((2, CACHE, HD), lambda i, m, *_: (0, m[0], 0))
    fresh = pl.BlockSpec((STEPS, 2, HD), lambda i, m, *_: (0, 0, m[0]))
    return pl.pallas_call(
        attend_kernel,
        out_shape=jax.ShapeDtypeStruct((PAD, FEAT), bf16),
        grid_spec=pltpu.PrefetchScalarGridSpec(
            num_scalar_prefetch=3,
            grid=(1,),
            in_specs=[whole(STEPS, 2, FEAT), cache, cache, fresh, fresh],
            out_specs=whole(PAD, FEAT),
            scratch_shapes=[
                pltpu.VMEM((ROWS, FEAT), f32),
                pltpu.VMEM((ROWS, HD), f32),
                pltpu.VMEM((ROWS, HD), f32),
            ],
        ),
        compiler_params=SMALL,
        name="attend",
    )(head, lengths, ids, queries, cache_keys, cache_values, new_keys, new_values)


VMEM = pl.BlockSpec(memory_space=pltpu.VMEM)
SMEM = pl.BlockSpec(memory_space=pltpu.SMEM)
HBM = pl.BlockSpec(memory_space=pl.ANY)


def cut_kernel(place_ref, cot_ref, act_ref, one_ref, pack_ref, window, turned, sem):
    z_lo = place_ref[3]
    q = 2 * ((place_ref[1] - shift_of(z_lo, place_ref[4])) & 7) + (place_ref[2] ^ (z_lo & 1))
    start = pl.multiple_of(((q * 5) >> 1) * 128, 128)
    copy = pltpu.make_async_copy(cot_ref.at[:, pl.ds(start, 384)], window, sem)
    copy.start()
    pack_ref[:HALF, :] = act_ref[HALF:, :]
    copy.wait()
    turned[...] = window[...].astype(f32).T
    shift = pl.multiple_of((q & 1) * 64, 64)
    one_ref[...] = turned[pl.ds(shift, COLS), :HALF].astype(bf16)
    for n in range(4):
        place = pl.ds(pl.multiple_of(shift + n * PART, 16), PART)
        pack_ref[HALF:, n * HALF : (n + 1) * HALF] = turned[place, HALF:].astype(bf16)


def cut_of(place, cot, act):
    return pl.pallas_call(
        cut_kernel,
        out_shape=(
            jax.ShapeDtypeStruct((COLS, HALF), bf16),
            jax.ShapeDtypeStruct((HALF + PART, FEAT), bf16),
        ),
        in_specs=[SMEM, HBM, VMEM],
        out_specs=(VMEM, VMEM),
        scratch_shapes=[
            pltpu.VMEM((TOK, 384), bf16),
            pltpu.VMEM((384, TOK), f32),
            pltpu.SemaphoreType.DMA(()),
        ],
        compiler_params=SMALL,
        name="cut",
    )(place, cot, act)


def half_kernel(place_ref, act_ref, one_ref, pack_ref, rows_ref, cut_ref, out_ref):
    @pl.when(place_ref[0] == 1)
    def _():
        out_ref[0, :HALF, :] = act_ref[:HALF, :]
        cut_ref[...] = one_ref[...]

    @pl.when(place_ref[0] == 0)
    def _():
        out_ref[0, :HALF, :] = pack_ref[:HALF, :]
        for n in range(4):
            cut_ref[n * PART : (n + 1) * PART, :] = pack_ref[HALF:, n * HALF : (n + 1) * HALF]

    out_ref[0, HALF:, :] = rows_ref[...]
    out_ref[1] = out_ref[0]


def half_of(place, *parts):
    return pl.pallas_call(
        half_kernel,
        out_shape=(
            jax.ShapeDtypeStruct((COLS, HALF), bf16),
            jax.ShapeDtypeStruct((2, HALF + PAD, FEAT), bf16),
        ),
        in_specs=[SMEM] + [VMEM] * 4,
        out_specs=(VMEM, VMEM),
        compiler_params=SMALL,
        name="half",
    )(place, *parts)


def base_kernel(halves_ref, cut_ref, out_ref, spread_ref):
    for z_hi in range(2):
        out_ref[z_hi * HALF : (z_hi + 1) * HALF, :] = halves_ref[z_hi, :HALF, :]
    rows = [halves_ref[z_hi, HALF:, :].astype(f32)[:ROWS] for z_hi in range(2)]
    out_ref[TOK:, :] = jnp.concatenate(rows, axis=0).astype(bf16)
    for n in range(16):
        spread_ref[n] = cut_ref[...]


def base_of(*operands):
    return pl.pallas_call(
        base_kernel,
        out_shape=(
            jax.ShapeDtypeStruct((TOK + PAD, FEAT), bf16),
            jax.ShapeDtypeStruct((16, COLS, HALF), bf16),
        ),
        in_specs=[VMEM] * 2,
        out_specs=(VMEM, VMEM),
        compiler_params=SMALL,
        name="base",
    )(*operands)


def gradient_kernel(place_ref, *refs):
    chunks, blocks, (out_ref, rows_ref) = refs[:8], refs[8], refs[9:11]
    chunk_rows, block_tiles, block_rows, row_tiles, sems = refs[11:]
    block_copy = pltpu.make_async_copy(blocks, block_tiles, sems.at[0])
    act_copies = [
        pltpu.make_async_copy(
            chunks[n].at[:TOK], chunk_rows.at[pl.ds(n * TOK, TOK)], sems.at[4 + n]
        )
        for n in range(8)
    ]
    row_copies = [
        pltpu.make_async_copy(chunks[n].at[TOK:], row_tiles.at[n], sems.at[12 + n])
        for n in range(8)
    ]
    for copy in [block_copy] + act_copies + row_copies:
        copy.start()
    block_copy.wait()
    side, y, z_hi = (place_ref[n] for n in range(3))
    places = []
    for n, hop in enumerate(HOPS):
        shift = jnp.where(side == 1, 4 if hop == 4 else -hop, hop)
        for block_zh in range(2):
            at = 2 * n + block_zh
            z_lo = 2 * ((shift + 3) >> 2) + (z_hi ^ block_zh)
            block_rows[:, at * HALF : (at + 1) * HALF] = block_tiles[
                4 * z_lo + ((shift + 3) & 3)
            ]
            places.append(2 * ((y + shift) & 7) + block_zh)
    for half in range(2):
        for n in range(4 * half, 4 * half + 4):
            act_copies[n].wait()
        span = pl.ds(half * 4 * TOK, 4 * TOK)
        part = jnp.dot(block_rows[:, span], chunk_rows[span, :], preferred_element_type=f32)
        if half == 0:
            out_ref[...] = part
        else:
            out_ref[...] += part
    for n in range(8):
        row_copies[n].wait()
        rows = row_tiles[n].astype(f32)
        for block_zh in range(2):
            place = pl.multiple_of(places[2 * n + block_zh] * ROWS, ROWS)
            rows_ref[pl.ds(place, ROWS), :] = rows[block_zh * ROWS : (block_zh + 1) * ROWS]


def gradient(place, chunks, blocks):
    return pl.pallas_call(
        gradient_kernel,
        out_shape=(
            jax.ShapeDtypeStruct((COLS, FEAT), f32),
            jax.ShapeDtypeStruct((16 * ROWS, FEAT), f32),
        ),
        in_specs=[SMEM] + [HBM] * 9,
        out_specs=(VMEM, VMEM),
        scratch_shapes=[
            pltpu.VMEM((8 * TOK, FEAT), bf16),
            pltpu.VMEM((16, COLS, HALF), bf16),
            pltpu.VMEM((COLS, 8 * TOK), bf16),
            pltpu.VMEM((8, PAD, FEAT), bf16),
            pltpu.SemaphoreType.DMA((20,)),
        ],
        compiler_params=pltpu.CompilerParams(vmem_limit_bytes=60 * 2**20),
        cost_estimate=pl.CostEstimate(
            flops=2 * 8 * TOK * COLS * FEAT, bytes_accessed=6 * 2**20, transcendentals=0
        ),
        name="gradient",
    )(place, *chunks, blocks)


def adam_kernel(mine_ref, got_ref, one_ref, two_ref, out_ref):
    grad = mine_ref[...] + got_ref[...]
    first_moment = beta_one * one_ref[...] + (1.0 - beta_one) * grad
    second_moment = beta_two * two_ref[...] + (1.0 - beta_two) * grad * grad
    out_ref[...] = (
        first_moment / first_bias / (jnp.sqrt(second_moment / second_bias) + epsilon)
    ).astype(bf16)


def adam(*operands):
    return pl.pallas_call(
        adam_kernel,
        out_shape=jax.ShapeDtypeStruct((COLS, FEAT), bf16),
        in_specs=[VMEM] * 4,
        out_specs=VMEM,
        compiler_params=pltpu.CompilerParams(vmem_limit_bytes=12 * 2**20),
        name="adam",
    )(*operands)


def step_kernel(
    place_ref, update_ref, update_got, rows_ref, weight_ref, taken_ref, out_ref, part_ref
):
    update = jnp.where(place_ref[0] == 1, update_ref[...], update_got[...])
    taken_ref[...] = update
    widened = weight_ref[...].astype(f32)
    renewed = (
        widened - learning_rate * (update.astype(f32) + weight_decay * widened)
    ).astype(bf16)
    rows = rows_ref[...].astype(bf16)
    part_ref[...] = lax.dot_general(
        rows, renewed, (((1,), (1,)), ((), ())), preferred_element_type=f32
    )
    for n in range(16):
        z_lo, x = divmod(n, 4)
        block = 2 * ((place_ref[1] + shift_of(z_lo, x)) & 7) + (place_ref[2] ^ (z_lo & 1))
        out_ref[n] = part_ref[pl.ds(pl.multiple_of(block * ROWS, ROWS), ROWS), :]


def step(place, *operands):
    return pl.pallas_call(
        step_kernel,
        out_shape=(
            jax.ShapeDtypeStruct((COLS, FEAT), bf16),
            jax.ShapeDtypeStruct((16, ROWS, COLS), f32),
        ),
        in_specs=[SMEM] + [VMEM] * 4,
        out_specs=(VMEM, VMEM),
        scratch_shapes=[pltpu.VMEM((16 * ROWS, COLS), f32)],
        compiler_params=pltpu.CompilerParams(vmem_limit_bytes=12 * 2**20),
        name="step",
    )(place, *operands)


def join_kernel(place_ref, blocks_ref, out_ref, pair):
    for y in range(8):
        shift = ((place_ref[1] - y + 3) & 7) - 3
        for z_hi in range(2):
            z_lo = 2 * ((shift + 3) >> 2) + (place_ref[2] ^ z_hi)
            block = blocks_ref[4 * z_lo + ((shift + 3) & 3)]
            pair[:, z_hi * COLS : (z_hi + 1) * COLS] = block.astype(f32)
        out_ref[:, y * 2 * COLS : (y + 1) * 2 * COLS] = pair[...].astype(bf16)


def join(place, blocks):
    return pl.pallas_call(
        join_kernel,
        out_shape=jax.ShapeDtypeStruct((ROWS, D), bf16),
        in_specs=[SMEM, VMEM],
        out_specs=VMEM,
        scratch_shapes=[pltpu.VMEM((ROWS, 2 * COLS), f32)],
        compiler_params=SMALL,
        name="join",
    )(place, blocks)


def local(
    activations,
    cotangent,
    weight,
    moment_one,
    moment_two,
    queries,
    cache_keys,
    cache_values,
    new_keys,
    new_values,
    lengths,
    token_ids,
):
    q = lax.axis_index(TENSOR)
    place = jnp.stack([lax.axis_index(axis) for axis in AXES]).astype(jnp.int32)

    act = activations[0]
    cut_one, pack = cut_of(place, cotangent[0], act)
    pack_got = permute(pack, to_rollout)
    rows = attend(
        (q >> 1).reshape(1),
        queries,
        cache_keys,
        cache_values,
        new_keys,
        new_values,
        lengths,
        token_ids.T,
    )
    cut, halves = half_of(place, act, cut_one, pack_got, rows)
    own = permute(cut, cot_shifted)
    base, own_spread = base_of(gather(halves, "z_hi"), own)
    blocks = gather(own_spread, TENSOR)
    ahead = back = base
    first, second = [], []
    for _ in range(3):
        first.append(permute(ahead, along_y(1)))
        second.append(permute(back, along_y(-1)))
        ahead, back = lax.optimization_barrier((first[-1], second[-1]))
    first.append(permute(ahead, along_y(1)))
    chunks = [base] + first + second

    mine, all_rows = gradient(place, chunks, blocks)
    got = permute(mine, to_learner)
    update = adam(mine, got, moment_one[0].T, moment_two[0].T)
    update_got = permute(update, to_rollout)
    update, partial = step(place, update, update_got, all_rows, weight.T)

    shares = gather(partial, TENSOR)
    summed = jnp.sum(shares, axis=0).astype(bf16)
    block = permute(summed, rows_shifted)
    spread = jnp.broadcast_to(block[None], (16, ROWS, COLS))
    decoded = join(place, gather(spread, TENSOR)).reshape(STEPS, ROWS // STEPS, D)
    return (update.T, decoded)


def solution(mesh):
    fine = Mesh(mesh.devices.reshape(SHAPE), AXES)
    return jax.shard_map(
        local,
        mesh=fine,
        in_specs=(
            P("group", DP, TENSOR),
            P("group", DP, None),
            P(TENSOR, DP),
            P("group", TENSOR, DP),
            P("group", TENSOR, DP),
            P(None, DP, TENSOR),
            P(DP, None, None),
            P(DP, None, None),
            P(None, DP, None),
            P(None, DP, None),
            P(DP),
            P(None, DP),
        ),
        out_specs=(P(TENSOR, DP), P(None, DP, None)),
        check_vma=False,
    )
```

```python
import math

import jax
import jax.numpy as jnp
import numpy as np
from jax import lax
from jax.experimental import pallas as pl
from jax.experimental.pallas import tpu as pltpu
from jax.sharding import Mesh
from jax.sharding import PartitionSpec as P

D = 5120
KVH = 8
HD = 128
EOS = 151645
STEPS = 4
CACHE = 256

learning_rate = 0.0003
weight_decay = 0.1
beta_one = 0.9
beta_two = 0.95
first_bias = 1.0 - 0.9**10
second_bias = 1.0 - 0.95**10
epsilon = 1e-08

AXES = ("group", "y", "z_hi", "z_lo", "x")
SHAPE = (2, 8, 2, 4, 4)
DP, TENSOR = ("y", "z_hi"), ("z_lo", "x")
TOK = 256
HALF = 128
FEAT = 512
COLS = 320
PART = 80
ROWS = 8
PAD = 16
f32, bf16 = jnp.float32, jnp.bfloat16


def permute(value, target):
    pairs = []
    for flat, place in enumerate(np.ndindex(*SHAPE)):
        to = target(*place)
        if to is not None:
            pairs.append((flat, int(np.ravel_multi_index(to, SHAPE))))
    return lax.ppermute(value, AXES, pairs)


def gather(value, axes):
    return lax.all_to_all(value, axes, split_axis=0, concat_axis=0, tiled=True)


def to_partner(g, y, zh, zl, x):
    return (g, y, 1 - zh, zl, x)


def along_y(step):
    return lambda g, y, zh, zl, x: (g, (y + (step if g == 1 else -step)) % 8, zh, zl, x)


def shift_of(z_lo, x):
    return 4 * (z_lo >> 1) + x - 3


def cot_shifted(g, y, zh, zl, x):
    return (g, (y - shift_of(zl, x)) % 8, zh ^ (zl & 1), zl, x)


def rows_shifted(g, y, zh, zl, x):
    return (g, (y + shift_of(zl, x)) % 8, zh ^ (zl & 1), zl, x)


def to_learner(g, y, zh, zl, x):
    return (1, y, zh, zl, x) if g == 0 else None


def to_rollout(g, y, zh, zl, x):
    return (0, y, zh, zl, x) if g == 1 else None


HOPS = (0, 1, 2, 3, 4, -1, -2, -3)


SMALL = pltpu.CompilerParams(vmem_limit_bytes=6 * 2**20)
LONG = pl.CostEstimate(flops=0, bytes_accessed=2**26, transcendentals=0)


def attend_kernel(
    head_ref, lengths_ref, ids_ref, q_ref, k_ref, v_ref, nk_ref, nv_ref, _, out_ref, q_rows, nk_rows, nv_rows
):
    for t in range(STEPS):
        place = slice(2 * t, 2 * t + 2)
        q_rows[place, :] = q_ref[t].astype(f32)
        nk_rows[place, :] = nk_ref[t].astype(f32)
        nv_rows[place, :] = nv_ref[t].astype(f32)
    queries = q_rows[...]
    query = jnp.concatenate(
        [queries[:, h * HD : (h + 1) * HD] for h in range(4)], axis=0
    ).astype(bf16)
    keys = k_ref[...].reshape(2 * CACHE, HD)
    values = v_ref[...].reshape(2 * CACHE, HD)
    fresh_keys = nk_rows[...].astype(bf16)
    fresh_values = nv_rows[...].astype(bf16)
    scale = 1.0 / math.sqrt(HD)
    nt = (((1,), (1,)), ((), ()))
    cache_scores = lax.dot_general(query, keys, nt, preferred_element_type=f32) * scale
    step_scores = lax.dot_general(query, fresh_keys, nt, preferred_element_type=f32) * scale
    count = 4 * ROWS

    def place(width):
        place_row = lax.broadcasted_iota(jnp.int32, (count, width), 0) & (ROWS - 1)
        place_key = lax.broadcasted_iota(jnp.int32, (count, width), 1)
        return place_row >> 1, place_row & 1, place_key

    step, row, key = place(2 * CACHE)
    length = jnp.where(row == 0, lengths_ref[0], lengths_ref[1])
    cache_valid = ((key >> 8) == row) & ((key & (CACHE - 1)) < length)
    step, row, key = place(ROWS)
    step_valid = ((key & 1) == row) & ((key >> 1) <= step)
    cache_scores = jnp.where(cache_valid, cache_scores, -jnp.inf)
    step_scores = jnp.where(step_valid, step_scores, -jnp.inf)
    peak = jnp.maximum(
        jnp.max(cache_scores, axis=-1, keepdims=True), jnp.max(step_scores, axis=-1, keepdims=True)
    )
    cache_exp = jnp.exp(cache_scores - peak)
    step_exp = jnp.exp(step_scores - peak)
    denominator = jnp.sum(cache_exp, axis=-1, keepdims=True) + jnp.sum(
        step_exp, axis=-1, keepdims=True
    )
    cache_probs = (cache_exp / denominator).astype(bf16)
    step_probs = (step_exp / denominator).astype(bf16)
    nn = (((1,), (0,)), ((), ()))
    mixed = lax.dot_general(cache_probs, values, nn, preferred_element_type=f32)
    mixed = mixed + lax.dot_general(step_probs, fresh_values, nn, preferred_element_type=f32)
    step, row, _ = place(HD)
    dead = jnp.zeros((count, HD), jnp.int32)
    for u in range(STEPS - 1):
        for r in range(2):
            ended = (ids_ref[r, u] == EOS).astype(jnp.int32)
            dead = dead + jnp.where((row == r) & (step > u), ended, 0)
    mixed = jnp.where(dead == 0, mixed, 0.0)
    flat = jnp.concatenate([mixed[h * ROWS : (h + 1) * ROWS] for h in range(4)], axis=1)
    out_ref[...] = jnp.concatenate([flat, jnp.zeros_like(flat)], axis=0).astype(bf16)


def attend(head, queries, cache_keys, cache_values, new_keys, new_values, lengths, ids, after):
    whole = lambda *shape: pl.BlockSpec(shape, lambda i, *_: (0,) * len(shape))
    cache = pl.BlockSpec((2, CACHE, HD), lambda i, m, *_: (0, m[0], 0))
    fresh = pl.BlockSpec((STEPS, 2, HD), lambda i, m, *_: (0, 0, m[0]))
    return pl.pallas_call(
        attend_kernel,
        out_shape=jax.ShapeDtypeStruct((PAD, FEAT), bf16),
        grid_spec=pltpu.PrefetchScalarGridSpec(
            num_scalar_prefetch=3,
            grid=(1,),
            in_specs=[whole(STEPS, 2, FEAT), cache, cache, fresh, fresh, pl.BlockSpec(memory_space=pl.ANY)],
            out_specs=whole(PAD, FEAT),
            scratch_shapes=[
                pltpu.VMEM((ROWS, FEAT), f32),
                pltpu.VMEM((ROWS, HD), f32),
                pltpu.VMEM((ROWS, HD), f32),
            ],
        ),
        compiler_params=SMALL,
        name="attend",
    )(head, lengths, ids, queries, cache_keys, cache_values, new_keys, new_values, after)


VMEM = pl.BlockSpec(memory_space=pltpu.VMEM)
SMEM = pl.BlockSpec(memory_space=pltpu.SMEM)
HBM = pl.BlockSpec(memory_space=pl.ANY)


def cut_kernel(place_ref, cot_ref, act_ref, one_ref, pack_ref, window, turned, sem):
    z_lo = place_ref[3]
    q = 2 * ((place_ref[1] - shift_of(z_lo, place_ref[4])) & 7) + (place_ref[2] ^ (z_lo & 1))
    start = pl.multiple_of(((q * 5) >> 1) * 128, 128)
    copy = pltpu.make_async_copy(cot_ref.at[:, pl.ds(start, 384)], window, sem)
    copy.start()
    pack_ref[:HALF, :] = act_ref[HALF:, :]
    copy.wait()
    turned[...] = window[...].astype(f32).T
    shift = pl.multiple_of((q & 1) * 64, 64)
    one_ref[...] = turned[pl.ds(shift, COLS), :HALF].astype(bf16)
    for n in range(4):
        place = pl.ds(pl.multiple_of(shift + n * PART, 16), PART)
        pack_ref[HALF:, n * HALF : (n + 1) * HALF] = turned[place, HALF:].astype(bf16)


def cut_of(place, cot, act):
    return pl.pallas_call(
        cut_kernel,
        out_shape=(
            jax.ShapeDtypeStruct((COLS, HALF), bf16),
            jax.ShapeDtypeStruct((HALF + PART, FEAT), bf16),
        ),
        in_specs=[SMEM, HBM, VMEM],
        out_specs=(VMEM, VMEM),
        scratch_shapes=[
            pltpu.VMEM((TOK, 384), bf16),
            pltpu.VMEM((384, TOK), f32),
            pltpu.SemaphoreType.DMA(()),
        ],
        compiler_params=pltpu.CompilerParams(vmem_limit_bytes=60 * 2**20),
        name="cut",
    )(place, cot, act)


def unpack_kernel(place_ref, one_ref, pack_ref, out_ref):
    @pl.when(place_ref[0] == 1)
    def _():
        out_ref[...] = one_ref[...]

    @pl.when(place_ref[0] == 0)
    def _():
        for n in range(4):
            out_ref[n * PART : (n + 1) * PART, :] = pack_ref[HALF:, n * HALF : (n + 1) * HALF]


def unpack(place, *parts):
    return pl.pallas_call(
        unpack_kernel,
        out_shape=jax.ShapeDtypeStruct((COLS, HALF), bf16),
        in_specs=[SMEM] + [VMEM] * 2,
        out_specs=VMEM,
        compiler_params=SMALL,
        name="unpack",
    )(place, *parts)


def half_kernel(place_ref, act_ref, pack_ref, rows_ref, _, out_ref):
    @pl.when(place_ref[0] == 1)
    def _():
        out_ref[:HALF, :] = act_ref[:HALF, :]

    @pl.when(place_ref[0] == 0)
    def _():
        out_ref[:HALF, :] = pack_ref[:HALF, :]

    out_ref[HALF:, :] = rows_ref[...]


def half_of(place, *parts):
    return pl.pallas_call(
        half_kernel,
        out_shape=jax.ShapeDtypeStruct((HALF + PAD, FEAT), bf16),
        in_specs=[SMEM] + [VMEM] * 3 + [HBM],
        out_specs=VMEM,
        compiler_params=SMALL,
        cost_estimate=LONG,
        name="half",
    )(place, *parts)


def spread_kernel(cut_ref, _, out_ref):
    for n in range(16):
        out_ref[n] = cut_ref[...]


def spread_of(*operands):
    return pl.pallas_call(
        spread_kernel,
        out_shape=jax.ShapeDtypeStruct((16, COLS, HALF), bf16),
        in_specs=[VMEM, HBM],
        out_specs=VMEM,
        compiler_params=SMALL,
        cost_estimate=LONG,
        name="spread",
    )(*operands)


def base_kernel(place_ref, mine_ref, got_ref, _, out_ref):
    z_hi = place_ref[2]
    for ref, side in ((mine_ref, z_hi), (got_ref, 1 - z_hi)):
        out_ref[pl.ds(pl.multiple_of(side * HALF, HALF), HALF), :] = ref[:HALF, :]
    mine, got = (ref[HALF:, :].astype(f32)[:ROWS] for ref in (mine_ref, got_ref))
    rows = [jnp.where(z_hi == 0, mine, got), jnp.where(z_hi == 0, got, mine)]
    out_ref[TOK:, :] = jnp.concatenate(rows, axis=0).astype(bf16)


def base_of(place, *operands):
    return pl.pallas_call(
        base_kernel,
        out_shape=jax.ShapeDtypeStruct((TOK + PAD, FEAT), bf16),
        in_specs=[SMEM] + [VMEM] * 2 + [HBM],
        out_specs=VMEM,
        compiler_params=SMALL,
        name="base",
    )(place, *operands)


def gradient_kernel(place_ref, *refs):
    chunks, blocks, (out_ref, rows_ref) = refs[:8], refs[8], refs[9:11]
    chunk_rows, block_tiles, block_rows, row_tiles, sems = refs[11:]
    block_copy = pltpu.make_async_copy(blocks, block_tiles, sems.at[0])
    act_copies = [
        pltpu.make_async_copy(
            chunks[n].at[:TOK], chunk_rows.at[pl.ds(n * TOK, TOK)], sems.at[4 + n]
        )
        for n in range(8)
    ]
    row_copies = [
        pltpu.make_async_copy(chunks[n].at[TOK:], row_tiles.at[n], sems.at[12 + n])
        for n in range(8)
    ]
    for copy in [block_copy] + act_copies + row_copies:
        copy.start()
    block_copy.wait()
    side, y, z_hi = (place_ref[n] for n in range(3))
    places = []
    for n, hop in enumerate(HOPS):
        shift = jnp.where(side == 1, 4 if hop == 4 else -hop, hop)
        for block_zh in range(2):
            at = 2 * n + block_zh
            z_lo = 2 * ((shift + 3) >> 2) + (z_hi ^ block_zh)
            block_rows[:, at * HALF : (at + 1) * HALF] = block_tiles[
                4 * z_lo + ((shift + 3) & 3)
            ]
            places.append(2 * ((y + shift) & 7) + block_zh)
    for half in range(2):
        for n in range(4 * half, 4 * half + 4):
            act_copies[n].wait()
        span = pl.ds(half * 4 * TOK, 4 * TOK)
        part = jnp.dot(block_rows[:, span], chunk_rows[span, :], preferred_element_type=f32)
        if half == 0:
            out_ref[...] = part
        else:
            out_ref[...] += part
    for n in range(8):
        row_copies[n].wait()
        rows = row_tiles[n].astype(f32)
        for block_zh in range(2):
            place = pl.multiple_of(places[2 * n + block_zh] * ROWS, ROWS)
            rows_ref[pl.ds(place, ROWS), :] = rows[block_zh * ROWS : (block_zh + 1) * ROWS]


def gradient(place, chunks, blocks):
    return pl.pallas_call(
        gradient_kernel,
        out_shape=(
            jax.ShapeDtypeStruct((COLS, FEAT), f32),
            jax.ShapeDtypeStruct((16 * ROWS, FEAT), f32),
        ),
        in_specs=[SMEM] + [HBM] * 9,
        out_specs=(VMEM, VMEM),
        scratch_shapes=[
            pltpu.VMEM((8 * TOK, FEAT), bf16),
            pltpu.VMEM((16, COLS, HALF), bf16),
            pltpu.VMEM((COLS, 8 * TOK), bf16),
            pltpu.VMEM((8, PAD, FEAT), bf16),
            pltpu.SemaphoreType.DMA((20,)),
        ],
        compiler_params=pltpu.CompilerParams(vmem_limit_bytes=60 * 2**20),
        cost_estimate=pl.CostEstimate(
            flops=2 * 8 * TOK * COLS * FEAT, bytes_accessed=6 * 2**20, transcendentals=0
        ),
        name="gradient",
    )(place, *chunks, blocks)


def adam_kernel(mine_ref, got_ref, one_ref, two_ref, out_ref):
    grad = mine_ref[...] + got_ref[...]
    first_moment = beta_one * one_ref[...] + (1.0 - beta_one) * grad
    second_moment = beta_two * two_ref[...] + (1.0 - beta_two) * grad * grad
    out_ref[...] = (
        first_moment / first_bias / (jnp.sqrt(second_moment / second_bias) + epsilon)
    ).astype(bf16)


def adam(*operands):
    return pl.pallas_call(
        adam_kernel,
        out_shape=jax.ShapeDtypeStruct((COLS, FEAT), bf16),
        in_specs=[VMEM] * 4,
        out_specs=VMEM,
        compiler_params=pltpu.CompilerParams(vmem_limit_bytes=12 * 2**20),
        name="adam",
    )(*operands)


def step_kernel(
    place_ref, update_ref, update_got, rows_ref, weight_ref, taken_ref, out_ref, part_ref
):
    update = jnp.where(place_ref[0] == 1, update_ref[...], update_got[...])
    taken_ref[...] = update
    widened = weight_ref[...].astype(f32)
    renewed = (
        widened - learning_rate * (update.astype(f32) + weight_decay * widened)
    ).astype(bf16)
    rows = rows_ref[...].astype(bf16)
    part_ref[...] = lax.dot_general(
        rows, renewed, (((1,), (1,)), ((), ())), preferred_element_type=f32
    )
    for n in range(16):
        z_lo, x = divmod(n, 4)
        block = 2 * ((place_ref[1] + shift_of(z_lo, x)) & 7) + (place_ref[2] ^ (z_lo & 1))
        out_ref[n] = part_ref[pl.ds(pl.multiple_of(block * ROWS, ROWS), ROWS), :]


def step(place, *operands):
    return pl.pallas_call(
        step_kernel,
        out_shape=(
            jax.ShapeDtypeStruct((COLS, FEAT), bf16),
            jax.ShapeDtypeStruct((16, ROWS, COLS), f32),
        ),
        in_specs=[SMEM] + [VMEM] * 4,
        out_specs=(VMEM, VMEM),
        scratch_shapes=[pltpu.VMEM((16 * ROWS, COLS), f32)],
        compiler_params=pltpu.CompilerParams(vmem_limit_bytes=12 * 2**20),
        name="step",
    )(place, *operands)


def join_kernel(place_ref, blocks_ref, out_ref, pair):
    for y in range(8):
        shift = ((place_ref[1] - y + 3) & 7) - 3
        for z_hi in range(2):
            z_lo = 2 * ((shift + 3) >> 2) + (place_ref[2] ^ z_hi)
            block = blocks_ref[4 * z_lo + ((shift + 3) & 3)]
            pair[:, z_hi * COLS : (z_hi + 1) * COLS] = block.astype(f32)
        out_ref[:, y * 2 * COLS : (y + 1) * 2 * COLS] = pair[...].astype(bf16)


def join(place, blocks):
    return pl.pallas_call(
        join_kernel,
        out_shape=jax.ShapeDtypeStruct((ROWS, D), bf16),
        in_specs=[SMEM, VMEM],
        out_specs=VMEM,
        scratch_shapes=[pltpu.VMEM((ROWS, 2 * COLS), f32)],
        compiler_params=SMALL,
        name="join",
    )(place, blocks)


def local(
    activations,
    cotangent,
    weight,
    moment_one,
    moment_two,
    queries,
    cache_keys,
    cache_values,
    new_keys,
    new_values,
    lengths,
    token_ids,
):
    q = lax.axis_index(TENSOR)
    place = jnp.stack([lax.axis_index(axis) for axis in AXES]).astype(jnp.int32)

    act = activations[0]
    cut_one, pack = cut_of(place, cotangent[0], act)
    pack_got = permute(pack, to_rollout)
    cut = unpack(place, cut_one, pack_got)
    own = permute(cut, cot_shifted)
    rows = attend(
        (q >> 1).reshape(1),
        queries,
        cache_keys,
        cache_values,
        new_keys,
        new_values,
        lengths,
        token_ids.T,
        cut,
    )
    half = half_of(place, act, pack_got, rows, own)
    half_got = permute(half, to_partner)
    own_spread = spread_of(own, half)
    blocks = gather(own_spread, TENSOR)
    base = base_of(place, half, half_got, own_spread)
    ahead = back = base
    first, second = [], []
    for _ in range(3):
        first.append(permute(ahead, along_y(1)))
        second.append(permute(back, along_y(-1)))
        ahead, back = lax.optimization_barrier((first[-1], second[-1]))
    first.append(permute(ahead, along_y(1)))
    chunks = [base] + first + second

    mine, all_rows = gradient(place, chunks, blocks)
    got = permute(mine, to_learner)
    update = adam(mine, got, moment_one[0].T, moment_two[0].T)
    update_got = permute(update, to_rollout)
    update, partial = step(place, update, update_got, all_rows, weight.T)

    shares = gather(partial, TENSOR)
    summed = jnp.sum(shares, axis=0).astype(bf16)
    block = permute(summed, rows_shifted)
    spread = jnp.broadcast_to(block[None], (16, ROWS, COLS))
    decoded = join(place, gather(spread, TENSOR)).reshape(STEPS, ROWS // STEPS, D)
    return (update.T, decoded)


def solution(mesh):
    fine = Mesh(mesh.devices.reshape(SHAPE), AXES)
    return jax.shard_map(
        local,
        mesh=fine,
        in_specs=(
            P("group", DP, TENSOR),
            P("group", DP, None),
            P(TENSOR, DP),
            P("group", TENSOR, DP),
            P("group", TENSOR, DP),
            P(None, DP, TENSOR),
            P(DP, None, None),
            P(DP, None, None),
            P(None, DP, None),
            P(None, DP, None),
            P(DP),
            P(None, DP),
        ),
        out_specs=(P(TENSOR, DP), P(None, DP, None)),
        check_vma=False,
    )
```

```python
import math

import jax
import jax.numpy as jnp
import numpy as np
from jax import lax
from jax.experimental import pallas as pl
from jax.experimental.pallas import tpu as pltpu
from jax.sharding import Mesh
from jax.sharding import PartitionSpec as P

D = 5120
KVH = 8
HD = 128
EOS = 151645
STEPS = 4
CACHE = 256

learning_rate = 0.0003
weight_decay = 0.1
beta_one = 0.9
beta_two = 0.95
first_bias = 1.0 - 0.9**10
second_bias = 1.0 - 0.95**10
epsilon = 1e-08

AXES = ("group", "y", "z_hi", "z_lo", "x")
SHAPE = (2, 8, 2, 4, 4)
DP, TENSOR = ("y", "z_hi"), ("z_lo", "x")
TOK = 256
FEAT = 512
COLS = 320
ROWS = 8
PAD = 16
f32, bf16 = jnp.float32, jnp.bfloat16


def permute(value, target):
    pairs = []
    for flat, place in enumerate(np.ndindex(*SHAPE)):
        to = target(*place)
        if to is not None:
            pairs.append((flat, int(np.ravel_multi_index(to, SHAPE))))
    return lax.ppermute(value, AXES, pairs)


def gather(value, axes):
    return lax.all_to_all(value, axes, split_axis=0, concat_axis=0, tiled=True)


def to_partner(g, y, zh, zl, x):
    return (0, y, 1 - zh, zl, x) if g == 1 else None


def keeper(zl):
    return 1 - (zl & 1)


def shift_of(z_lo, x):
    return 4 * (z_lo >> 1) + x - 3


def cot_shifted(g, y, zh, zl, x):
    to = (keeper(zl), (y - shift_of(zl, x)) % 8, zh ^ (zl & 1), zl, x)
    return to if g == 1 else None


def along_zl(flip):
    return lambda g, y, zh, zl, x: (g, y, zh, zl ^ flip, x) if g == keeper(zl) else None


def along_x(step):
    return lambda g, y, zh, zl, x: (g, y, zh, zl, (x + (step if g == 1 else -step)) % 4)


def transposed(g, y, zh, zl, x):
    return (g, zl * 2 + (x >> 1), x & 1, y >> 1, (y & 1) * 2 + zh)


def other_core(g, y, zh, zl, x):
    return (1 - g, y, zh, zl, x)


def to_rollout(g, y, zh, zl, x):
    return (0, y, zh, zl, x) if g == 1 else None


SMALL = pltpu.CompilerParams(vmem_limit_bytes=6 * 2**20)


def attend_kernel(
    head_ref, lengths_ref, ids_ref, q_ref, k_ref, v_ref, nk_ref, nv_ref, out_ref, q_rows, nk_rows, nv_rows
):
    for t in range(STEPS):
        place = slice(2 * t, 2 * t + 2)
        q_rows[place, :] = q_ref[t].astype(f32)
        nk_rows[place, :] = nk_ref[t].astype(f32)
        nv_rows[place, :] = nv_ref[t].astype(f32)
    queries = q_rows[...]
    query = jnp.concatenate(
        [queries[:, h * HD : (h + 1) * HD] for h in range(4)], axis=0
    ).astype(bf16)
    keys = k_ref[...].reshape(2 * CACHE, HD)
    values = v_ref[...].reshape(2 * CACHE, HD)
    fresh_keys = nk_rows[...].astype(bf16)
    fresh_values = nv_rows[...].astype(bf16)
    scale = 1.0 / math.sqrt(HD)
    nt = (((1,), (1,)), ((), ()))
    cache_scores = lax.dot_general(query, keys, nt, preferred_element_type=f32) * scale
    step_scores = lax.dot_general(query, fresh_keys, nt, preferred_element_type=f32) * scale
    count = 4 * ROWS

    def place(width):
        place_row = lax.broadcasted_iota(jnp.int32, (count, width), 0) & (ROWS - 1)
        place_key = lax.broadcasted_iota(jnp.int32, (count, width), 1)
        return place_row >> 1, place_row & 1, place_key

    step, row, key = place(2 * CACHE)
    length = jnp.where(row == 0, lengths_ref[0], lengths_ref[1])
    cache_valid = ((key >> 8) == row) & ((key & (CACHE - 1)) < length)
    step, row, key = place(ROWS)
    step_valid = ((key & 1) == row) & ((key >> 1) <= step)
    cache_scores = jnp.where(cache_valid, cache_scores, -jnp.inf)
    step_scores = jnp.where(step_valid, step_scores, -jnp.inf)
    peak = jnp.maximum(
        jnp.max(cache_scores, axis=-1, keepdims=True), jnp.max(step_scores, axis=-1, keepdims=True)
    )
    cache_exp = jnp.exp(cache_scores - peak)
    step_exp = jnp.exp(step_scores - peak)
    denominator = jnp.sum(cache_exp, axis=-1, keepdims=True) + jnp.sum(
        step_exp, axis=-1, keepdims=True
    )
    cache_probs = (cache_exp / denominator).astype(bf16)
    step_probs = (step_exp / denominator).astype(bf16)
    nn = (((1,), (0,)), ((), ()))
    mixed = lax.dot_general(cache_probs, values, nn, preferred_element_type=f32)
    mixed = mixed + lax.dot_general(step_probs, fresh_values, nn, preferred_element_type=f32)
    step, row, _ = place(HD)
    dead = jnp.zeros((count, HD), jnp.int32)
    for u in range(STEPS - 1):
        for r in range(2):
            ended = (ids_ref[r, u] == EOS).astype(jnp.int32)
            dead = dead + jnp.where((row == r) & (step > u), ended, 0)
    mixed = jnp.where(dead == 0, mixed, 0.0)
    flat = jnp.concatenate([mixed[h * ROWS : (h + 1) * ROWS] for h in range(4)], axis=1)
    out_ref[...] = jnp.concatenate([flat, jnp.zeros_like(flat)], axis=0).astype(bf16)


def attend(head, queries, cache_keys, cache_values, new_keys, new_values, lengths, ids):
    whole = lambda *shape: pl.BlockSpec(shape, lambda i, *_: (0,) * len(shape))
    cache = pl.BlockSpec((2, CACHE, HD), lambda i, m, *_: (0, m[0], 0))
    fresh = pl.BlockSpec((STEPS, 2, HD), lambda i, m, *_: (0, 0, m[0]))
    return pl.pallas_call(
        attend_kernel,
        out_shape=jax.ShapeDtypeStruct((PAD, FEAT), bf16),
        grid_spec=pltpu.PrefetchScalarGridSpec(
            num_scalar_prefetch=3,
            grid=(1,),
            in_specs=[whole(STEPS, 2, FEAT), cache, cache, fresh, fresh],
            out_specs=whole(PAD, FEAT),
            scratch_shapes=[
                pltpu.VMEM((ROWS, FEAT), f32),
                pltpu.VMEM((ROWS, HD), f32),
                pltpu.VMEM((ROWS, HD), f32),
            ],
        ),
        compiler_params=SMALL,
        name="attend",
    )(head, lengths, ids, queries, cache_keys, cache_values, new_keys, new_values)


VMEM = pl.BlockSpec(memory_space=pltpu.VMEM)
SMEM = pl.BlockSpec(memory_space=pltpu.SMEM)
HBM = pl.BlockSpec(memory_space=pl.ANY)


BIG = pltpu.CompilerParams(vmem_limit_bytes=60 * 2**20)


def cut_kernel(place_ref, cot_ref, out_ref, window, turned, sem):
    z_lo = place_ref[3]
    q = 2 * ((place_ref[1] - shift_of(z_lo, place_ref[4])) & 7) + (place_ref[2] ^ (z_lo & 1))
    start = pl.multiple_of(((q * 5) >> 1) * 128, 128)
    copy = pltpu.make_async_copy(cot_ref.at[:, pl.ds(start, 384)], window, sem)
    copy.start()
    copy.wait()
    turned[...] = window[...].astype(f32).T
    out_ref[...] = turned[pl.ds(pl.multiple_of((q & 1) * 64, 64), COLS), :].astype(bf16)


def cut_of(place, cot):
    return pl.pallas_call(
        cut_kernel,
        out_shape=jax.ShapeDtypeStruct((COLS, TOK), bf16),
        in_specs=[SMEM, HBM],
        out_specs=VMEM,
        scratch_shapes=[
            pltpu.VMEM((TOK, 384), bf16),
            pltpu.VMEM((384, TOK), f32),
            pltpu.SemaphoreType.DMA(()),
        ],
        compiler_params=BIG,
        name="cut",
    )(place, cot)


def base_kernel(place_ref, act_ref, act_got, rows_ref, rows_got, out_ref):
    @pl.when(place_ref[0] == 1)
    def _():
        out_ref[:TOK, :] = act_ref[...]
        out_ref[TOK:, :] = rows_ref[...]

    @pl.when(place_ref[0] == 0)
    def _():
        out_ref[:TOK, :] = act_got[...]
        out_ref[TOK:, :] = rows_got[...]


def base_of(place, *parts):
    return pl.pallas_call(
        base_kernel,
        out_shape=jax.ShapeDtypeStruct((TOK + PAD, FEAT), bf16),
        in_specs=[SMEM] + [VMEM] * 4,
        out_specs=VMEM,
        compiler_params=SMALL,
        name="base",
    )(place, *parts)


def gradient_kernel(place_ref, chunks_ref, *refs):
    blocks, (out_ref, chunk_rows, block_rows, row_tiles, sems) = refs[:4], refs[-5:]
    side, y, z_hi, own_z_lo, x = (place_ref[n] for n in range(5))
    token_zh = jnp.where(side == 1, z_hi, 1 - z_hi)
    act_copies = [
        pltpu.make_async_copy(
            chunks_ref.at[n, :TOK], chunk_rows.at[pl.ds(n * TOK, TOK)], sems.at[n]
        )
        for n in range(8)
    ]
    row_copies = [
        pltpu.make_async_copy(chunks_ref.at[n, TOK:], row_tiles.at[n], sems.at[16 + n])
        for n in range(8)
    ]
    for n in range(8):
        shift = ((n - y + 3) & 7) - 3
        slot = ((shift + 3) >> 2) ^ (own_z_lo >> 1)
        source = (shift + 3) - x
        source = jnp.where(side == 1, -source, source) & 3
        act_copies[n].start()
        for b in range(4):

            @pl.when(source == b)
            def _():
                pltpu.make_async_copy(
                    blocks[b].at[slot], block_rows.at[:, pl.ds(n * TOK, TOK)], sems.at[8 + n]
                ).start()

        row_copies[n].start()
    out_ref[COLS:, :] = jnp.zeros((16 * ROWS, FEAT), f32)
    for half in range(2):
        for n in range(4 * half, 4 * half + 4):
            act_copies[n].wait()
            pltpu.make_async_copy(
                blocks[0].at[0], block_rows.at[:, pl.ds(n * TOK, TOK)], sems.at[8 + n]
            ).wait()
        span = pl.ds(half * 4 * TOK, 4 * TOK)
        part = jnp.dot(block_rows[:, span], chunk_rows[span, :], preferred_element_type=f32)
        if half == 0:
            out_ref[:COLS, :] = part
        else:
            out_ref[:COLS, :] += part
    for n in range(8):
        row_copies[n].wait()
        place = pl.multiple_of(COLS + (2 * n + token_zh) * ROWS, ROWS)
        out_ref[pl.ds(place, ROWS), :] = row_tiles[n].astype(f32)[:ROWS]


def gradient(place, chunks, blocks, others):
    operands = (chunks, *blocks, *others)
    return pl.pallas_call(
        gradient_kernel,
        out_shape=jax.ShapeDtypeStruct((COLS + 16 * ROWS, FEAT), f32),
        in_specs=[SMEM] + [HBM] * len(operands),
        out_specs=VMEM,
        scratch_shapes=[
            pltpu.VMEM((8 * TOK, FEAT), bf16),
            pltpu.VMEM((COLS, 8 * TOK), bf16),
            pltpu.VMEM((8, PAD, FEAT), bf16),
            pltpu.SemaphoreType.DMA((24,)),
        ],
        compiler_params=BIG,
        name="gradient",
    )(place, *operands)


def step_kernel(
    place_ref, mine_ref, got_ref, one_ref, one_got, two_ref, two_got, weight_ref, update_ref, out_ref
):
    learner = place_ref[0] == 1
    grad = mine_ref[:COLS, :] + got_ref[:COLS, :]
    moment_one = jnp.where(learner, one_ref[...], one_got[...])
    moment_two = jnp.where(learner, two_ref[...], two_got[...])
    first_moment = beta_one * moment_one + (1.0 - beta_one) * grad
    second_moment = beta_two * moment_two + (1.0 - beta_two) * grad * grad
    update = (
        first_moment / first_bias / (jnp.sqrt(second_moment / second_bias) + epsilon)
    ).astype(bf16)
    update_ref[...] = update
    widened = weight_ref[...].astype(f32)
    renewed = (
        widened - learning_rate * (update.astype(f32) + weight_decay * widened)
    ).astype(bf16)
    rows = (mine_ref[COLS:, :] + got_ref[COLS:, :]).astype(bf16)
    part = lax.dot_general(rows, renewed, (((1,), (1,)), ((), ())), preferred_element_type=f32)
    out_ref[...] = part.reshape(16, ROWS, COLS)


def step(place, mine, got, one, one_got, two, two_got, weight):
    return pl.pallas_call(
        step_kernel,
        out_shape=(
            jax.ShapeDtypeStruct((COLS, FEAT), bf16),
            jax.ShapeDtypeStruct((16, ROWS, COLS), f32),
        ),
        in_specs=[SMEM] + [VMEM] * 7,
        out_specs=(VMEM, VMEM),
        compiler_params=pltpu.CompilerParams(vmem_limit_bytes=16 * 2**20),
        name="step",
    )(place, mine, got, one, one_got, two, two_got, weight)


def local(
    activations,
    cotangent,
    weight,
    moment_one,
    moment_two,
    queries,
    cache_keys,
    cache_values,
    new_keys,
    new_values,
    lengths,
    token_ids,
):
    q = lax.axis_index(TENSOR)
    place = jnp.stack([lax.axis_index(axis) for axis in AXES]).astype(jnp.int32)

    act = activations[0]
    act_got = permute(act, to_partner)
    cut = cut_of(place, cotangent[0])
    own = permute(cut, cot_shifted)
    rows = attend(
        (q >> 1).reshape(1),
        queries,
        cache_keys,
        cache_values,
        new_keys,
        new_values,
        lengths,
        token_ids.T,
    )
    rows_got = permute(rows, to_partner)
    base = base_of(place, act, act_got, rows, rows_got)
    chunks = lax.all_gather(base, "y", axis=0)

    one, two = moment_one[0].T, moment_two[0].T
    one_tied, two_tied, own, _ = lax.optimization_barrier((one, two, own, base))
    pair = jnp.stack([own, permute(own, along_zl(2))])
    pair_got = permute(pair, along_zl(1))
    pair = jnp.where(place[0] == keeper(place[3]), pair, pair_got)
    blocks = [pair] + [permute(pair, along_x(step)) for step in (1, 2, -1)]
    one_got = permute(one_tied, to_rollout)
    two_got = permute(two_tied, to_rollout)

    mine = gradient(place, chunks, blocks, (one_got, two_got))
    got = permute(mine, other_core)
    update, partial = step(place, mine, got, one, one_got, two, two_got, weight.T)

    shares = gather(partial, TENSOR)
    summed = jnp.sum(shares, axis=0).astype(bf16)
    block = permute(summed, transposed)
    spread = jnp.broadcast_to(block[None], (16, ROWS, COLS))
    gathered = gather(spread, TENSOR)
    decoded = gathered.transpose(1, 0, 2).reshape(STEPS, ROWS // STEPS, D)
    return (update.T, decoded)


def solution(mesh):
    fine = Mesh(mesh.devices.reshape(SHAPE), AXES)
    return jax.shard_map(
        local,
        mesh=fine,
        in_specs=(
            P("group", DP, TENSOR),
            P("group", DP, None),
            P(TENSOR, DP),
            P("group", TENSOR, DP),
            P("group", TENSOR, DP),
            P(None, DP, TENSOR),
            P(DP, None, None),
            P(DP, None, None),
            P(None, DP, None),
            P(None, DP, None),
            P(DP),
            P(None, DP),
        ),
        out_specs=(P(TENSOR, DP), P(None, DP, None)),
        check_vma=False,
    )
```

```python
import math

import jax
import jax.numpy as jnp
import numpy as np
from jax import lax
from jax.experimental import pallas as pl
from jax.experimental.pallas import tpu as pltpu
from jax.sharding import Mesh
from jax.sharding import PartitionSpec as P

D = 5120
KVH = 8
HD = 128
EOS = 151645
STEPS = 4
CACHE = 256

learning_rate = 0.0003
weight_decay = 0.1
beta_one = 0.9
beta_two = 0.95
first_bias = 1.0 - 0.9**10
second_bias = 1.0 - 0.95**10
epsilon = 1e-08

AXES = ("group", "y", "z_hi", "z_lo", "x")
SHAPE = (2, 8, 2, 4, 4)
DP, TENSOR = ("y", "z_hi"), ("z_lo", "x")
TOK = 256
FEAT = 512
COLS = 320
ROWS = 8
PAD = 16
f32, bf16 = jnp.float32, jnp.bfloat16


def permute(value, target):
    pairs = []
    for flat, place in enumerate(np.ndindex(*SHAPE)):
        to = target(*place)
        if to is not None:
            pairs.append((flat, int(np.ravel_multi_index(to, SHAPE))))
    return lax.ppermute(value, AXES, pairs)


def gather(value, axes):
    return lax.all_to_all(value, axes, split_axis=0, concat_axis=0, tiled=True)


def to_partner(g, y, zh, zl, x):
    return (0, y, 1 - zh, zl, x) if g == 1 else None


def keeper(zl):
    return 1 - (zl & 1)


def shift_of(z_lo, x):
    return 4 * (z_lo >> 1) + x - 3


def cot_shifted(g, y, zh, zl, x):
    to = (keeper(zl), (y - shift_of(zl, x)) % 8, zh ^ (zl & 1), zl, x)
    return to if g == 1 else None


def along_zl(flip):
    return lambda g, y, zh, zl, x: (g, y, zh, zl ^ flip, x) if g == keeper(zl) else None


def along_x(step):
    return lambda g, y, zh, zl, x: (g, y, zh, zl, (x + (step if g == 1 else -step)) % 4)


def transposed(g, y, zh, zl, x):
    return (g, zl * 2 + (x >> 1), x & 1, y >> 1, (y & 1) * 2 + zh)


def other_core(g, y, zh, zl, x):
    return (1 - g, y, zh, zl, x)


def to_rollout(g, y, zh, zl, x):
    return (0, y, zh, zl, x) if g == 1 else None


SMALL = pltpu.CompilerParams(vmem_limit_bytes=6 * 2**20)


def attend_kernel(
    head_ref, lengths_ref, ids_ref, q_ref, k_ref, v_ref, nk_ref, nv_ref, out_ref, q_rows, nk_rows, nv_rows
):
    for t in range(STEPS):
        place = slice(2 * t, 2 * t + 2)
        q_rows[place, :] = q_ref[t].astype(f32)
        nk_rows[place, :] = nk_ref[t].astype(f32)
        nv_rows[place, :] = nv_ref[t].astype(f32)
    queries = q_rows[...]
    query = jnp.concatenate(
        [queries[:, h * HD : (h + 1) * HD] for h in range(4)], axis=0
    ).astype(bf16)
    keys = k_ref[...].reshape(2 * CACHE, HD)
    values = v_ref[...].reshape(2 * CACHE, HD)
    fresh_keys = nk_rows[...].astype(bf16)
    fresh_values = nv_rows[...].astype(bf16)
    scale = 1.0 / math.sqrt(HD)
    nt = (((1,), (1,)), ((), ()))
    cache_scores = lax.dot_general(query, keys, nt, preferred_element_type=f32) * scale
    step_scores = lax.dot_general(query, fresh_keys, nt, preferred_element_type=f32) * scale
    count = 4 * ROWS

    def place(width):
        place_row = lax.broadcasted_iota(jnp.int32, (count, width), 0) & (ROWS - 1)
        place_key = lax.broadcasted_iota(jnp.int32, (count, width), 1)
        return place_row >> 1, place_row & 1, place_key

    step, row, key = place(2 * CACHE)
    length = jnp.where(row == 0, lengths_ref[0], lengths_ref[1])
    cache_valid = ((key >> 8) == row) & ((key & (CACHE - 1)) < length)
    step, row, key = place(ROWS)
    step_valid = ((key & 1) == row) & ((key >> 1) <= step)
    cache_scores = jnp.where(cache_valid, cache_scores, -jnp.inf)
    step_scores = jnp.where(step_valid, step_scores, -jnp.inf)
    peak = jnp.maximum(
        jnp.max(cache_scores, axis=-1, keepdims=True), jnp.max(step_scores, axis=-1, keepdims=True)
    )
    cache_exp = jnp.exp(cache_scores - peak)
    step_exp = jnp.exp(step_scores - peak)
    denominator = jnp.sum(cache_exp, axis=-1, keepdims=True) + jnp.sum(
        step_exp, axis=-1, keepdims=True
    )
    cache_probs = (cache_exp / denominator).astype(bf16)
    step_probs = (step_exp / denominator).astype(bf16)
    nn = (((1,), (0,)), ((), ()))
    mixed = lax.dot_general(cache_probs, values, nn, preferred_element_type=f32)
    mixed = mixed + lax.dot_general(step_probs, fresh_values, nn, preferred_element_type=f32)
    step, row, _ = place(HD)
    dead = jnp.zeros((count, HD), jnp.int32)
    for u in range(STEPS - 1):
        for r in range(2):
            ended = (ids_ref[r, u] == EOS).astype(jnp.int32)
            dead = dead + jnp.where((row == r) & (step > u), ended, 0)
    mixed = jnp.where(dead == 0, mixed, 0.0)
    flat = jnp.concatenate([mixed[h * ROWS : (h + 1) * ROWS] for h in range(4)], axis=1)
    out_ref[...] = jnp.concatenate([flat, jnp.zeros_like(flat)], axis=0).astype(bf16)


def attend(head, queries, cache_keys, cache_values, new_keys, new_values, lengths, ids):
    whole = lambda *shape: pl.BlockSpec(shape, lambda i, *_: (0,) * len(shape))
    cache = pl.BlockSpec((2, CACHE, HD), lambda i, m, *_: (0, m[0], 0))
    fresh = pl.BlockSpec((STEPS, 2, HD), lambda i, m, *_: (0, 0, m[0]))
    return pl.pallas_call(
        attend_kernel,
        out_shape=jax.ShapeDtypeStruct((PAD, FEAT), bf16),
        grid_spec=pltpu.PrefetchScalarGridSpec(
            num_scalar_prefetch=3,
            grid=(1,),
            in_specs=[whole(STEPS, 2, FEAT), cache, cache, fresh, fresh],
            out_specs=whole(PAD, FEAT),
            scratch_shapes=[
                pltpu.VMEM((ROWS, FEAT), f32),
                pltpu.VMEM((ROWS, HD), f32),
                pltpu.VMEM((ROWS, HD), f32),
            ],
        ),
        compiler_params=SMALL,
        name="attend",
    )(head, lengths, ids, queries, cache_keys, cache_values, new_keys, new_values)


VMEM = pl.BlockSpec(memory_space=pltpu.VMEM)
SMEM = pl.BlockSpec(memory_space=pltpu.SMEM)
HBM = pl.BlockSpec(memory_space=pl.ANY)


def cut_kernel(place_ref, cot_ref, out_ref, window, turned, sem):
    z_lo = place_ref[3]
    q = 2 * ((place_ref[1] - shift_of(z_lo, place_ref[4])) & 7) + (place_ref[2] ^ (z_lo & 1))
    start = pl.multiple_of(((q * 5) >> 1) * 128, 128)
    copy = pltpu.make_async_copy(cot_ref.at[:, pl.ds(start, 384)], window, sem)
    copy.start()
    copy.wait()
    turned[...] = window[...].astype(f32).T
    out_ref[...] = turned[pl.ds(pl.multiple_of((q & 1) * 64, 64), COLS), :].astype(bf16)


def cut_of(place, cot):
    return pl.pallas_call(
        cut_kernel,
        out_shape=jax.ShapeDtypeStruct((COLS, TOK), bf16),
        in_specs=[SMEM, HBM],
        out_specs=VMEM,
        scratch_shapes=[
            pltpu.VMEM((TOK, 384), bf16),
            pltpu.VMEM((384, TOK), f32),
            pltpu.SemaphoreType.DMA(()),
        ],
        compiler_params=SMALL,
        name="cut",
    )(place, cot)


def base_kernel(place_ref, act_ref, act_got, rows_ref, rows_got, _, out_ref):
    @pl.when(place_ref[0] == 1)
    def _():
        out_ref[:TOK, :] = act_ref[...]
        out_ref[TOK:, :] = rows_ref[...]

    @pl.when(place_ref[0] == 0)
    def _():
        out_ref[:TOK, :] = act_got[...]
        out_ref[TOK:, :] = rows_got[...]


def base_of(place, *parts):
    return pl.pallas_call(
        base_kernel,
        out_shape=jax.ShapeDtypeStruct((TOK + PAD, FEAT), bf16),
        in_specs=[SMEM] + [VMEM] * 4 + [HBM],
        out_specs=VMEM,
        compiler_params=SMALL,
        name="base",
    )(place, *parts)


def gradient_kernel(place_ref, chunks_ref, *refs):
    blocks, (out_ref, chunk_rows, block_rows, row_tiles, sems) = refs[:4], refs[-5:]
    side, y, z_hi, own_z_lo, x = (place_ref[n] for n in range(5))
    token_zh = jnp.where(side == 1, z_hi, 1 - z_hi)
    act_copies = [
        pltpu.make_async_copy(
            chunks_ref.at[n, :TOK], chunk_rows.at[pl.ds(n * TOK, TOK)], sems.at[n]
        )
        for n in range(8)
    ]
    row_copies = [
        pltpu.make_async_copy(chunks_ref.at[n, TOK:], row_tiles.at[n], sems.at[16 + n])
        for n in range(8)
    ]
    for n in range(8):
        shift = ((n - y + 3) & 7) - 3
        slot = ((shift + 3) >> 2) ^ (own_z_lo >> 1)
        source = (shift + 3) - x
        source = jnp.where(side == 1, -source, source) & 3
        act_copies[n].start()
        for b in range(4):

            @pl.when(source == b)
            def _():
                pltpu.make_async_copy(
                    blocks[b].at[slot], block_rows.at[:, pl.ds(n * TOK, TOK)], sems.at[8 + n]
                ).start()

        row_copies[n].start()
    out_ref[COLS:, :] = jnp.zeros((16 * ROWS, FEAT), f32)
    for half in range(2):
        for n in range(4 * half, 4 * half + 4):
            act_copies[n].wait()
            pltpu.make_async_copy(
                blocks[0].at[0], block_rows.at[:, pl.ds(n * TOK, TOK)], sems.at[8 + n]
            ).wait()
        span = pl.ds(half * 4 * TOK, 4 * TOK)
        part = jnp.dot(block_rows[:, span], chunk_rows[span, :], preferred_element_type=f32)
        if half == 0:
            out_ref[:COLS, :] = part
        else:
            out_ref[:COLS, :] += part
    for n in range(8):
        row_copies[n].wait()
        place = pl.multiple_of(COLS + (2 * n + token_zh) * ROWS, ROWS)
        out_ref[pl.ds(place, ROWS), :] = row_tiles[n].astype(f32)[:ROWS]


def gradient(place, chunks, blocks, others):
    operands = (chunks, *blocks, *others)
    return pl.pallas_call(
        gradient_kernel,
        out_shape=jax.ShapeDtypeStruct((COLS + 16 * ROWS, FEAT), f32),
        in_specs=[SMEM] + [HBM] * len(operands),
        out_specs=VMEM,
        scratch_shapes=[
            pltpu.VMEM((8 * TOK, FEAT), bf16),
            pltpu.VMEM((COLS, 8 * TOK), bf16),
            pltpu.VMEM((8, PAD, FEAT), bf16),
            pltpu.SemaphoreType.DMA((24,)),
        ],
        compiler_params=pltpu.CompilerParams(vmem_limit_bytes=16 * 2**20),
        name="gradient",
    )(place, *operands)


def step_kernel(
    place_ref, mine_ref, got_ref, one_ref, one_got, two_ref, two_got, weight_ref, update_ref, out_ref
):
    learner = place_ref[0] == 1
    grad = mine_ref[:COLS, :] + got_ref[:COLS, :]
    moment_one = jnp.where(learner, one_ref[...], one_got[...])
    moment_two = jnp.where(learner, two_ref[...], two_got[...])
    first_moment = beta_one * moment_one + (1.0 - beta_one) * grad
    second_moment = beta_two * moment_two + (1.0 - beta_two) * grad * grad
    update = (
        first_moment / first_bias / (jnp.sqrt(second_moment / second_bias) + epsilon)
    ).astype(bf16)
    update_ref[...] = update
    widened = weight_ref[...].astype(f32)
    renewed = (
        widened - learning_rate * (update.astype(f32) + weight_decay * widened)
    ).astype(bf16)
    rows = (mine_ref[COLS:, :] + got_ref[COLS:, :]).astype(bf16)
    part = lax.dot_general(rows, renewed, (((1,), (1,)), ((), ())), preferred_element_type=f32)
    out_ref[...] = part.reshape(16, ROWS, COLS)


def step(place, mine, got, one, one_got, two, two_got, weight):
    return pl.pallas_call(
        step_kernel,
        out_shape=(
            jax.ShapeDtypeStruct((COLS, FEAT), bf16),
            jax.ShapeDtypeStruct((16, ROWS, COLS), f32),
        ),
        in_specs=[SMEM] + [VMEM] * 7,
        out_specs=(VMEM, VMEM),
        compiler_params=pltpu.CompilerParams(vmem_limit_bytes=16 * 2**20),
        name="step",
    )(place, mine, got, one, one_got, two, two_got, weight)


def local(
    activations,
    cotangent,
    weight,
    moment_one,
    moment_two,
    queries,
    cache_keys,
    cache_values,
    new_keys,
    new_values,
    lengths,
    token_ids,
):
    q = lax.axis_index(TENSOR)
    place = jnp.stack([lax.axis_index(axis) for axis in AXES]).astype(jnp.int32)

    act = activations[0]
    act_got = permute(act, to_partner)
    cut = cut_of(place, cotangent[0])
    own = permute(cut, cot_shifted)
    rows = attend(
        (q >> 1).reshape(1),
        queries,
        cache_keys,
        cache_values,
        new_keys,
        new_values,
        lengths,
        token_ids.T,
    )
    rows_got = permute(rows, to_partner)
    base = base_of(place, act, act_got, rows, rows_got, own)
    chunks = lax.all_gather(base, "y", axis=0)

    one, two = moment_one[0].T, moment_two[0].T
    own, _ = lax.optimization_barrier((own, base))
    pair = jnp.stack([own, permute(own, along_zl(2))])
    pair_got = permute(pair, along_zl(1))
    pair = jnp.where(place[0] == keeper(place[3]), pair, pair_got)
    blocks = [pair] + [permute(pair, along_x(step)) for step in (1, 2, -1)]
    one_tied, two_tied, blocks[1] = lax.optimization_barrier((one, two, blocks[1]))
    one_got = permute(one_tied, to_rollout)
    two_got = permute(two_tied, to_rollout)

    mine = gradient(place, chunks, blocks, (one_got, two_got))
    got = permute(mine, other_core)
    update, partial = step(place, mine, got, one, one_got, two, two_got, weight.T)

    shares = gather(partial, TENSOR)
    summed = jnp.sum(shares, axis=0).astype(bf16)
    block = permute(summed, transposed)
    spread = jnp.broadcast_to(block[None], (16, ROWS, COLS))
    gathered = gather(spread, TENSOR)
    decoded = gathered.transpose(1, 0, 2).reshape(STEPS, ROWS // STEPS, D)
    return (update.T, decoded)


def solution(mesh):
    fine = Mesh(mesh.devices.reshape(SHAPE), AXES)
    return jax.shard_map(
        local,
        mesh=fine,
        in_specs=(
            P("group", DP, TENSOR),
            P("group", DP, None),
            P(TENSOR, DP),
            P("group", TENSOR, DP),
            P("group", TENSOR, DP),
            P(None, DP, TENSOR),
            P(DP, None, None),
            P(DP, None, None),
            P(None, DP, None),
            P(None, DP, None),
            P(DP),
            P(None, DP),
        ),
        out_specs=(P(TENSOR, DP), P(None, DP, None)),
        check_vma=False,
    )
```

```python
import math

import jax
import jax.numpy as jnp
import numpy as np
from jax import lax
from jax.experimental import pallas as pl
from jax.experimental.pallas import tpu as pltpu
from jax.sharding import Mesh
from jax.sharding import PartitionSpec as P

D = 5120
KVH = 8
HD = 128
EOS = 151645
STEPS = 4
CACHE = 256

learning_rate = 0.0003
weight_decay = 0.1
beta_one = 0.9
beta_two = 0.95
first_bias = 1.0 - 0.9**10
second_bias = 1.0 - 0.95**10
epsilon = 1e-08

AXES = ("group", "y", "z_hi", "z_lo", "x")
SHAPE = (2, 8, 2, 4, 4)
DP, TENSOR = ("y", "z_hi"), ("z_lo", "x")
TOK = 256
FEAT = 512
COLS = 320
ROWS = 8
PAD = 16
f32, bf16 = jnp.float32, jnp.bfloat16


def permute(value, target):
    pairs = []
    for flat, place in enumerate(np.ndindex(*SHAPE)):
        to = target(*place)
        if to is not None:
            pairs.append((flat, int(np.ravel_multi_index(to, SHAPE))))
    return lax.ppermute(value, AXES, pairs)


def gather(value, axes):
    return lax.all_to_all(value, axes, split_axis=0, concat_axis=0, tiled=True)


def to_partner(g, y, zh, zl, x):
    return (0, y, 1 - zh, zl, x) if g == 1 else None


def keeper(zl):
    return 1 - (zl & 1)


def shift_of(z_lo, x):
    return 4 * (z_lo >> 1) + x - 3


def cot_shifted(g, y, zh, zl, x):
    to = (keeper(zl), (y - shift_of(zl, x)) % 8, zh ^ (zl & 1), zl, x)
    return to if g == 1 else None


def along_zl(flip):
    return lambda g, y, zh, zl, x: (g, y, zh, zl ^ flip, x) if g == keeper(zl) else None


def along_x(step):
    return lambda g, y, zh, zl, x: (g, y, zh, zl, (x + (step if g == 1 else -step)) % 4)


def transposed(g, y, zh, zl, x):
    return (g, zl * 2 + (x >> 1), x & 1, y >> 1, (y & 1) * 2 + zh)


def other_core(g, y, zh, zl, x):
    return (1 - g, y, zh, zl, x)


def to_rollout(g, y, zh, zl, x):
    return (0, y, zh, zl, x) if g == 1 else None


SMALL = pltpu.CompilerParams(vmem_limit_bytes=6 * 2**20)


def attend_kernel(
    head_ref, lengths_ref, ids_ref, q_ref, k_ref, v_ref, nk_ref, nv_ref, out_ref, q_rows, nk_rows, nv_rows
):
    for t in range(STEPS):
        place = slice(2 * t, 2 * t + 2)
        q_rows[place, :] = q_ref[t].astype(f32)
        nk_rows[place, :] = nk_ref[t].astype(f32)
        nv_rows[place, :] = nv_ref[t].astype(f32)
    queries = q_rows[...]
    query = jnp.concatenate(
        [queries[:, h * HD : (h + 1) * HD] for h in range(4)], axis=0
    ).astype(bf16)
    keys = k_ref[...].reshape(2 * CACHE, HD)
    values = v_ref[...].reshape(2 * CACHE, HD)
    fresh_keys = nk_rows[...].astype(bf16)
    fresh_values = nv_rows[...].astype(bf16)
    scale = 1.0 / math.sqrt(HD)
    nt = (((1,), (1,)), ((), ()))
    cache_scores = lax.dot_general(query, keys, nt, preferred_element_type=f32) * scale
    step_scores = lax.dot_general(query, fresh_keys, nt, preferred_element_type=f32) * scale
    count = 4 * ROWS

    def place(width):
        place_row = lax.broadcasted_iota(jnp.int32, (count, width), 0) & (ROWS - 1)
        place_key = lax.broadcasted_iota(jnp.int32, (count, width), 1)
        return place_row >> 1, place_row & 1, place_key

    step, row, key = place(2 * CACHE)
    length = jnp.where(row == 0, lengths_ref[0], lengths_ref[1])
    cache_valid = ((key >> 8) == row) & ((key & (CACHE - 1)) < length)
    step, row, key = place(ROWS)
    step_valid = ((key & 1) == row) & ((key >> 1) <= step)
    cache_scores = jnp.where(cache_valid, cache_scores, -jnp.inf)
    step_scores = jnp.where(step_valid, step_scores, -jnp.inf)
    peak = jnp.maximum(
        jnp.max(cache_scores, axis=-1, keepdims=True), jnp.max(step_scores, axis=-1, keepdims=True)
    )
    cache_exp = jnp.exp(cache_scores - peak)
    step_exp = jnp.exp(step_scores - peak)
    denominator = jnp.sum(cache_exp, axis=-1, keepdims=True) + jnp.sum(
        step_exp, axis=-1, keepdims=True
    )
    cache_probs = (cache_exp / denominator).astype(bf16)
    step_probs = (step_exp / denominator).astype(bf16)
    nn = (((1,), (0,)), ((), ()))
    mixed = lax.dot_general(cache_probs, values, nn, preferred_element_type=f32)
    mixed = mixed + lax.dot_general(step_probs, fresh_values, nn, preferred_element_type=f32)
    step, row, _ = place(HD)
    dead = jnp.zeros((count, HD), jnp.int32)
    for u in range(STEPS - 1):
        for r in range(2):
            ended = (ids_ref[r, u] == EOS).astype(jnp.int32)
            dead = dead + jnp.where((row == r) & (step > u), ended, 0)
    mixed = jnp.where(dead == 0, mixed, 0.0)
    flat = jnp.concatenate([mixed[h * ROWS : (h + 1) * ROWS] for h in range(4)], axis=1)
    out_ref[...] = jnp.concatenate([flat, jnp.zeros_like(flat)], axis=0).astype(bf16)


def attend(head, queries, cache_keys, cache_values, new_keys, new_values, lengths, ids):
    whole = lambda *shape: pl.BlockSpec(shape, lambda i, *_: (0,) * len(shape))
    cache = pl.BlockSpec((2, CACHE, HD), lambda i, m, *_: (0, m[0], 0))
    fresh = pl.BlockSpec((STEPS, 2, HD), lambda i, m, *_: (0, 0, m[0]))
    return pl.pallas_call(
        attend_kernel,
        out_shape=jax.ShapeDtypeStruct((PAD, FEAT), bf16),
        grid_spec=pltpu.PrefetchScalarGridSpec(
            num_scalar_prefetch=3,
            grid=(1,),
            in_specs=[whole(STEPS, 2, FEAT), cache, cache, fresh, fresh],
            out_specs=whole(PAD, FEAT),
            scratch_shapes=[
                pltpu.VMEM((ROWS, FEAT), f32),
                pltpu.VMEM((ROWS, HD), f32),
                pltpu.VMEM((ROWS, HD), f32),
            ],
        ),
        compiler_params=SMALL,
        name="attend",
    )(head, lengths, ids, queries, cache_keys, cache_values, new_keys, new_values)


VMEM = pl.BlockSpec(memory_space=pltpu.VMEM)
SMEM = pl.BlockSpec(memory_space=pltpu.SMEM)
HBM = pl.BlockSpec(memory_space=pl.ANY)


def cut_kernel(place_ref, cot_ref, out_ref, window, turned, sem):
    z_lo = place_ref[3]
    q = 2 * ((place_ref[1] - shift_of(z_lo, place_ref[4])) & 7) + (place_ref[2] ^ (z_lo & 1))
    start = pl.multiple_of(((q * 5) >> 1) * 128, 128)
    copy = pltpu.make_async_copy(cot_ref.at[:, pl.ds(start, 384)], window, sem)
    copy.start()
    copy.wait()
    turned[...] = window[...].astype(f32).T
    out_ref[...] = turned[pl.ds(pl.multiple_of((q & 1) * 64, 64), COLS), :].astype(bf16)


def cut_of(place, cot):
    return pl.pallas_call(
        cut_kernel,
        out_shape=jax.ShapeDtypeStruct((COLS, TOK), bf16),
        in_specs=[SMEM, HBM],
        out_specs=VMEM,
        scratch_shapes=[
            pltpu.VMEM((TOK, 384), bf16),
            pltpu.VMEM((384, TOK), f32),
            pltpu.SemaphoreType.DMA(()),
        ],
        compiler_params=SMALL,
        name="cut",
    )(place, cot)


def base_kernel(place_ref, act_ref, act_got, rows_ref, rows_got, _, out_ref):
    @pl.when(place_ref[0] == 1)
    def _():
        out_ref[:TOK, :] = act_ref[...]
        out_ref[TOK:, :] = rows_ref[...]

    @pl.when(place_ref[0] == 0)
    def _():
        out_ref[:TOK, :] = act_got[...]
        out_ref[TOK:, :] = rows_got[...]


def base_of(place, *parts):
    return pl.pallas_call(
        base_kernel,
        out_shape=jax.ShapeDtypeStruct((TOK + PAD, FEAT), bf16),
        in_specs=[SMEM] + [VMEM] * 4 + [HBM],
        out_specs=VMEM,
        compiler_params=SMALL,
        name="base",
    )(place, *parts)


def gradient_kernel(place_ref, chunks_ref, *refs):
    blocks, (out_ref, chunk_rows, block_rows, row_tiles, sems) = refs[:4], refs[-5:]
    side, y, z_hi, own_z_lo, x = (place_ref[n] for n in range(5))
    token_zh = jnp.where(side == 1, z_hi, 1 - z_hi)
    act_copies = [
        pltpu.make_async_copy(
            chunks_ref.at[n, :TOK], chunk_rows.at[pl.ds(n * TOK, TOK)], sems.at[n]
        )
        for n in range(8)
    ]
    row_copies = [
        pltpu.make_async_copy(chunks_ref.at[n, TOK:], row_tiles.at[n], sems.at[16 + n])
        for n in range(8)
    ]
    for n in range(8):
        shift = ((n - y + 3) & 7) - 3
        slot = ((shift + 3) >> 2) ^ (own_z_lo >> 1)
        source = (shift + 3) - x
        source = jnp.where(side == 1, -source, source) & 3
        act_copies[n].start()
        for b in range(4):

            @pl.when(source == b)
            def _():
                pltpu.make_async_copy(
                    blocks[b].at[slot], block_rows.at[:, pl.ds(n * TOK, TOK)], sems.at[8 + n]
                ).start()

        row_copies[n].start()
    out_ref[COLS:, :] = jnp.zeros((16 * ROWS, FEAT), f32)
    for half in range(2):
        for n in range(4 * half, 4 * half + 4):
            act_copies[n].wait()
            pltpu.make_async_copy(
                blocks[0].at[0], block_rows.at[:, pl.ds(n * TOK, TOK)], sems.at[8 + n]
            ).wait()
        span = pl.ds(half * 4 * TOK, 4 * TOK)
        part = jnp.dot(block_rows[:, span], chunk_rows[span, :], preferred_element_type=f32)
        if half == 0:
            out_ref[:COLS, :] = part
        else:
            out_ref[:COLS, :] += part
    for n in range(8):
        row_copies[n].wait()
        place = pl.multiple_of(COLS + (2 * n + token_zh) * ROWS, ROWS)
        out_ref[pl.ds(place, ROWS), :] = row_tiles[n].astype(f32)[:ROWS]


def gradient(place, chunks, blocks, others):
    operands = (chunks, *blocks, *others)
    return pl.pallas_call(
        gradient_kernel,
        out_shape=jax.ShapeDtypeStruct((COLS + 16 * ROWS, FEAT), f32),
        in_specs=[SMEM] + [HBM] * len(operands),
        out_specs=VMEM,
        scratch_shapes=[
            pltpu.VMEM((8 * TOK, FEAT), bf16),
            pltpu.VMEM((COLS, 8 * TOK), bf16),
            pltpu.VMEM((8, PAD, FEAT), bf16),
            pltpu.SemaphoreType.DMA((24,)),
        ],
        compiler_params=pltpu.CompilerParams(vmem_limit_bytes=16 * 2**20),
        name="gradient",
    )(place, *operands)


def step_kernel(
    place_ref, mine_ref, got_ref, one_ref, one_got, two_ref, two_got, weight_ref, update_ref, out_ref
):
    learner = place_ref[0] == 1
    grad = mine_ref[:COLS, :] + got_ref[:COLS, :]
    moment_one = jnp.where(learner, one_ref[...], one_got[...])
    moment_two = jnp.where(learner, two_ref[...], two_got[...])
    first_moment = beta_one * moment_one + (1.0 - beta_one) * grad
    second_moment = beta_two * moment_two + (1.0 - beta_two) * grad * grad
    update = (
        first_moment / first_bias / (jnp.sqrt(second_moment / second_bias) + epsilon)
    ).astype(bf16)
    update_ref[...] = update
    widened = weight_ref[...].astype(f32)
    renewed = (
        widened - learning_rate * (update.astype(f32) + weight_decay * widened)
    ).astype(bf16)
    rows = (mine_ref[COLS:, :] + got_ref[COLS:, :]).astype(bf16)
    part = lax.dot_general(rows, renewed, (((1,), (1,)), ((), ())), preferred_element_type=f32)
    out_ref[...] = part.reshape(16, ROWS, COLS)


def step(place, mine, got, one, one_got, two, two_got, weight):
    return pl.pallas_call(
        step_kernel,
        out_shape=(
            jax.ShapeDtypeStruct((COLS, FEAT), bf16),
            jax.ShapeDtypeStruct((16, ROWS, COLS), f32),
        ),
        in_specs=[SMEM] + [VMEM] * 7,
        out_specs=(VMEM, VMEM),
        compiler_params=pltpu.CompilerParams(vmem_limit_bytes=16 * 2**20),
        name="step",
    )(place, mine, got, one, one_got, two, two_got, weight)


def local(
    activations,
    cotangent,
    weight,
    moment_one,
    moment_two,
    queries,
    cache_keys,
    cache_values,
    new_keys,
    new_values,
    lengths,
    token_ids,
):
    q = lax.axis_index(TENSOR)
    place = jnp.stack([lax.axis_index(axis) for axis in AXES]).astype(jnp.int32)

    act = activations[0]
    act_got = permute(act, to_partner)
    cut = cut_of(place, cotangent[0])
    own = permute(cut, cot_shifted)
    rows = attend(
        (q >> 1).reshape(1),
        queries,
        cache_keys,
        cache_values,
        new_keys,
        new_values,
        lengths,
        token_ids.T,
    )
    rows_got = permute(rows, to_partner)
    base = base_of(place, act, act_got, rows, rows_got, own)
    chunks = lax.all_gather(base, "y", axis=0)

    one, two = moment_one[0].T, moment_two[0].T
    own, _ = lax.optimization_barrier((own, base))
    pair = jnp.stack([own, permute(own, along_zl(2))])
    pair_got = permute(pair, along_zl(1))
    pair = jnp.where(place[0] == keeper(place[3]), pair, pair_got)
    blocks = [pair] + [permute(pair, along_x(step)) for step in (1, 2, -1)]
    one_tied, two_tied, _ = lax.optimization_barrier((one, two, base))
    one_got = permute(one_tied, to_rollout)
    two_got = permute(two_tied, to_rollout)

    mine = gradient(place, chunks, blocks, (one_got, two_got))
    got = permute(mine, other_core)
    update, partial = step(place, mine, got, one, one_got, two, two_got, weight.T)

    shares = gather(partial, TENSOR)
    summed = jnp.sum(shares, axis=0).astype(bf16)
    block = permute(summed, transposed)
    spread = jnp.broadcast_to(block[None], (16, ROWS, COLS))
    gathered = gather(spread, TENSOR)
    decoded = gathered.transpose(1, 0, 2).reshape(STEPS, ROWS // STEPS, D)
    return (update.T, decoded)


def solution(mesh):
    fine = Mesh(mesh.devices.reshape(SHAPE), AXES)
    return jax.shard_map(
        local,
        mesh=fine,
        in_specs=(
            P("group", DP, TENSOR),
            P("group", DP, None),
            P(TENSOR, DP),
            P("group", TENSOR, DP),
            P("group", TENSOR, DP),
            P(None, DP, TENSOR),
            P(DP, None, None),
            P(DP, None, None),
            P(None, DP, None),
            P(None, DP, None),
            P(DP),
            P(None, DP),
        ),
        out_specs=(P(TENSOR, DP), P(None, DP, None)),
        check_vma=False,
    )
```

```python
import math

import jax
import jax.numpy as jnp
import numpy as np
from jax import lax
from jax.experimental import pallas as pl
from jax.experimental.pallas import tpu as pltpu
from jax.sharding import Mesh
from jax.sharding import PartitionSpec as P

D = 5120
KVH = 8
HD = 128
EOS = 151645
STEPS = 4
CACHE = 256

learning_rate = 0.0003
weight_decay = 0.1
beta_one = 0.9
beta_two = 0.95
first_bias = 1.0 - 0.9**10
second_bias = 1.0 - 0.95**10
epsilon = 1e-08

AXES = ("group", "y", "z_hi", "z_lo", "x")
SHAPE = (2, 8, 2, 4, 4)
DP, TENSOR = ("y", "z_hi"), ("z_lo", "x")
TOK = 256
FEAT = 512
COLS = 320
ROWS = 8
PAD = 16
f32, bf16 = jnp.float32, jnp.bfloat16


def permute(value, target):
    pairs = []
    for flat, place in enumerate(np.ndindex(*SHAPE)):
        to = target(*place)
        if to is not None:
            pairs.append((flat, int(np.ravel_multi_index(to, SHAPE))))
    return lax.ppermute(value, AXES, pairs)


def gather(value, axes):
    return lax.all_to_all(value, axes, split_axis=0, concat_axis=0, tiled=True)


def to_partner(g, y, zh, zl, x):
    return (0, y, 1 - zh, zl, x) if g == 1 else None


def back_two(zh, zl):
    z = (zh * 4 + zl - 2) % 8
    return z // 4, z % 4


def to_partner_or_back(g, y, zh, zl, x):
    if g == 0:
        return None
    return (0, y, 1 - zh, zl, x) if zl % 2 == 0 else (0, y, *back_two(zh, zl), x)


def rest_back(g, y, zh, zl, x):
    return (0, y, *back_two(zh, zl), x) if g == 0 and zl % 2 == 1 else None


def keeper(zl):
    return 1 - (zl & 1)


def shift_of(z_lo, x):
    return 4 * (z_lo >> 1) + x - 3


def cot_shifted(g, y, zh, zl, x):
    to = (keeper(zl), (y - shift_of(zl, x)) % 8, zh ^ (zl & 1), zl, x)
    return to if g == 1 else None


def along_zl(flip):
    return lambda g, y, zh, zl, x: (g, y, zh, zl ^ flip, x) if g == keeper(zl) else None


def along_x(step):
    return lambda g, y, zh, zl, x: (g, y, zh, zl, (x + (step if g == 1 else -step)) % 4)


def transposed(g, y, zh, zl, x):
    return (g, zl * 2 + (x >> 1), x & 1, y >> 1, (y & 1) * 2 + zh)


def other_core(g, y, zh, zl, x):
    return (1 - g, y, zh, zl, x)


def to_rollout(g, y, zh, zl, x):
    return (0, y, zh, zl, x) if g == 1 else None


SMALL = pltpu.CompilerParams(vmem_limit_bytes=6 * 2**20)


def attend_kernel(
    head_ref, lengths_ref, ids_ref, q_ref, k_ref, v_ref, nk_ref, nv_ref, out_ref, q_rows, nk_rows, nv_rows
):
    for t in range(STEPS):
        place = slice(2 * t, 2 * t + 2)
        q_rows[place, :] = q_ref[t].astype(f32)
        nk_rows[place, :] = nk_ref[t].astype(f32)
        nv_rows[place, :] = nv_ref[t].astype(f32)
    queries = q_rows[...]
    query = jnp.concatenate(
        [queries[:, h * HD : (h + 1) * HD] for h in range(4)], axis=0
    ).astype(bf16)
    keys = k_ref[...].reshape(2 * CACHE, HD)
    values = v_ref[...].reshape(2 * CACHE, HD)
    fresh_keys = nk_rows[...].astype(bf16)
    fresh_values = nv_rows[...].astype(bf16)
    scale = 1.0 / math.sqrt(HD)
    nt = (((1,), (1,)), ((), ()))
    cache_scores = lax.dot_general(query, keys, nt, preferred_element_type=f32) * scale
    step_scores = lax.dot_general(query, fresh_keys, nt, preferred_element_type=f32) * scale
    count = 4 * ROWS

    def place(width):
        place_row = lax.broadcasted_iota(jnp.int32, (count, width), 0) & (ROWS - 1)
        place_key = lax.broadcasted_iota(jnp.int32, (count, width), 1)
        return place_row >> 1, place_row & 1, place_key

    step, row, key = place(2 * CACHE)
    length = jnp.where(row == 0, lengths_ref[0], lengths_ref[1])
    cache_valid = ((key >> 8) == row) & ((key & (CACHE - 1)) < length)
    step, row, key = place(ROWS)
    step_valid = ((key & 1) == row) & ((key >> 1) <= step)
    cache_scores = jnp.where(cache_valid, cache_scores, -jnp.inf)
    step_scores = jnp.where(step_valid, step_scores, -jnp.inf)
    peak = jnp.maximum(
        jnp.max(cache_scores, axis=-1, keepdims=True), jnp.max(step_scores, axis=-1, keepdims=True)
    )
    cache_exp = jnp.exp(cache_scores - peak)
    step_exp = jnp.exp(step_scores - peak)
    denominator = jnp.sum(cache_exp, axis=-1, keepdims=True) + jnp.sum(
        step_exp, axis=-1, keepdims=True
    )
    cache_probs = (cache_exp / denominator).astype(bf16)
    step_probs = (step_exp / denominator).astype(bf16)
    nn = (((1,), (0,)), ((), ()))
    mixed = lax.dot_general(cache_probs, values, nn, preferred_element_type=f32)
    mixed = mixed + lax.dot_general(step_probs, fresh_values, nn, preferred_element_type=f32)
    step, row, _ = place(HD)
    dead = jnp.zeros((count, HD), jnp.int32)
    for u in range(STEPS - 1):
        for r in range(2):
            ended = (ids_ref[r, u] == EOS).astype(jnp.int32)
            dead = dead + jnp.where((row == r) & (step > u), ended, 0)
    mixed = jnp.where(dead == 0, mixed, 0.0)
    flat = jnp.concatenate([mixed[h * ROWS : (h + 1) * ROWS] for h in range(4)], axis=1)
    out_ref[...] = jnp.concatenate([flat, jnp.zeros_like(flat)], axis=0).astype(bf16)


def attend(head, queries, cache_keys, cache_values, new_keys, new_values, lengths, ids):
    whole = lambda *shape: pl.BlockSpec(shape, lambda i, *_: (0,) * len(shape))
    cache = pl.BlockSpec((2, CACHE, HD), lambda i, m, *_: (0, m[0], 0))
    fresh = pl.BlockSpec((STEPS, 2, HD), lambda i, m, *_: (0, 0, m[0]))
    return pl.pallas_call(
        attend_kernel,
        out_shape=jax.ShapeDtypeStruct((PAD, FEAT), bf16),
        grid_spec=pltpu.PrefetchScalarGridSpec(
            num_scalar_prefetch=3,
            grid=(1,),
            in_specs=[whole(STEPS, 2, FEAT), cache, cache, fresh, fresh],
            out_specs=whole(PAD, FEAT),
            scratch_shapes=[
                pltpu.VMEM((ROWS, FEAT), f32),
                pltpu.VMEM((ROWS, HD), f32),
                pltpu.VMEM((ROWS, HD), f32),
            ],
        ),
        compiler_params=SMALL,
        name="attend",
    )(head, lengths, ids, queries, cache_keys, cache_values, new_keys, new_values)


VMEM = pl.BlockSpec(memory_space=pltpu.VMEM)
SMEM = pl.BlockSpec(memory_space=pltpu.SMEM)
HBM = pl.BlockSpec(memory_space=pl.ANY)


def cut_kernel(place_ref, cot_ref, out_ref, window, turned, sem):
    z_lo = place_ref[3]
    q = 2 * ((place_ref[1] - shift_of(z_lo, place_ref[4])) & 7) + (place_ref[2] ^ (z_lo & 1))
    start = pl.multiple_of(((q * 5) >> 1) * 128, 128)
    copy = pltpu.make_async_copy(cot_ref.at[:, pl.ds(start, 384)], window, sem)
    copy.start()
    copy.wait()
    turned[...] = window[...].astype(f32).T
    out_ref[...] = turned[pl.ds(pl.multiple_of((q & 1) * 64, 64), COLS), :].astype(bf16)


def cut_of(place, cot):
    return pl.pallas_call(
        cut_kernel,
        out_shape=jax.ShapeDtypeStruct((COLS, TOK), bf16),
        in_specs=[SMEM, HBM],
        out_specs=VMEM,
        scratch_shapes=[
            pltpu.VMEM((TOK, 384), bf16),
            pltpu.VMEM((384, TOK), f32),
            pltpu.SemaphoreType.DMA(()),
        ],
        compiler_params=SMALL,
        name="cut",
    )(place, cot)


def base_kernel(place_ref, act_ref, act_got, act_passed, rows_ref, rows_got, _, out_ref):
    @pl.when(place_ref[0] == 1)
    def _():
        out_ref[:TOK, :] = act_ref[...]
        out_ref[TOK:, :] = rows_ref[...]

    @pl.when((place_ref[0] == 0) & ((place_ref[3] & 1) == 0))
    def _():
        out_ref[:TOK, :] = act_got[...]

    @pl.when((place_ref[0] == 0) & ((place_ref[3] & 1) == 1))
    def _():
        out_ref[:TOK, :] = act_passed[...]

    @pl.when(place_ref[0] == 0)
    def _():
        out_ref[TOK:, :] = rows_got[...]


def base_of(place, *parts):
    return pl.pallas_call(
        base_kernel,
        out_shape=jax.ShapeDtypeStruct((TOK + PAD, FEAT), bf16),
        in_specs=[SMEM] + [VMEM] * 5 + [HBM],
        out_specs=VMEM,
        compiler_params=SMALL,
        name="base",
    )(place, *parts)


def gradient_kernel(place_ref, chunks_ref, *refs):
    blocks, (out_ref, chunk_rows, block_rows, row_tiles, sems) = refs[:4], refs[-5:]
    side, y, z_hi, own_z_lo, x = (place_ref[n] for n in range(5))
    token_zh = jnp.where(side == 1, z_hi, 1 - z_hi)
    act_copies = [
        pltpu.make_async_copy(
            chunks_ref.at[n, :TOK], chunk_rows.at[pl.ds(n * TOK, TOK)], sems.at[n]
        )
        for n in range(8)
    ]
    row_copies = [
        pltpu.make_async_copy(chunks_ref.at[n, TOK:], row_tiles.at[n], sems.at[16 + n])
        for n in range(8)
    ]
    for n in range(8):
        shift = ((n - y + 3) & 7) - 3
        slot = ((shift + 3) >> 2) ^ (own_z_lo >> 1)
        source = (shift + 3) - x
        source = jnp.where(side == 1, -source, source) & 3
        act_copies[n].start()
        for b in range(4):

            @pl.when(source == b)
            def _():
                pltpu.make_async_copy(
                    blocks[b].at[slot], block_rows.at[:, pl.ds(n * TOK, TOK)], sems.at[8 + n]
                ).start()

        row_copies[n].start()
    out_ref[COLS:, :] = jnp.zeros((16 * ROWS, FEAT), f32)
    for half in range(2):
        for n in range(4 * half, 4 * half + 4):
            act_copies[n].wait()
            pltpu.make_async_copy(
                blocks[0].at[0], block_rows.at[:, pl.ds(n * TOK, TOK)], sems.at[8 + n]
            ).wait()
        span = pl.ds(half * 4 * TOK, 4 * TOK)
        part = jnp.dot(block_rows[:, span], chunk_rows[span, :], preferred_element_type=f32)
        if half == 0:
            out_ref[:COLS, :] = part
        else:
            out_ref[:COLS, :] += part
    for n in range(8):
        row_copies[n].wait()
        place = pl.multiple_of(COLS + (2 * n + token_zh) * ROWS, ROWS)
        out_ref[pl.ds(place, ROWS), :] = row_tiles[n].astype(f32)[:ROWS]


def gradient(place, chunks, blocks, others):
    operands = (chunks, *blocks, *others)
    return pl.pallas_call(
        gradient_kernel,
        out_shape=jax.ShapeDtypeStruct((COLS + 16 * ROWS, FEAT), f32),
        in_specs=[SMEM] + [HBM] * len(operands),
        out_specs=VMEM,
        scratch_shapes=[
            pltpu.VMEM((8 * TOK, FEAT), bf16),
            pltpu.VMEM((COLS, 8 * TOK), bf16),
            pltpu.VMEM((8, PAD, FEAT), bf16),
            pltpu.SemaphoreType.DMA((24,)),
        ],
        compiler_params=pltpu.CompilerParams(vmem_limit_bytes=16 * 2**20),
        name="gradient",
    )(place, *operands)


def step_kernel(
    place_ref, mine_ref, got_ref, one_ref, one_got, two_ref, two_got, weight_ref, update_ref, out_ref
):
    learner = place_ref[0] == 1
    grad = mine_ref[:COLS, :] + got_ref[:COLS, :]
    moment_one = jnp.where(learner, one_ref[...], one_got[...])
    moment_two = jnp.where(learner, two_ref[...], two_got[...])
    first_moment = beta_one * moment_one + (1.0 - beta_one) * grad
    second_moment = beta_two * moment_two + (1.0 - beta_two) * grad * grad
    update = (
        first_moment / first_bias / (jnp.sqrt(second_moment / second_bias) + epsilon)
    ).astype(bf16)
    update_ref[...] = update
    widened = weight_ref[...].astype(f32)
    renewed = (
        widened - learning_rate * (update.astype(f32) + weight_decay * widened)
    ).astype(bf16)
    rows = (mine_ref[COLS:, :] + got_ref[COLS:, :]).astype(bf16)
    part = lax.dot_general(rows, renewed, (((1,), (1,)), ((), ())), preferred_element_type=f32)
    out_ref[...] = part.reshape(16, ROWS, COLS)


def step(place, mine, got, one, one_got, two, two_got, weight):
    return pl.pallas_call(
        step_kernel,
        out_shape=(
            jax.ShapeDtypeStruct((COLS, FEAT), bf16),
            jax.ShapeDtypeStruct((16, ROWS, COLS), f32),
        ),
        in_specs=[SMEM] + [VMEM] * 7,
        out_specs=(VMEM, VMEM),
        compiler_params=pltpu.CompilerParams(vmem_limit_bytes=16 * 2**20),
        name="step",
    )(place, mine, got, one, one_got, two, two_got, weight)


def local(
    activations,
    cotangent,
    weight,
    moment_one,
    moment_two,
    queries,
    cache_keys,
    cache_values,
    new_keys,
    new_values,
    lengths,
    token_ids,
):
    q = lax.axis_index(TENSOR)
    place = jnp.stack([lax.axis_index(axis) for axis in AXES]).astype(jnp.int32)

    act = activations[0]
    act_got = permute(act, to_partner_or_back)
    cut = cut_of(place, cotangent[0])
    own = permute(cut, cot_shifted)
    rows = attend(
        (q >> 1).reshape(1),
        queries,
        cache_keys,
        cache_values,
        new_keys,
        new_values,
        lengths,
        token_ids.T,
    )
    rows_got = permute(rows, to_partner)
    act_relay, _, _ = lax.optimization_barrier((act_got, cut, rows))
    act_passed = permute(act_relay, rest_back)
    base = base_of(place, act, act_got, act_passed, rows, rows_got, own)
    chunks = lax.all_gather(base, "y", axis=0)

    one, two = moment_one[0].T, moment_two[0].T
    own, _ = lax.optimization_barrier((own, base))
    pair = jnp.stack([own, permute(own, along_zl(2))])
    pair_got = permute(pair, along_zl(1))
    pair = jnp.where(place[0] == keeper(place[3]), pair, pair_got)
    blocks = [pair] + [permute(pair, along_x(step)) for step in (1, 2, -1)]
    one_tied, two_tied, _ = lax.optimization_barrier((one, two, base))
    one_got = permute(one_tied, to_rollout)
    two_got = permute(two_tied, to_rollout)

    mine = gradient(place, chunks, blocks, (one_got, two_got))
    got = permute(mine, other_core)
    update, partial = step(place, mine, got, one, one_got, two, two_got, weight.T)

    shares = gather(partial, TENSOR)
    summed = jnp.sum(shares, axis=0).astype(bf16)
    block = permute(summed, transposed)
    spread = jnp.broadcast_to(block[None], (16, ROWS, COLS))
    gathered = gather(spread, TENSOR)
    decoded = gathered.transpose(1, 0, 2).reshape(STEPS, ROWS // STEPS, D)
    return (update.T, decoded)


def solution(mesh):
    fine = Mesh(mesh.devices.reshape(SHAPE), AXES)
    return jax.shard_map(
        local,
        mesh=fine,
        in_specs=(
            P("group", DP, TENSOR),
            P("group", DP, None),
            P(TENSOR, DP),
            P("group", TENSOR, DP),
            P("group", TENSOR, DP),
            P(None, DP, TENSOR),
            P(DP, None, None),
            P(DP, None, None),
            P(None, DP, None),
            P(None, DP, None),
            P(DP),
            P(None, DP),
        ),
        out_specs=(P(TENSOR, DP), P(None, DP, None)),
        check_vma=False,
    )
```

```python
import math

import jax
import jax.numpy as jnp
import numpy as np
from jax import lax
from jax.experimental import pallas as pl
from jax.experimental.pallas import tpu as pltpu
from jax.sharding import Mesh
from jax.sharding import PartitionSpec as P

D = 5120
KVH = 8
HD = 128
EOS = 151645
STEPS = 4
CACHE = 256

learning_rate = 0.0003
weight_decay = 0.1
beta_one = 0.9
beta_two = 0.95
first_bias = 1.0 - 0.9**10
second_bias = 1.0 - 0.95**10
epsilon = 1e-08

AXES = ("group", "y", "z_hi", "z_lo", "x")
SHAPE = (2, 8, 2, 4, 4)
DP, TENSOR = ("y", "z_hi"), ("z_lo", "x")
TOK = 256
FEAT = 512
COLS = 320
ROWS = 8
PAD = 16
f32, bf16 = jnp.float32, jnp.bfloat16


def permute(value, target):
    pairs = []
    for flat, place in enumerate(np.ndindex(*SHAPE)):
        to = target(*place)
        if to is not None:
            pairs.append((flat, int(np.ravel_multi_index(to, SHAPE))))
    return lax.ppermute(value, AXES, pairs)


def gather(value, axes):
    return lax.all_to_all(value, axes, split_axis=0, concat_axis=0, tiled=True)


def to_partner(g, y, zh, zl, x):
    return (0, y, 1 - zh, zl, x) if g == 1 else None


def keeper(zl):
    return 1 - (zl & 1)


def shift_of(z_lo, x):
    return 4 * (z_lo >> 1) + x - 3


def cot_shifted(g, y, zh, zl, x):
    to = (keeper(zl), (y - shift_of(zl, x)) % 8, zh ^ (zl & 1), zl, x)
    return to if g == 1 else None


def along_zl(flip):
    return lambda g, y, zh, zl, x: (g, y, zh, zl ^ flip, x) if g == keeper(zl) else None


def along_x(step):
    return lambda g, y, zh, zl, x: (g, y, zh, zl, (x + (step if g == 1 else -step)) % 4)


def transposed(g, y, zh, zl, x):
    return (g, zl * 2 + (x >> 1), x & 1, y >> 1, (y & 1) * 2 + zh)


def other_core(g, y, zh, zl, x):
    return (1 - g, y, zh, zl, x)


def to_rollout(g, y, zh, zl, x):
    return (0, y, zh, zl, x) if g == 1 else None


SMALL = pltpu.CompilerParams(vmem_limit_bytes=6 * 2**20)


def attend_kernel(
    head_ref, lengths_ref, ids_ref, q_ref, k_ref, v_ref, nk_ref, nv_ref, out_ref, q_rows, nk_rows, nv_rows
):
    for t in range(STEPS):
        place = slice(2 * t, 2 * t + 2)
        q_rows[place, :] = q_ref[t].astype(f32)
        nk_rows[place, :] = nk_ref[t].astype(f32)
        nv_rows[place, :] = nv_ref[t].astype(f32)
    queries = q_rows[...]
    query = jnp.concatenate(
        [queries[:, h * HD : (h + 1) * HD] for h in range(4)], axis=0
    ).astype(bf16)
    keys = k_ref[...].reshape(2 * CACHE, HD)
    values = v_ref[...].reshape(2 * CACHE, HD)
    fresh_keys = nk_rows[...].astype(bf16)
    fresh_values = nv_rows[...].astype(bf16)
    scale = 1.0 / math.sqrt(HD)
    nt = (((1,), (1,)), ((), ()))
    cache_scores = lax.dot_general(query, keys, nt, preferred_element_type=f32) * scale
    step_scores = lax.dot_general(query, fresh_keys, nt, preferred_element_type=f32) * scale
    count = 4 * ROWS

    def place(width):
        place_row = lax.broadcasted_iota(jnp.int32, (count, width), 0) & (ROWS - 1)
        place_key = lax.broadcasted_iota(jnp.int32, (count, width), 1)
        return place_row >> 1, place_row & 1, place_key

    step, row, key = place(2 * CACHE)
    length = jnp.where(row == 0, lengths_ref[0], lengths_ref[1])
    cache_valid = ((key >> 8) == row) & ((key & (CACHE - 1)) < length)
    step, row, key = place(ROWS)
    step_valid = ((key & 1) == row) & ((key >> 1) <= step)
    cache_scores = jnp.where(cache_valid, cache_scores, -jnp.inf)
    step_scores = jnp.where(step_valid, step_scores, -jnp.inf)
    peak = jnp.maximum(
        jnp.max(cache_scores, axis=-1, keepdims=True), jnp.max(step_scores, axis=-1, keepdims=True)
    )
    cache_exp = jnp.exp(cache_scores - peak)
    step_exp = jnp.exp(step_scores - peak)
    denominator = jnp.sum(cache_exp, axis=-1, keepdims=True) + jnp.sum(
        step_exp, axis=-1, keepdims=True
    )
    cache_probs = (cache_exp / denominator).astype(bf16)
    step_probs = (step_exp / denominator).astype(bf16)
    nn = (((1,), (0,)), ((), ()))
    mixed = lax.dot_general(cache_probs, values, nn, preferred_element_type=f32)
    mixed = mixed + lax.dot_general(step_probs, fresh_values, nn, preferred_element_type=f32)
    step, row, _ = place(HD)
    dead = jnp.zeros((count, HD), jnp.int32)
    for u in range(STEPS - 1):
        for r in range(2):
            ended = (ids_ref[r, u] == EOS).astype(jnp.int32)
            dead = dead + jnp.where((row == r) & (step > u), ended, 0)
    mixed = jnp.where(dead == 0, mixed, 0.0)
    flat = jnp.concatenate([mixed[h * ROWS : (h + 1) * ROWS] for h in range(4)], axis=1)
    out_ref[...] = jnp.concatenate([flat, jnp.zeros_like(flat)], axis=0).astype(bf16)


def attend(head, queries, cache_keys, cache_values, new_keys, new_values, lengths, ids):
    whole = lambda *shape: pl.BlockSpec(shape, lambda i, *_: (0,) * len(shape))
    cache = pl.BlockSpec((2, CACHE, HD), lambda i, m, *_: (0, m[0], 0))
    fresh = pl.BlockSpec((STEPS, 2, HD), lambda i, m, *_: (0, 0, m[0]))
    return pl.pallas_call(
        attend_kernel,
        out_shape=jax.ShapeDtypeStruct((PAD, FEAT), bf16),
        grid_spec=pltpu.PrefetchScalarGridSpec(
            num_scalar_prefetch=3,
            grid=(1,),
            in_specs=[whole(STEPS, 2, FEAT), cache, cache, fresh, fresh],
            out_specs=whole(PAD, FEAT),
            scratch_shapes=[
                pltpu.VMEM((ROWS, FEAT), f32),
                pltpu.VMEM((ROWS, HD), f32),
                pltpu.VMEM((ROWS, HD), f32),
            ],
        ),
        compiler_params=SMALL,
        name="attend",
    )(head, lengths, ids, queries, cache_keys, cache_values, new_keys, new_values)


VMEM = pl.BlockSpec(memory_space=pltpu.VMEM)
SMEM = pl.BlockSpec(memory_space=pltpu.SMEM)
HBM = pl.BlockSpec(memory_space=pl.ANY)


def cut_kernel(place_ref, cot_ref, out_ref, window, turned, sem):
    z_lo = place_ref[3]
    q = 2 * ((place_ref[1] - shift_of(z_lo, place_ref[4])) & 7) + (place_ref[2] ^ (z_lo & 1))
    start = pl.multiple_of(((q * 5) >> 1) * 128, 128)
    copy = pltpu.make_async_copy(cot_ref.at[:, pl.ds(start, 384)], window, sem)
    copy.start()
    copy.wait()
    turned[...] = window[...].astype(f32).T
    out_ref[...] = turned[pl.ds(pl.multiple_of((q & 1) * 64, 64), COLS), :].astype(bf16)


def cut_of(place, cot):
    return pl.pallas_call(
        cut_kernel,
        out_shape=jax.ShapeDtypeStruct((COLS, TOK), bf16),
        in_specs=[SMEM, HBM],
        out_specs=VMEM,
        scratch_shapes=[
            pltpu.VMEM((TOK, 384), bf16),
            pltpu.VMEM((384, TOK), f32),
            pltpu.SemaphoreType.DMA(()),
        ],
        compiler_params=SMALL,
        name="cut",
    )(place, cot)


def base_kernel(place_ref, act_ref, act_got, rows_ref, rows_got, _, out_ref):
    @pl.when(place_ref[0] == 1)
    def _():
        out_ref[:TOK, :] = act_ref[...]
        out_ref[TOK:, :] = rows_ref[...]

    @pl.when(place_ref[0] == 0)
    def _():
        out_ref[:TOK, :] = act_got[...]
        out_ref[TOK:, :] = rows_got[...]


def base_of(place, *parts):
    return pl.pallas_call(
        base_kernel,
        out_shape=jax.ShapeDtypeStruct((TOK + PAD, FEAT), bf16),
        in_specs=[SMEM] + [VMEM] * 4 + [HBM],
        out_specs=VMEM,
        compiler_params=SMALL,
        name="base",
    )(place, *parts)


def gradient_kernel(place_ref, chunks_ref, *refs):
    blocks, (out_ref, chunk_rows, block_rows, row_tiles, sems) = refs[:4], refs[-5:]
    side, y, z_hi, own_z_lo, x = (place_ref[n] for n in range(5))
    token_zh = jnp.where(side == 1, z_hi, 1 - z_hi)
    act_copies = [
        pltpu.make_async_copy(
            chunks_ref.at[n, :TOK], chunk_rows.at[pl.ds(n * TOK, TOK)], sems.at[n]
        )
        for n in range(8)
    ]
    row_copies = [
        pltpu.make_async_copy(chunks_ref.at[n, TOK:], row_tiles.at[n], sems.at[16 + n])
        for n in range(8)
    ]
    for n in range(8):
        shift = ((n - y + 3) & 7) - 3
        slot = ((shift + 3) >> 2) ^ (own_z_lo >> 1)
        source = (shift + 3) - x
        source = jnp.where(side == 1, -source, source) & 3
        act_copies[n].start()
        for b in range(4):

            @pl.when(source == b)
            def _():
                pltpu.make_async_copy(
                    blocks[b].at[slot], block_rows.at[:, pl.ds(n * TOK, TOK)], sems.at[8 + n]
                ).start()

        row_copies[n].start()
    out_ref[COLS:, :] = jnp.zeros((16 * ROWS, FEAT), f32)
    for half in range(2):
        for n in range(4 * half, 4 * half + 4):
            act_copies[n].wait()
            pltpu.make_async_copy(
                blocks[0].at[0], block_rows.at[:, pl.ds(n * TOK, TOK)], sems.at[8 + n]
            ).wait()
        span = pl.ds(half * 4 * TOK, 4 * TOK)
        part = jnp.dot(block_rows[:, span], chunk_rows[span, :], preferred_element_type=f32)
        if half == 0:
            out_ref[:COLS, :] = part
        else:
            out_ref[:COLS, :] += part
    for n in range(8):
        row_copies[n].wait()
        place = pl.multiple_of(COLS + (2 * n + token_zh) * ROWS, ROWS)
        out_ref[pl.ds(place, ROWS), :] = row_tiles[n].astype(f32)[:ROWS]


def gradient(place, chunks, blocks, others):
    operands = (chunks, *blocks, *others)
    return pl.pallas_call(
        gradient_kernel,
        out_shape=jax.ShapeDtypeStruct((COLS + 16 * ROWS, FEAT), f32),
        in_specs=[SMEM] + [HBM] * len(operands),
        out_specs=VMEM,
        scratch_shapes=[
            pltpu.VMEM((8 * TOK, FEAT), bf16),
            pltpu.VMEM((COLS, 8 * TOK), bf16),
            pltpu.VMEM((8, PAD, FEAT), bf16),
            pltpu.SemaphoreType.DMA((24,)),
        ],
        compiler_params=pltpu.CompilerParams(vmem_limit_bytes=16 * 2**20),
        name="gradient",
    )(place, *operands)


def step_kernel(
    place_ref, mine_ref, got_ref, one_ref, one_got, two_ref, two_got, weight_ref, update_ref, out_ref
):
    learner = place_ref[0] == 1
    grad = mine_ref[:COLS, :] + got_ref[:COLS, :]
    moment_one = jnp.where(learner, one_ref[...], one_got[...])
    moment_two = jnp.where(learner, two_ref[...], two_got[...])
    first_moment = beta_one * moment_one + (1.0 - beta_one) * grad
    second_moment = beta_two * moment_two + (1.0 - beta_two) * grad * grad
    update = (
        first_moment / first_bias / (jnp.sqrt(second_moment / second_bias) + epsilon)
    ).astype(bf16)
    update_ref[...] = update
    widened = weight_ref[...].astype(f32)
    renewed = (
        widened - learning_rate * (update.astype(f32) + weight_decay * widened)
    ).astype(bf16)
    rows = (mine_ref[COLS:, :] + got_ref[COLS:, :]).astype(bf16)
    part = lax.dot_general(rows, renewed, (((1,), (1,)), ((), ())), preferred_element_type=f32)
    out_ref[...] = part.reshape(16, ROWS, COLS)


def step(place, mine, got, one, one_got, two, two_got, weight):
    return pl.pallas_call(
        step_kernel,
        out_shape=(
            jax.ShapeDtypeStruct((COLS, FEAT), bf16),
            jax.ShapeDtypeStruct((16, ROWS, COLS), f32),
        ),
        in_specs=[SMEM] + [VMEM] * 7,
        out_specs=(VMEM, VMEM),
        compiler_params=pltpu.CompilerParams(vmem_limit_bytes=16 * 2**20),
        name="step",
    )(place, mine, got, one, one_got, two, two_got, weight)


def local(
    activations,
    cotangent,
    weight,
    moment_one,
    moment_two,
    queries,
    cache_keys,
    cache_values,
    new_keys,
    new_values,
    lengths,
    token_ids,
):
    q = lax.axis_index(TENSOR)
    place = jnp.stack([lax.axis_index(axis) for axis in AXES]).astype(jnp.int32)

    act = activations[0]
    cut = cut_of(place, cotangent[0])
    own = permute(cut, cot_shifted)
    rows = attend(
        (q >> 1).reshape(1),
        queries,
        cache_keys,
        cache_values,
        new_keys,
        new_values,
        lengths,
        token_ids.T,
    )
    act_tied, rows, _ = lax.optimization_barrier((act, rows, cut))
    act_got = permute(act_tied, to_partner)
    rows_got = permute(rows, to_partner)
    base = base_of(place, act, act_got, rows, rows_got, own)
    chunks = lax.all_gather(base, "y", axis=0)

    one, two = moment_one[0].T, moment_two[0].T
    own, _ = lax.optimization_barrier((own, base))
    pair = jnp.stack([own, permute(own, along_zl(2))])
    pair_got = permute(pair, along_zl(1))
    pair = jnp.where(place[0] == keeper(place[3]), pair, pair_got)
    blocks = [pair] + [permute(pair, along_x(step)) for step in (1, 2, -1)]
    one_tied, two_tied, _ = lax.optimization_barrier((one, two, base))
    one_got = permute(one_tied, to_rollout)
    two_got = permute(two_tied, to_rollout)

    mine = gradient(place, chunks, blocks, (one_got, two_got))
    got = permute(mine, other_core)
    update, partial = step(place, mine, got, one, one_got, two, two_got, weight.T)

    shares = gather(partial, TENSOR)
    summed = jnp.sum(shares, axis=0).astype(bf16)
    block = permute(summed, transposed)
    spread = jnp.broadcast_to(block[None], (16, ROWS, COLS))
    gathered = gather(spread, TENSOR)
    decoded = gathered.transpose(1, 0, 2).reshape(STEPS, ROWS // STEPS, D)
    return (update.T, decoded)


def solution(mesh):
    fine = Mesh(mesh.devices.reshape(SHAPE), AXES)
    return jax.shard_map(
        local,
        mesh=fine,
        in_specs=(
            P("group", DP, TENSOR),
            P("group", DP, None),
            P(TENSOR, DP),
            P("group", TENSOR, DP),
            P("group", TENSOR, DP),
            P(None, DP, TENSOR),
            P(DP, None, None),
            P(DP, None, None),
            P(None, DP, None),
            P(None, DP, None),
            P(DP),
            P(None, DP),
        ),
        out_specs=(P(TENSOR, DP), P(None, DP, None)),
        check_vma=False,
    )
```

```python
import math

import jax
import jax.numpy as jnp
import numpy as np
from jax import lax
from jax.experimental import pallas as pl
from jax.experimental.pallas import tpu as pltpu
from jax.sharding import Mesh
from jax.sharding import PartitionSpec as P

D = 5120
KVH = 8
HD = 128
EOS = 151645
STEPS = 4
CACHE = 256

learning_rate = 0.0003
weight_decay = 0.1
beta_one = 0.9
beta_two = 0.95
first_bias = 1.0 - 0.9**10
second_bias = 1.0 - 0.95**10
epsilon = 1e-08

AXES = ("group", "y", "z_hi", "z_lo", "x")
SHAPE = (2, 8, 2, 4, 4)
DP, TENSOR = ("y", "z_hi"), ("z_lo", "x")
TOK = 256
FEAT = 512
COLS = 320
ROWS = 8
PAD = 16
f32, bf16 = jnp.float32, jnp.bfloat16


def permute(value, target):
    pairs = []
    for flat, place in enumerate(np.ndindex(*SHAPE)):
        to = target(*place)
        if to is not None:
            pairs.append((flat, int(np.ravel_multi_index(to, SHAPE))))
    return lax.ppermute(value, AXES, pairs)


def gather(value, axes):
    return lax.all_to_all(value, axes, split_axis=0, concat_axis=0, tiled=True)


def to_partner(g, y, zh, zl, x):
    return (0, y, 1 - zh, zl, x) if g == 1 else None


def keeper(zl):
    return 1 - (zl & 1)


def shift_of(z_lo, x):
    return 4 * (z_lo >> 1) + x - 3


def cot_shifted(g, y, zh, zl, x):
    to = (keeper(zl), (y - shift_of(zl, x)) % 8, zh ^ (zl & 1), zl, x)
    return to if g == 1 else None


def along_zl(flip):
    return lambda g, y, zh, zl, x: (g, y, zh, zl ^ flip, x) if g == keeper(zl) else None


def along_x(step):
    return lambda g, y, zh, zl, x: (g, y, zh, zl, (x + (step if g == 1 else -step)) % 4)


def transposed(g, y, zh, zl, x):
    return (g, zl * 2 + (x >> 1), x & 1, y >> 1, (y & 1) * 2 + zh)


def other_core(g, y, zh, zl, x):
    return (1 - g, y, zh, zl, x)


def to_rollout(g, y, zh, zl, x):
    return (0, y, zh, zl, x) if g == 1 else None


SMALL = pltpu.CompilerParams(vmem_limit_bytes=6 * 2**20)


def attend_kernel(
    head_ref, lengths_ref, ids_ref, q_ref, k_ref, v_ref, nk_ref, nv_ref, out_ref, q_rows, nk_rows, nv_rows
):
    for t in range(STEPS):
        place = slice(2 * t, 2 * t + 2)
        q_rows[place, :] = q_ref[t].astype(f32)
        nk_rows[place, :] = nk_ref[t].astype(f32)
        nv_rows[place, :] = nv_ref[t].astype(f32)
    queries = q_rows[...]
    query = jnp.concatenate(
        [queries[:, h * HD : (h + 1) * HD] for h in range(4)], axis=0
    ).astype(bf16)
    keys = k_ref[...].reshape(2 * CACHE, HD)
    values = v_ref[...].reshape(2 * CACHE, HD)
    fresh_keys = nk_rows[...].astype(bf16)
    fresh_values = nv_rows[...].astype(bf16)
    scale = 1.0 / math.sqrt(HD)
    nt = (((1,), (1,)), ((), ()))
    cache_scores = lax.dot_general(query, keys, nt, preferred_element_type=f32) * scale
    step_scores = lax.dot_general(query, fresh_keys, nt, preferred_element_type=f32) * scale
    count = 4 * ROWS

    def place(width):
        place_row = lax.broadcasted_iota(jnp.int32, (count, width), 0) & (ROWS - 1)
        place_key = lax.broadcasted_iota(jnp.int32, (count, width), 1)
        return place_row >> 1, place_row & 1, place_key

    step, row, key = place(2 * CACHE)
    length = jnp.where(row == 0, lengths_ref[0], lengths_ref[1])
    cache_valid = ((key >> 8) == row) & ((key & (CACHE - 1)) < length)
    step, row, key = place(ROWS)
    step_valid = ((key & 1) == row) & ((key >> 1) <= step)
    cache_scores = jnp.where(cache_valid, cache_scores, -jnp.inf)
    step_scores = jnp.where(step_valid, step_scores, -jnp.inf)
    peak = jnp.maximum(
        jnp.max(cache_scores, axis=-1, keepdims=True), jnp.max(step_scores, axis=-1, keepdims=True)
    )
    cache_exp = jnp.exp(cache_scores - peak)
    step_exp = jnp.exp(step_scores - peak)
    denominator = jnp.sum(cache_exp, axis=-1, keepdims=True) + jnp.sum(
        step_exp, axis=-1, keepdims=True
    )
    cache_probs = (cache_exp / denominator).astype(bf16)
    step_probs = (step_exp / denominator).astype(bf16)
    nn = (((1,), (0,)), ((), ()))
    mixed = lax.dot_general(cache_probs, values, nn, preferred_element_type=f32)
    mixed = mixed + lax.dot_general(step_probs, fresh_values, nn, preferred_element_type=f32)
    step, row, _ = place(HD)
    dead = jnp.zeros((count, HD), jnp.int32)
    for u in range(STEPS - 1):
        for r in range(2):
            ended = (ids_ref[r, u] == EOS).astype(jnp.int32)
            dead = dead + jnp.where((row == r) & (step > u), ended, 0)
    mixed = jnp.where(dead == 0, mixed, 0.0)
    flat = jnp.concatenate([mixed[h * ROWS : (h + 1) * ROWS] for h in range(4)], axis=1)
    out_ref[...] = jnp.concatenate([flat, jnp.zeros_like(flat)], axis=0).astype(bf16)


def attend(head, queries, cache_keys, cache_values, new_keys, new_values, lengths, ids):
    whole = lambda *shape: pl.BlockSpec(shape, lambda i, *_: (0,) * len(shape))
    cache = pl.BlockSpec((2, CACHE, HD), lambda i, m, *_: (0, m[0], 0))
    fresh = pl.BlockSpec((STEPS, 2, HD), lambda i, m, *_: (0, 0, m[0]))
    return pl.pallas_call(
        attend_kernel,
        out_shape=jax.ShapeDtypeStruct((PAD, FEAT), bf16),
        grid_spec=pltpu.PrefetchScalarGridSpec(
            num_scalar_prefetch=3,
            grid=(1,),
            in_specs=[whole(STEPS, 2, FEAT), cache, cache, fresh, fresh],
            out_specs=whole(PAD, FEAT),
            scratch_shapes=[
                pltpu.VMEM((ROWS, FEAT), f32),
                pltpu.VMEM((ROWS, HD), f32),
                pltpu.VMEM((ROWS, HD), f32),
            ],
        ),
        compiler_params=SMALL,
        name="attend",
    )(head, lengths, ids, queries, cache_keys, cache_values, new_keys, new_values)


VMEM = pl.BlockSpec(memory_space=pltpu.VMEM)
SMEM = pl.BlockSpec(memory_space=pltpu.SMEM)
HBM = pl.BlockSpec(memory_space=pl.ANY)


def cut_kernel(place_ref, cot_ref, out_ref, window, turned, sem):
    z_lo = place_ref[3]
    q = 2 * ((place_ref[1] - shift_of(z_lo, place_ref[4])) & 7) + (place_ref[2] ^ (z_lo & 1))
    start = pl.multiple_of(((q * 5) >> 1) * 128, 128)
    copy = pltpu.make_async_copy(cot_ref.at[:, pl.ds(start, 384)], window, sem)
    copy.start()
    copy.wait()
    turned[...] = window[...].astype(f32).T
    out_ref[...] = turned[pl.ds(pl.multiple_of((q & 1) * 64, 64), COLS), :].astype(bf16)


def cut_of(place, cot):
    return pl.pallas_call(
        cut_kernel,
        out_shape=jax.ShapeDtypeStruct((COLS, TOK), bf16),
        in_specs=[SMEM, HBM],
        out_specs=VMEM,
        scratch_shapes=[
            pltpu.VMEM((TOK, 384), bf16),
            pltpu.VMEM((384, TOK), f32),
            pltpu.SemaphoreType.DMA(()),
        ],
        compiler_params=SMALL,
        name="cut",
    )(place, cot)


def base_kernel(place_ref, act_ref, act_got, rows_ref, rows_got, _, out_ref):
    @pl.when(place_ref[0] == 1)
    def _():
        out_ref[:TOK, :] = act_ref[...]
        out_ref[TOK:, :] = rows_ref[...]

    @pl.when(place_ref[0] == 0)
    def _():
        out_ref[:TOK, :] = act_got[...]
        out_ref[TOK:, :] = rows_got[...]


def base_of(place, *parts):
    return pl.pallas_call(
        base_kernel,
        out_shape=jax.ShapeDtypeStruct((TOK + PAD, FEAT), bf16),
        in_specs=[SMEM] + [VMEM] * 4 + [HBM],
        out_specs=VMEM,
        compiler_params=SMALL,
        name="base",
    )(place, *parts)


def gradient_kernel(place_ref, chunks_ref, *refs):
    blocks, (out_ref, chunk_rows, block_rows, row_tiles, sems) = refs[:4], refs[-5:]
    side, y, z_hi, own_z_lo, x = (place_ref[n] for n in range(5))
    token_zh = jnp.where(side == 1, z_hi, 1 - z_hi)
    act_copies = [
        pltpu.make_async_copy(
            chunks_ref.at[n, :TOK], chunk_rows.at[pl.ds(n * TOK, TOK)], sems.at[n]
        )
        for n in range(8)
    ]
    row_copies = [
        pltpu.make_async_copy(chunks_ref.at[n, TOK:], row_tiles.at[n], sems.at[16 + n])
        for n in range(8)
    ]
    for n in range(8):
        shift = ((n - y + 3) & 7) - 3
        slot = ((shift + 3) >> 2) ^ (own_z_lo >> 1)
        source = (shift + 3) - x
        source = jnp.where(side == 1, -source, source) & 3
        act_copies[n].start()
        for b in range(4):

            @pl.when(source == b)
            def _():
                pltpu.make_async_copy(
                    blocks[b].at[slot], block_rows.at[:, pl.ds(n * TOK, TOK)], sems.at[8 + n]
                ).start()

        row_copies[n].start()
    out_ref[COLS:, :] = jnp.zeros((16 * ROWS, FEAT), f32)
    for half in range(2):
        for n in range(4 * half, 4 * half + 4):
            act_copies[n].wait()
            pltpu.make_async_copy(
                blocks[0].at[0], block_rows.at[:, pl.ds(n * TOK, TOK)], sems.at[8 + n]
            ).wait()
        span = pl.ds(half * 4 * TOK, 4 * TOK)
        part = jnp.dot(block_rows[:, span], chunk_rows[span, :], preferred_element_type=f32)
        if half == 0:
            out_ref[:COLS, :] = part
        else:
            out_ref[:COLS, :] += part
    for n in range(8):
        row_copies[n].wait()
        place = pl.multiple_of(COLS + (2 * n + token_zh) * ROWS, ROWS)
        out_ref[pl.ds(place, ROWS), :] = row_tiles[n].astype(f32)[:ROWS]


def gradient(place, chunks, blocks, others):
    operands = (chunks, *blocks, *others)
    return pl.pallas_call(
        gradient_kernel,
        out_shape=jax.ShapeDtypeStruct((COLS + 16 * ROWS, FEAT), f32),
        in_specs=[SMEM] + [HBM] * len(operands),
        out_specs=VMEM,
        scratch_shapes=[
            pltpu.VMEM((8 * TOK, FEAT), bf16),
            pltpu.VMEM((COLS, 8 * TOK), bf16),
            pltpu.VMEM((8, PAD, FEAT), bf16),
            pltpu.SemaphoreType.DMA((24,)),
        ],
        compiler_params=pltpu.CompilerParams(vmem_limit_bytes=16 * 2**20),
        name="gradient",
    )(place, *operands)


def step_kernel(
    place_ref, mine_ref, got_ref, one_ref, one_got, two_ref, two_got, weight_ref, update_ref, out_ref
):
    learner = place_ref[0] == 1
    grad = mine_ref[:COLS, :] + got_ref[:COLS, :]
    moment_one = jnp.where(learner, one_ref[...], one_got[...])
    moment_two = jnp.where(learner, two_ref[...], two_got[...])
    first_moment = beta_one * moment_one + (1.0 - beta_one) * grad
    second_moment = beta_two * moment_two + (1.0 - beta_two) * grad * grad
    update = (
        first_moment / first_bias / (jnp.sqrt(second_moment / second_bias) + epsilon)
    ).astype(bf16)
    update_ref[...] = update
    widened = weight_ref[...].astype(f32)
    renewed = (
        widened - learning_rate * (update.astype(f32) + weight_decay * widened)
    ).astype(bf16)
    rows = (mine_ref[COLS:, :] + got_ref[COLS:, :]).astype(bf16)
    part = lax.dot_general(rows, renewed, (((1,), (1,)), ((), ())), preferred_element_type=f32)
    out_ref[...] = part.reshape(16, ROWS, COLS)


def step(place, mine, got, one, one_got, two, two_got, weight):
    return pl.pallas_call(
        step_kernel,
        out_shape=(
            jax.ShapeDtypeStruct((COLS, FEAT), bf16),
            jax.ShapeDtypeStruct((16, ROWS, COLS), f32),
        ),
        in_specs=[SMEM] + [VMEM] * 7,
        out_specs=(VMEM, VMEM),
        compiler_params=pltpu.CompilerParams(vmem_limit_bytes=16 * 2**20),
        name="step",
    )(place, mine, got, one, one_got, two, two_got, weight)


def local(
    activations,
    cotangent,
    weight,
    moment_one,
    moment_two,
    queries,
    cache_keys,
    cache_values,
    new_keys,
    new_values,
    lengths,
    token_ids,
):
    q = lax.axis_index(TENSOR)
    place = jnp.stack([lax.axis_index(axis) for axis in AXES]).astype(jnp.int32)

    act = activations[0]
    act_got = permute(act, to_partner)
    cut = cut_of(place, cotangent[0])
    own = permute(cut, cot_shifted)
    rows = attend(
        (q >> 1).reshape(1),
        queries,
        cache_keys,
        cache_values,
        new_keys,
        new_values,
        lengths,
        token_ids.T,
    )
    rows_got = permute(rows, to_partner)
    base = base_of(place, act, act_got, rows, rows_got, cut)
    chunks = lax.all_gather(base, "y", axis=0)

    one, two = moment_one[0].T, moment_two[0].T
    own, _ = lax.optimization_barrier((own, base))
    pair = jnp.stack([own, permute(own, along_zl(2))])
    pair_got = permute(pair, along_zl(1))
    pair = jnp.where(place[0] == keeper(place[3]), pair, pair_got)
    blocks = [pair] + [permute(pair, along_x(step)) for step in (1, 2, -1)]
    one_tied, two_tied, _ = lax.optimization_barrier((one, two, base))
    one_got = permute(one_tied, to_rollout)
    two_got = permute(two_tied, to_rollout)

    mine = gradient(place, chunks, blocks, (one_got, two_got))
    got = permute(mine, other_core)
    update, partial = step(place, mine, got, one, one_got, two, two_got, weight.T)

    shares = gather(partial, TENSOR)
    summed = jnp.sum(shares, axis=0).astype(bf16)
    block = permute(summed, transposed)
    spread = jnp.broadcast_to(block[None], (16, ROWS, COLS))
    gathered = gather(spread, TENSOR)
    decoded = gathered.transpose(1, 0, 2).reshape(STEPS, ROWS // STEPS, D)
    return (update.T, decoded)


def solution(mesh):
    fine = Mesh(mesh.devices.reshape(SHAPE), AXES)
    return jax.shard_map(
        local,
        mesh=fine,
        in_specs=(
            P("group", DP, TENSOR),
            P("group", DP, None),
            P(TENSOR, DP),
            P("group", TENSOR, DP),
            P("group", TENSOR, DP),
            P(None, DP, TENSOR),
            P(DP, None, None),
            P(DP, None, None),
            P(None, DP, None),
            P(None, DP, None),
            P(DP),
            P(None, DP),
        ),
        out_specs=(P(TENSOR, DP), P(None, DP, None)),
        check_vma=False,
    )
```

```python
import math

import jax
import jax.numpy as jnp
import numpy as np
from jax import lax
from jax.experimental import pallas as pl
from jax.experimental.pallas import tpu as pltpu
from jax.sharding import Mesh
from jax.sharding import PartitionSpec as P

D = 5120
KVH = 8
HD = 128
EOS = 151645
STEPS = 4
CACHE = 256

learning_rate = 0.0003
weight_decay = 0.1
beta_one = 0.9
beta_two = 0.95
first_bias = 1.0 - 0.9**10
second_bias = 1.0 - 0.95**10
epsilon = 1e-08

AXES = ("group", "y", "z_hi", "z_lo", "x")
SHAPE = (2, 8, 2, 4, 4)
DP, TENSOR = ("y", "z_hi"), ("z_lo", "x")
TOK = 256
FEAT = 512
COLS = 320
ROWS = 8
PAD = 16
f32, bf16 = jnp.float32, jnp.bfloat16


def permute(value, target):
    pairs = []
    for flat, place in enumerate(np.ndindex(*SHAPE)):
        to = target(*place)
        if to is not None:
            pairs.append((flat, int(np.ravel_multi_index(to, SHAPE))))
    return lax.ppermute(value, AXES, pairs)


def gather(value, axes):
    return lax.all_to_all(value, axes, split_axis=0, concat_axis=0, tiled=True)


def to_partner(g, y, zh, zl, x):
    return (0, y, 1 - zh, zl, x) if g == 1 else None


def keeper(zl):
    return 1 - (zl & 1)


def shift_of(z_lo, x):
    return 4 * (z_lo >> 1) + x - 3


def cot_shifted(g, y, zh, zl, x):
    to = (keeper(zl), (y - shift_of(zl, x)) % 8, zh ^ (zl & 1), zl, x)
    return to if g == 1 else None


def along_zl(flip):
    return lambda g, y, zh, zl, x: (g, y, zh, zl ^ flip, x) if g == keeper(zl) else None


def along_x(step):
    return lambda g, y, zh, zl, x: (g, y, zh, zl, (x + (step if g == 1 else -step)) % 4)


def transposed(g, y, zh, zl, x):
    return (g, zl * 2 + (x >> 1), x & 1, y >> 1, (y & 1) * 2 + zh)


def other_core(g, y, zh, zl, x):
    return (1 - g, y, zh, zl, x)


def to_rollout(g, y, zh, zl, x):
    return (0, y, zh, zl, x) if g == 1 else None


SMALL = pltpu.CompilerParams(vmem_limit_bytes=6 * 2**20)


def attend_kernel(
    head_ref, lengths_ref, ids_ref, q_ref, k_ref, v_ref, nk_ref, nv_ref, _, out_ref, q_rows, nk_rows, nv_rows
):
    for t in range(STEPS):
        place = slice(2 * t, 2 * t + 2)
        q_rows[place, :] = q_ref[t].astype(f32)
        nk_rows[place, :] = nk_ref[t].astype(f32)
        nv_rows[place, :] = nv_ref[t].astype(f32)
    queries = q_rows[...]
    query = jnp.concatenate(
        [queries[:, h * HD : (h + 1) * HD] for h in range(4)], axis=0
    ).astype(bf16)
    keys = k_ref[...].reshape(2 * CACHE, HD)
    values = v_ref[...].reshape(2 * CACHE, HD)
    fresh_keys = nk_rows[...].astype(bf16)
    fresh_values = nv_rows[...].astype(bf16)
    scale = 1.0 / math.sqrt(HD)
    nt = (((1,), (1,)), ((), ()))
    cache_scores = lax.dot_general(query, keys, nt, preferred_element_type=f32) * scale
    step_scores = lax.dot_general(query, fresh_keys, nt, preferred_element_type=f32) * scale
    count = 4 * ROWS

    def place(width):
        place_row = lax.broadcasted_iota(jnp.int32, (count, width), 0) & (ROWS - 1)
        place_key = lax.broadcasted_iota(jnp.int32, (count, width), 1)
        return place_row >> 1, place_row & 1, place_key

    step, row, key = place(2 * CACHE)
    length = jnp.where(row == 0, lengths_ref[0], lengths_ref[1])
    cache_valid = ((key >> 8) == row) & ((key & (CACHE - 1)) < length)
    step, row, key = place(ROWS)
    step_valid = ((key & 1) == row) & ((key >> 1) <= step)
    cache_scores = jnp.where(cache_valid, cache_scores, -jnp.inf)
    step_scores = jnp.where(step_valid, step_scores, -jnp.inf)
    peak = jnp.maximum(
        jnp.max(cache_scores, axis=-1, keepdims=True), jnp.max(step_scores, axis=-1, keepdims=True)
    )
    cache_exp = jnp.exp(cache_scores - peak)
    step_exp = jnp.exp(step_scores - peak)
    denominator = jnp.sum(cache_exp, axis=-1, keepdims=True) + jnp.sum(
        step_exp, axis=-1, keepdims=True
    )
    cache_probs = (cache_exp / denominator).astype(bf16)
    step_probs = (step_exp / denominator).astype(bf16)
    nn = (((1,), (0,)), ((), ()))
    mixed = lax.dot_general(cache_probs, values, nn, preferred_element_type=f32)
    mixed = mixed + lax.dot_general(step_probs, fresh_values, nn, preferred_element_type=f32)
    step, row, _ = place(HD)
    dead = jnp.zeros((count, HD), jnp.int32)
    for u in range(STEPS - 1):
        for r in range(2):
            ended = (ids_ref[r, u] == EOS).astype(jnp.int32)
            dead = dead + jnp.where((row == r) & (step > u), ended, 0)
    mixed = jnp.where(dead == 0, mixed, 0.0)
    flat = jnp.concatenate([mixed[h * ROWS : (h + 1) * ROWS] for h in range(4)], axis=1)
    out_ref[...] = jnp.concatenate([flat, jnp.zeros_like(flat)], axis=0).astype(bf16)


def attend(head, queries, cache_keys, cache_values, new_keys, new_values, lengths, ids, after):
    whole = lambda *shape: pl.BlockSpec(shape, lambda i, *_: (0,) * len(shape))
    cache = pl.BlockSpec((2, CACHE, HD), lambda i, m, *_: (0, m[0], 0))
    fresh = pl.BlockSpec((STEPS, 2, HD), lambda i, m, *_: (0, 0, m[0]))
    return pl.pallas_call(
        attend_kernel,
        out_shape=jax.ShapeDtypeStruct((PAD, FEAT), bf16),
        grid_spec=pltpu.PrefetchScalarGridSpec(
            num_scalar_prefetch=3,
            grid=(1,),
            in_specs=[whole(STEPS, 2, FEAT), cache, cache, fresh, fresh, pl.BlockSpec(memory_space=pl.ANY)],
            out_specs=whole(PAD, FEAT),
            scratch_shapes=[
                pltpu.VMEM((ROWS, FEAT), f32),
                pltpu.VMEM((ROWS, HD), f32),
                pltpu.VMEM((ROWS, HD), f32),
            ],
        ),
        compiler_params=SMALL,
        name="attend",
    )(head, lengths, ids, queries, cache_keys, cache_values, new_keys, new_values, after)


VMEM = pl.BlockSpec(memory_space=pltpu.VMEM)
SMEM = pl.BlockSpec(memory_space=pltpu.SMEM)
HBM = pl.BlockSpec(memory_space=pl.ANY)


def cut_kernel(place_ref, cot_ref, out_ref, window, turned, sem):
    z_lo = place_ref[3]
    q = 2 * ((place_ref[1] - shift_of(z_lo, place_ref[4])) & 7) + (place_ref[2] ^ (z_lo & 1))
    start = pl.multiple_of(((q * 5) >> 1) * 128, 128)
    copy = pltpu.make_async_copy(cot_ref.at[:, pl.ds(start, 384)], window, sem)
    copy.start()
    copy.wait()
    turned[...] = window[...].astype(f32).T
    out_ref[...] = turned[pl.ds(pl.multiple_of((q & 1) * 64, 64), COLS), :].astype(bf16)


def cut_of(place, cot):
    return pl.pallas_call(
        cut_kernel,
        out_shape=jax.ShapeDtypeStruct((COLS, TOK), bf16),
        in_specs=[SMEM, HBM],
        out_specs=VMEM,
        scratch_shapes=[
            pltpu.VMEM((TOK, 384), bf16),
            pltpu.VMEM((384, TOK), f32),
            pltpu.SemaphoreType.DMA(()),
        ],
        compiler_params=SMALL,
        name="cut",
    )(place, cot)


def base_kernel(place_ref, act_ref, act_got, rows_ref, rows_got, out_ref):
    @pl.when(place_ref[0] == 1)
    def _():
        out_ref[:TOK, :] = act_ref[...]
        out_ref[TOK:, :] = rows_ref[...]

    @pl.when(place_ref[0] == 0)
    def _():
        out_ref[:TOK, :] = act_got[...]
        out_ref[TOK:, :] = rows_got[...]


def base_of(place, *parts):
    return pl.pallas_call(
        base_kernel,
        out_shape=jax.ShapeDtypeStruct((TOK + PAD, FEAT), bf16),
        in_specs=[SMEM] + [VMEM] * 4,
        out_specs=VMEM,
        compiler_params=SMALL,
        name="base",
    )(place, *parts)


def gradient_kernel(place_ref, chunks_ref, *refs):
    blocks, (out_ref, chunk_rows, block_rows, row_tiles, sems) = refs[:4], refs[-5:]
    side, y, z_hi, own_z_lo, x = (place_ref[n] for n in range(5))
    token_zh = jnp.where(side == 1, z_hi, 1 - z_hi)
    act_copies = [
        pltpu.make_async_copy(
            chunks_ref.at[n, :TOK], chunk_rows.at[pl.ds(n * TOK, TOK)], sems.at[n]
        )
        for n in range(8)
    ]
    row_copies = [
        pltpu.make_async_copy(chunks_ref.at[n, TOK:], row_tiles.at[n], sems.at[16 + n])
        for n in range(8)
    ]
    for n in range(8):
        shift = ((n - y + 3) & 7) - 3
        slot = ((shift + 3) >> 2) ^ (own_z_lo >> 1)
        source = (shift + 3) - x
        source = jnp.where(side == 1, -source, source) & 3
        act_copies[n].start()
        for b in range(4):

            @pl.when(source == b)
            def _():
                pltpu.make_async_copy(
                    blocks[b].at[slot], block_rows.at[:, pl.ds(n * TOK, TOK)], sems.at[8 + n]
                ).start()

        row_copies[n].start()
    out_ref[COLS:, :] = jnp.zeros((16 * ROWS, FEAT), f32)
    for half in range(2):
        for n in range(4 * half, 4 * half + 4):
            act_copies[n].wait()
            pltpu.make_async_copy(
                blocks[0].at[0], block_rows.at[:, pl.ds(n * TOK, TOK)], sems.at[8 + n]
            ).wait()
        span = pl.ds(half * 4 * TOK, 4 * TOK)
        part = jnp.dot(block_rows[:, span], chunk_rows[span, :], preferred_element_type=f32)
        if half == 0:
            out_ref[:COLS, :] = part
        else:
            out_ref[:COLS, :] += part
    for n in range(8):
        row_copies[n].wait()
        place = pl.multiple_of(COLS + (2 * n + token_zh) * ROWS, ROWS)
        out_ref[pl.ds(place, ROWS), :] = row_tiles[n].astype(f32)[:ROWS]


def gradient(place, chunks, blocks, others):
    operands = (chunks, *blocks, *others)
    return pl.pallas_call(
        gradient_kernel,
        out_shape=jax.ShapeDtypeStruct((COLS + 16 * ROWS, FEAT), f32),
        in_specs=[SMEM] + [HBM] * len(operands),
        out_specs=VMEM,
        scratch_shapes=[
            pltpu.VMEM((8 * TOK, FEAT), bf16),
            pltpu.VMEM((COLS, 8 * TOK), bf16),
            pltpu.VMEM((8, PAD, FEAT), bf16),
            pltpu.SemaphoreType.DMA((24,)),
        ],
        compiler_params=pltpu.CompilerParams(vmem_limit_bytes=16 * 2**20),
        name="gradient",
    )(place, *operands)


def step_kernel(
    place_ref, mine_ref, got_ref, one_ref, one_got, two_ref, two_got, weight_ref, update_ref, out_ref
):
    learner = place_ref[0] == 1
    grad = mine_ref[:COLS, :] + got_ref[:COLS, :]
    moment_one = jnp.where(learner, one_ref[...], one_got[...])
    moment_two = jnp.where(learner, two_ref[...], two_got[...])
    first_moment = beta_one * moment_one + (1.0 - beta_one) * grad
    second_moment = beta_two * moment_two + (1.0 - beta_two) * grad * grad
    update = (
        first_moment / first_bias / (jnp.sqrt(second_moment / second_bias) + epsilon)
    ).astype(bf16)
    update_ref[...] = update
    widened = weight_ref[...].astype(f32)
    renewed = (
        widened - learning_rate * (update.astype(f32) + weight_decay * widened)
    ).astype(bf16)
    rows = (mine_ref[COLS:, :] + got_ref[COLS:, :]).astype(bf16)
    part = lax.dot_general(rows, renewed, (((1,), (1,)), ((), ())), preferred_element_type=f32)
    out_ref[...] = part.reshape(16, ROWS, COLS)


def step(place, mine, got, one, one_got, two, two_got, weight):
    return pl.pallas_call(
        step_kernel,
        out_shape=(
            jax.ShapeDtypeStruct((COLS, FEAT), bf16),
            jax.ShapeDtypeStruct((16, ROWS, COLS), f32),
        ),
        in_specs=[SMEM] + [VMEM] * 7,
        out_specs=(VMEM, VMEM),
        compiler_params=pltpu.CompilerParams(vmem_limit_bytes=16 * 2**20),
        name="step",
    )(place, mine, got, one, one_got, two, two_got, weight)


def local(
    activations,
    cotangent,
    weight,
    moment_one,
    moment_two,
    queries,
    cache_keys,
    cache_values,
    new_keys,
    new_values,
    lengths,
    token_ids,
):
    q = lax.axis_index(TENSOR)
    place = jnp.stack([lax.axis_index(axis) for axis in AXES]).astype(jnp.int32)

    act = activations[0]
    act_got = permute(act, to_partner)
    cut = cut_of(place, cotangent[0])
    own = permute(cut, cot_shifted)
    rows = attend(
        (q >> 1).reshape(1),
        queries,
        cache_keys,
        cache_values,
        new_keys,
        new_values,
        lengths,
        token_ids.T,
        cut,
    )
    rows_got = permute(rows, to_partner)
    base = base_of(place, act, act_got, rows, rows_got)
    chunks = lax.all_gather(base, "y", axis=0)

    one, two = moment_one[0].T, moment_two[0].T
    one_tied, two_tied, _ = lax.optimization_barrier((one, two, base))
    own, _ = lax.optimization_barrier((own, base))
    pair = jnp.stack([own, permute(own, along_zl(2))])
    pair_got = permute(pair, along_zl(1))
    pair = jnp.where(place[0] == keeper(place[3]), pair, pair_got)
    blocks = [pair] + [permute(pair, along_x(step)) for step in (1, 2, -1)]
    one_got = permute(one_tied, to_rollout)
    two_got = permute(two_tied, to_rollout)

    chunks, one_got, two_got = lax.optimization_barrier((chunks, one_got, two_got))
    mine = gradient(place, chunks, blocks, ())
    got = permute(mine, other_core)
    update, partial = step(place, mine, got, one, one_got, two, two_got, weight.T)

    shares = gather(partial, TENSOR)
    summed = jnp.sum(shares, axis=0).astype(bf16)
    block = permute(summed, transposed)
    spread = jnp.broadcast_to(block[None], (16, ROWS, COLS))
    gathered = gather(spread, TENSOR)
    decoded = gathered.transpose(1, 0, 2).reshape(STEPS, ROWS // STEPS, D)
    return (update.T, decoded)


def solution(mesh):
    fine = Mesh(mesh.devices.reshape(SHAPE), AXES)
    return jax.shard_map(
        local,
        mesh=fine,
        in_specs=(
            P("group", DP, TENSOR),
            P("group", DP, None),
            P(TENSOR, DP),
            P("group", TENSOR, DP),
            P("group", TENSOR, DP),
            P(None, DP, TENSOR),
            P(DP, None, None),
            P(DP, None, None),
            P(None, DP, None),
            P(None, DP, None),
            P(DP),
            P(None, DP),
        ),
        out_specs=(P(TENSOR, DP), P(None, DP, None)),
        check_vma=False,
    )
```

```python
import math

import jax
import jax.numpy as jnp
import numpy as np
from jax import lax
from jax.experimental import pallas as pl
from jax.experimental.pallas import tpu as pltpu
from jax.sharding import Mesh
from jax.sharding import PartitionSpec as P

D = 5120
KVH = 8
HD = 128
EOS = 151645
STEPS = 4
CACHE = 256

learning_rate = 0.0003
weight_decay = 0.1
beta_one = 0.9
beta_two = 0.95
first_bias = 1.0 - 0.9**10
second_bias = 1.0 - 0.95**10
epsilon = 1e-08

AXES = ("group", "y", "z_hi", "z_lo", "x")
SHAPE = (2, 8, 2, 4, 4)
DP, TENSOR = ("y", "z_hi"), ("z_lo", "x")
TOK = 256
FEAT = 512
COLS = 320
ROWS = 8
PAD = 16
f32, bf16 = jnp.float32, jnp.bfloat16


def permute(value, target):
    pairs = []
    for flat, place in enumerate(np.ndindex(*SHAPE)):
        to = target(*place)
        if to is not None:
            pairs.append((flat, int(np.ravel_multi_index(to, SHAPE))))
    return lax.ppermute(value, AXES, pairs)


def gather(value, axes):
    return lax.all_to_all(value, axes, split_axis=0, concat_axis=0, tiled=True)


def to_partner(g, y, zh, zl, x):
    return (0, y, 1 - zh, zl, x) if g == 1 else None


def keeper(zl):
    return 1 - (zl & 1)


def shift_of(z_lo, x):
    return 4 * (z_lo >> 1) + x - 3


def cot_shifted(g, y, zh, zl, x):
    to = (keeper(zl), (y - shift_of(zl, x)) % 8, zh ^ (zl & 1), zl, x)
    return to if g == 1 else None


def along_zl(flip):
    return lambda g, y, zh, zl, x: (g, y, zh, zl ^ flip, x) if g == keeper(zl) else None


def along_x(step):
    return lambda g, y, zh, zl, x: (g, y, zh, zl, (x + (step if g == 1 else -step)) % 4)


def transposed(g, y, zh, zl, x):
    return (g, zl * 2 + (x >> 1), x & 1, y >> 1, (y & 1) * 2 + zh)


def other_core(g, y, zh, zl, x):
    return (1 - g, y, zh, zl, x)


def to_rollout(g, y, zh, zl, x):
    return (0, y, zh, zl, x) if g == 1 else None


SMALL = pltpu.CompilerParams(vmem_limit_bytes=6 * 2**20)


def attend_kernel(
    head_ref, lengths_ref, ids_ref, q_ref, k_ref, v_ref, nk_ref, nv_ref, out_ref, q_rows, nk_rows, nv_rows
):
    for t in range(STEPS):
        place = slice(2 * t, 2 * t + 2)
        q_rows[place, :] = q_ref[t].astype(f32)
        nk_rows[place, :] = nk_ref[t].astype(f32)
        nv_rows[place, :] = nv_ref[t].astype(f32)
    queries = q_rows[...]
    query = jnp.concatenate(
        [queries[:, h * HD : (h + 1) * HD] for h in range(4)], axis=0
    ).astype(bf16)
    keys = k_ref[...].reshape(2 * CACHE, HD)
    values = v_ref[...].reshape(2 * CACHE, HD)
    fresh_keys = nk_rows[...].astype(bf16)
    fresh_values = nv_rows[...].astype(bf16)
    scale = 1.0 / math.sqrt(HD)
    nt = (((1,), (1,)), ((), ()))
    cache_scores = lax.dot_general(query, keys, nt, preferred_element_type=f32) * scale
    step_scores = lax.dot_general(query, fresh_keys, nt, preferred_element_type=f32) * scale
    count = 4 * ROWS

    def place(width):
        place_row = lax.broadcasted_iota(jnp.int32, (count, width), 0) & (ROWS - 1)
        place_key = lax.broadcasted_iota(jnp.int32, (count, width), 1)
        return place_row >> 1, place_row & 1, place_key

    step, row, key = place(2 * CACHE)
    length = jnp.where(row == 0, lengths_ref[0], lengths_ref[1])
    cache_valid = ((key >> 8) == row) & ((key & (CACHE - 1)) < length)
    step, row, key = place(ROWS)
    step_valid = ((key & 1) == row) & ((key >> 1) <= step)
    cache_scores = jnp.where(cache_valid, cache_scores, -jnp.inf)
    step_scores = jnp.where(step_valid, step_scores, -jnp.inf)
    peak = jnp.maximum(
        jnp.max(cache_scores, axis=-1, keepdims=True), jnp.max(step_scores, axis=-1, keepdims=True)
    )
    cache_exp = jnp.exp(cache_scores - peak)
    step_exp = jnp.exp(step_scores - peak)
    denominator = jnp.sum(cache_exp, axis=-1, keepdims=True) + jnp.sum(
        step_exp, axis=-1, keepdims=True
    )
    cache_probs = (cache_exp / denominator).astype(bf16)
    step_probs = (step_exp / denominator).astype(bf16)
    nn = (((1,), (0,)), ((), ()))
    mixed = lax.dot_general(cache_probs, values, nn, preferred_element_type=f32)
    mixed = mixed + lax.dot_general(step_probs, fresh_values, nn, preferred_element_type=f32)
    step, row, _ = place(HD)
    dead = jnp.zeros((count, HD), jnp.int32)
    for u in range(STEPS - 1):
        for r in range(2):
            ended = (ids_ref[r, u] == EOS).astype(jnp.int32)
            dead = dead + jnp.where((row == r) & (step > u), ended, 0)
    mixed = jnp.where(dead == 0, mixed, 0.0)
    flat = jnp.concatenate([mixed[h * ROWS : (h + 1) * ROWS] for h in range(4)], axis=1)
    out_ref[...] = jnp.concatenate([flat, jnp.zeros_like(flat)], axis=0).astype(bf16)


def attend(head, queries, cache_keys, cache_values, new_keys, new_values, lengths, ids):
    whole = lambda *shape: pl.BlockSpec(shape, lambda i, *_: (0,) * len(shape))
    cache = pl.BlockSpec((2, CACHE, HD), lambda i, m, *_: (0, m[0], 0))
    fresh = pl.BlockSpec((STEPS, 2, HD), lambda i, m, *_: (0, 0, m[0]))
    return pl.pallas_call(
        attend_kernel,
        out_shape=jax.ShapeDtypeStruct((PAD, FEAT), bf16),
        grid_spec=pltpu.PrefetchScalarGridSpec(
            num_scalar_prefetch=3,
            grid=(1,),
            in_specs=[whole(STEPS, 2, FEAT), cache, cache, fresh, fresh],
            out_specs=whole(PAD, FEAT),
            scratch_shapes=[
                pltpu.VMEM((ROWS, FEAT), f32),
                pltpu.VMEM((ROWS, HD), f32),
                pltpu.VMEM((ROWS, HD), f32),
            ],
        ),
        compiler_params=SMALL,
        name="attend",
    )(head, lengths, ids, queries, cache_keys, cache_values, new_keys, new_values)


VMEM = pl.BlockSpec(memory_space=pltpu.VMEM)
SMEM = pl.BlockSpec(memory_space=pltpu.SMEM)
HBM = pl.BlockSpec(memory_space=pl.ANY)


def cut_kernel(place_ref, cot_ref, out_ref, window, turned, sem):
    z_lo = place_ref[3]
    q = 2 * ((place_ref[1] - shift_of(z_lo, place_ref[4])) & 7) + (place_ref[2] ^ (z_lo & 1))
    start = pl.multiple_of(((q * 5) >> 1) * 128, 128)
    copy = pltpu.make_async_copy(cot_ref.at[:, pl.ds(start, 384)], window, sem)
    copy.start()
    copy.wait()
    turned[...] = window[...].astype(f32).T
    out_ref[...] = turned[pl.ds(pl.multiple_of((q & 1) * 64, 64), COLS), :].astype(bf16)


def cut_of(place, cot):
    return pl.pallas_call(
        cut_kernel,
        out_shape=jax.ShapeDtypeStruct((COLS, TOK), bf16),
        in_specs=[SMEM, HBM],
        out_specs=VMEM,
        scratch_shapes=[
            pltpu.VMEM((TOK, 384), bf16),
            pltpu.VMEM((384, TOK), f32),
            pltpu.SemaphoreType.DMA(()),
        ],
        compiler_params=SMALL,
        name="cut",
    )(place, cot)


def base_kernel(place_ref, act_ref, act_got, rows_ref, rows_got, _, out_ref):
    @pl.when(place_ref[0] == 1)
    def _():
        out_ref[:TOK, :] = act_ref[...]
        out_ref[TOK:, :] = rows_ref[...]

    @pl.when(place_ref[0] == 0)
    def _():
        out_ref[:TOK, :] = act_got[...]
        out_ref[TOK:, :] = rows_got[...]


def base_of(place, *parts):
    return pl.pallas_call(
        base_kernel,
        out_shape=jax.ShapeDtypeStruct((TOK + PAD, FEAT), bf16),
        in_specs=[SMEM] + [VMEM] * 4 + [HBM],
        out_specs=VMEM,
        compiler_params=SMALL,
        name="base",
    )(place, *parts)


def gradient_kernel(place_ref, chunks_ref, *refs):
    blocks, (out_ref, chunk_rows, block_rows, row_tiles, sems) = refs[:4], refs[-5:]
    side, y, z_hi, own_z_lo, x = (place_ref[n] for n in range(5))
    token_zh = jnp.where(side == 1, z_hi, 1 - z_hi)
    act_copies = [
        pltpu.make_async_copy(
            chunks_ref.at[n, :TOK], chunk_rows.at[pl.ds(n * TOK, TOK)], sems.at[n]
        )
        for n in range(8)
    ]
    row_copies = [
        pltpu.make_async_copy(chunks_ref.at[n, TOK:], row_tiles.at[n], sems.at[16 + n])
        for n in range(8)
    ]
    for n in range(8):
        shift = ((n - y + 3) & 7) - 3
        slot = ((shift + 3) >> 2) ^ (own_z_lo >> 1)
        source = (shift + 3) - x
        source = jnp.where(side == 1, -source, source) & 3
        act_copies[n].start()
        for b in range(4):

            @pl.when(source == b)
            def _():
                pltpu.make_async_copy(
                    blocks[b].at[slot], block_rows.at[:, pl.ds(n * TOK, TOK)], sems.at[8 + n]
                ).start()

        row_copies[n].start()
    out_ref[COLS:, :] = jnp.zeros((16 * ROWS, FEAT), f32)
    for half in range(2):
        for n in range(4 * half, 4 * half + 4):
            act_copies[n].wait()
            pltpu.make_async_copy(
                blocks[0].at[0], block_rows.at[:, pl.ds(n * TOK, TOK)], sems.at[8 + n]
            ).wait()
        span = pl.ds(half * 4 * TOK, 4 * TOK)
        part = jnp.dot(block_rows[:, span], chunk_rows[span, :], preferred_element_type=f32)
        if half == 0:
            out_ref[:COLS, :] = part
        else:
            out_ref[:COLS, :] += part
    for n in range(8):
        row_copies[n].wait()
        place = pl.multiple_of(COLS + (2 * n + token_zh) * ROWS, ROWS)
        out_ref[pl.ds(place, ROWS), :] = row_tiles[n].astype(f32)[:ROWS]


def gradient(place, chunks, blocks, others):
    operands = (chunks, *blocks, *others)
    return pl.pallas_call(
        gradient_kernel,
        out_shape=jax.ShapeDtypeStruct((COLS + 16 * ROWS, FEAT), f32),
        in_specs=[SMEM] + [HBM] * len(operands),
        out_specs=VMEM,
        scratch_shapes=[
            pltpu.VMEM((8 * TOK, FEAT), bf16),
            pltpu.VMEM((COLS, 8 * TOK), bf16),
            pltpu.VMEM((8, PAD, FEAT), bf16),
            pltpu.SemaphoreType.DMA((24,)),
        ],
        compiler_params=pltpu.CompilerParams(vmem_limit_bytes=16 * 2**20),
        name="gradient",
    )(place, *operands)


def step_kernel(
    place_ref, mine_ref, got_ref, one_ref, one_got, two_ref, two_got, weight_ref, update_ref, out_ref
):
    learner = place_ref[0] == 1
    grad = mine_ref[:COLS, :] + got_ref[:COLS, :]
    moment_one = jnp.where(learner, one_ref[...], one_got[...])
    moment_two = jnp.where(learner, two_ref[...], two_got[...])
    first_moment = beta_one * moment_one + (1.0 - beta_one) * grad
    second_moment = beta_two * moment_two + (1.0 - beta_two) * grad * grad
    update = (
        first_moment / first_bias / (jnp.sqrt(second_moment / second_bias) + epsilon)
    ).astype(bf16)
    update_ref[...] = update
    widened = weight_ref[...].astype(f32)
    renewed = (
        widened - learning_rate * (update.astype(f32) + weight_decay * widened)
    ).astype(bf16)
    rows = (mine_ref[COLS:, :] + got_ref[COLS:, :]).astype(bf16)
    part = lax.dot_general(rows, renewed, (((1,), (1,)), ((), ())), preferred_element_type=f32)
    out_ref[...] = part.reshape(16, ROWS, COLS)


def step(place, mine, got, one, one_got, two, two_got, weight):
    return pl.pallas_call(
        step_kernel,
        out_shape=(
            jax.ShapeDtypeStruct((COLS, FEAT), bf16),
            jax.ShapeDtypeStruct((16, ROWS, COLS), f32),
        ),
        in_specs=[SMEM] + [VMEM] * 7,
        out_specs=(VMEM, VMEM),
        compiler_params=pltpu.CompilerParams(vmem_limit_bytes=16 * 2**20),
        name="step",
    )(place, mine, got, one, one_got, two, two_got, weight)


def local(
    activations,
    cotangent,
    weight,
    moment_one,
    moment_two,
    queries,
    cache_keys,
    cache_values,
    new_keys,
    new_values,
    lengths,
    token_ids,
):
    q = lax.axis_index(TENSOR)
    place = jnp.stack([lax.axis_index(axis) for axis in AXES]).astype(jnp.int32)

    act = activations[0]
    act_got = permute(act, to_partner)
    cut = cut_of(place, cotangent[0])
    own = permute(cut, cot_shifted)
    rows = attend(
        (q >> 1).reshape(1),
        queries,
        cache_keys,
        cache_values,
        new_keys,
        new_values,
        lengths,
        token_ids.T,
    )
    rows_got = permute(rows, to_partner)
    base = base_of(place, act, act_got, rows, rows_got, own)
    chunks = lax.all_gather(base, "y", axis=0)

    one, two = moment_one[0].T, moment_two[0].T
    own, _ = lax.optimization_barrier((own, base))
    pair = jnp.stack([own, permute(own, along_zl(2))])
    pair_got = permute(pair, along_zl(1))
    pair = jnp.where(place[0] == keeper(place[3]), pair, pair_got)
    near, other = permute(pair, along_x(1)), permute(pair, along_x(-1))
    blocks = [pair, near, permute(pair, along_x(2)), other]
    one_tied, two_tied, _ = lax.optimization_barrier((one, two, base))
    one_got = permute(one_tied, to_rollout)
    two_got = permute(two_tied, to_rollout)

    mine = gradient(place, chunks, blocks, (one_got, two_got))
    got = permute(mine, other_core)
    update, partial = step(place, mine, got, one, one_got, two, two_got, weight.T)

    shares = gather(partial, TENSOR)
    summed = jnp.sum(shares, axis=0).astype(bf16)
    block = permute(summed, transposed)
    spread = jnp.broadcast_to(block[None], (16, ROWS, COLS))
    gathered = gather(spread, TENSOR)
    decoded = gathered.transpose(1, 0, 2).reshape(STEPS, ROWS // STEPS, D)
    return (update.T, decoded)


def solution(mesh):
    fine = Mesh(mesh.devices.reshape(SHAPE), AXES)
    return jax.shard_map(
        local,
        mesh=fine,
        in_specs=(
            P("group", DP, TENSOR),
            P("group", DP, None),
            P(TENSOR, DP),
            P("group", TENSOR, DP),
            P("group", TENSOR, DP),
            P(None, DP, TENSOR),
            P(DP, None, None),
            P(DP, None, None),
            P(None, DP, None),
            P(None, DP, None),
            P(DP),
            P(None, DP),
        ),
        out_specs=(P(TENSOR, DP), P(None, DP, None)),
        check_vma=False,
    )
```
